32 devices in a mesh: ctx: 8 (over y, x, core), fsdp: 4 (over z).
Axes of the slice: x: 2, y: 2, z: 4, core: 2. Of those that a mesh axis runs over, the one named last changes fastest.
Arguments:
- tokens: bfloat16 [4, 1024, 2048], P('fsdp', 'ctx'), may hold values from -6 to 6
- cotangent: bfloat16 [4, 1024, 2048], P('fsdp', 'ctx'), may hold values from -6 to 6
- doc_ids: int32 [4, 1024], P('fsdp', 'ctx'), may hold values from 0 to 2, as said below
- in_proj: bfloat16 [2048, 6656], P('fsdp'), may hold values from -0.125 to 0.125
- dt_proj: bfloat16 [2048, 48], P('fsdp'), may hold values from -0.125 to 0.125
- conv_weight: float32 [4, 3584], replicated, may hold values from -3 to 3
- conv_bias: float32 [3584], replicated, may hold values from -3 to 3
- dt_bias: float32 [48], replicated, may hold values from -7 to -3
- a_log: float32 [48], replicated, may hold values from -2 to 2
- d_skip: float32 [48], replicated, may hold values from 0.5 to 1.5
- mixer_gain: float32 [3072], replicated, may hold values from 0.5 to 1.5
- out_proj: bfloat16 [3072, 2048], P('fsdp'), may hold values from -0.109375 to 0.109375
- qkv_proj: bfloat16 [2048, 1536], P('fsdp'), may hold values from -0.125 to 0.125
- o_proj: bfloat16 [1024, 2048], P('fsdp'), may hold values from -3 to 3
- first_gain: float32 [2048], replicated, may hold values from 0.5 to 1.5
- second_gain: float32 [2048], replicated, may hold values from 0.5 to 1.5
- gate_up: bfloat16 [2048, 8192], P('fsdp'), may hold values from -0.125 to 0.125
- down_proj: bfloat16 [4096, 2048], P('fsdp'), may hold values from -0.09375 to 0.09375
Outputs:
- mixed: bfloat16 [4, 1024, 2048], P('fsdp', 'ctx')
- d_tokens: float32 [4, 1024, 2048], P('fsdp', 'ctx')
- in_proj_grad: float32 [2048, 6656], P('fsdp')
- dt_proj_grad: float32 [2048, 48], P('fsdp')
- conv_weight_grad: float32 [4, 3584], replicated
- conv_bias_grad: float32 [3584], replicated
- dt_bias_grad: float32 [48], replicated
- a_log_grad: float32 [48], replicated
- d_skip_grad: float32 [48], replicated
- mixer_gain_grad: float32 [3072], replicated
- out_proj_grad: float32 [3072, 2048], P('fsdp')
- qkv_proj_grad: float32 [2048, 1536], P('fsdp')
- o_proj_grad: float32 [1024, 2048], P('fsdp')
- first_gain_grad: float32 [2048], replicated
- second_gain_grad: float32 [2048], replicated
- gate_up_grad: float32 [2048, 8192], P('fsdp')
- down_proj_grad: float32 [4096, 2048], P('fsdp')
The draws below stay inside these ranges and needn't reach their ends.
Inputs may be any that keep to these rules, and one draw needn't show every extreme that they name: `doc_ids`: in each sequence, never falling; document 0 ends inside the first 128 tokens and document 2 begins inside the last 128, so document 1 covers every other token.
All inputs are finite; a program needn't handle non-finite values.
Results may differ from the reference program's by a relative error of at most 0.022.
Values may be sent and summed in bfloat16 or wider, within the bound.
No kernel may reach another device: no remote copies, remote signals or barrier semaphores. Data moves between devices by JAX's collectives and lax.ppermute only.
A program may use at most 640 MiB of HBM per device.

```python
import jax
import jax.numpy as jnp
from jax import lax

D = 2048
FF = 4096
NH = 48
HP = 64
NS = 256
KC = 4
HQ = 8
HK = 2
HA = 128
TOK_DEV = 128
DS = 3072
CH = 3584
SEQ = 1024
BATCH = 4


def draw_doc_ids(key, part):
    key = jax.random.fold_in(key, 7)
    head_key, tail_key = jax.random.split(key)
    head_len = jax.random.randint(head_key, (BATCH, 1), 1, TOK_DEV)
    tail_len = jax.random.randint(tail_key, (BATCH, 1), 1, TOK_DEV)
    places = jnp.arange(SEQ, dtype=jnp.int32)[None, :]
    return (places >= head_len).astype(jnp.int32) + (places >= SEQ - tail_len).astype(jnp.int32)


def shard_levels(rng, extent, shards, least, largest):
    def one(axis_at, blocks):
        heights = jax.random.uniform(jax.random.fold_in(jax.random.fold_in(rng, 6), axis_at), (blocks,), jnp.float32, least / len(shards), largest / len(shards))
        return jnp.repeat(jnp.exp(heights), extent[axis_at] // blocks).reshape((-1,) + (1,) * (len(extent) - axis_at - 1))

    level = one(*shards[0])
    for cut in shards[1:]:
        level = level * one(*cut)
    return level


def scatter_about(key, dims, deviation, reach, cuts=(), kind=jnp.bfloat16):
    result = jax.random.normal(key, dims, jnp.float32) * deviation
    if len(cuts) > 0:
        result = shard_levels(key, dims, cuts, -0.22, 0.18) * result
    return jnp.clip(result, min=-reach, max=reach).astype(kind)


def setup_inputs(seed: int = 0) -> dict:
    splits = jax.random.split(jax.random.key(seed), 19)
    tokens = scatter_about(splits[0], (BATCH, SEQ, D), 1.0, 6.0, ((0, 4), (1, 8)))
    cotangent = scatter_about(splits[1], (BATCH, SEQ, D), 1.0, 6.0, ((0, 4), (1, 8)))
    doc_ids = draw_doc_ids(jax.random.fold_in(splits[18], 71), 0)
    in_proj = scatter_about(splits[3], (D, 2 * DS + 2 * NS), D ** -0.5, 0.125, ((0, 4),))
    dt_proj = scatter_about(splits[4], (D, NH), D ** -0.5, 0.125, ((0, 4),))
    conv_weight = scatter_about(splits[5], (KC, CH), KC ** -0.5, 3.0, (), jnp.float32)
    conv_bias = scatter_about(splits[6], (CH,), 0.5, 3.0, (), jnp.float32)
    dt_bias = jnp.clip(jax.random.uniform(splits[7], (NH,), jnp.float32, -7.0, -3.0), -7.0, -3.0)
    a_log = jnp.clip(jax.random.uniform(splits[8], (NH,), jnp.float32, -2.0, 2.0), -2.0, 2.0)
    d_skip = jnp.clip(jax.random.uniform(splits[9], (NH,), jnp.float32, 0.5, 1.5), 0.5, 1.5)
    mixer_gain = jnp.clip(1.0 + 0.1 * jax.random.normal(splits[10], (DS,), jnp.float32), 0.5, 1.5)
    out_proj = scatter_about(splits[11], (DS, D), DS ** -0.5, 0.109375, ((0, 4),))
    qkv_proj = scatter_about(splits[12], (D, (HQ + 2 * HK) * HA), D ** -0.5, 0.125, ((0, 4),))
    o_proj = scatter_about(splits[13], (HQ * HA, D), 4 ** -0.5, 3.0, ((0, 4),))
    first_gain = jnp.clip(1.0 + 0.1 * jax.random.normal(splits[14], (D,), jnp.float32), 0.5, 1.5)
    second_gain = jnp.clip(1.0 + 0.1 * jax.random.normal(splits[15], (D,), jnp.float32), 0.5, 1.5)
    gate_up = scatter_about(splits[16], (D, 2 * FF), D ** -0.5, 0.125, ((0, 4),))
    down_proj = scatter_about(splits[17], (FF, D), FF ** -0.5, 0.09375, ((0, 4),))
    return {"tokens": tokens, "cotangent": cotangent, "doc_ids": doc_ids, "in_proj": in_proj, "dt_proj": dt_proj, "conv_weight": conv_weight, "conv_bias": conv_bias, "dt_bias": dt_bias, "a_log": a_log, "d_skip": d_skip, "mixer_gain": mixer_gain, "out_proj": out_proj, "qkv_proj": qkv_proj, "o_proj": o_proj, "first_gain": first_gain, "second_gain": second_gain, "gate_up": gate_up, "down_proj": down_proj}


HIGH = lax.Precision.HIGHEST
epsilon = 1e-05
rope_base = 100000000000.0

@jax.custom_vjp
def low(v):
    return lax.optimization_barrier(v.astype(jnp.bfloat16)).astype(jnp.float32)

@jax.custom_vjp
def low_back(v):
    return v

def low_keep(v):
    return (low(v), None)

def low_pass(kept, grad):
    return (grad,)

def back_keep(v):
    return (v, None)

def back_low(kept, grad):
    return (low(grad),)
low.defvjp(low_keep, low_pass)
low_back.defvjp(back_keep, back_low)

def product(left_side, right_side):
    return jnp.dot(left_side, right_side, precision=HIGH, preferred_element_type=jnp.float32)

def normed(operand, gain_vec):
    return operand * lax.rsqrt(lax.optimization_barrier(jnp.mean(operand * operand, axis=-1, keepdims=True)) + epsilon) * gain_vec

def rotate(operand, places, direction):
    half_width = operand.shape[-1] // 2
    frequency = rope_base ** (-jnp.arange(half_width, dtype=jnp.float32) * (2.0 / operand.shape[-1]))
    angles = places.astype(jnp.float32)[:, None] * frequency[None, :]
    cosine = jnp.cos(angles)[:, None, :]
    sine_part = direction * jnp.sin(angles)[:, None, :]
    first_half = operand[..., :half_width]
    second_half = operand[..., half_width:]
    return jnp.concatenate([first_half * cosine - second_half * sine_part, second_half * cosine + first_half * sine_part], -1)

def convolve(padded, pad_ids, row_ids, kernel_in, bias_in):
    length = row_ids.shape[0]
    total = jnp.zeros((length, padded.shape[1]), jnp.float32) + bias_in[None, :]
    for offset in range(KC):
        same_doc = (pad_ids[offset:offset + length] == row_ids).astype(jnp.float32)
        total = total + kernel_in[offset][None, :] * padded[offset:offset + length] * same_doc[:, None]
    return total

def ssm_local(states_x, step_size, log_decay, b_matrix, c_matrix, row_ids):
    length = states_x.shape[0]
    running = jnp.cumsum(log_decay, axis=0)
    places = jnp.arange(length, dtype=jnp.int32)
    allowed = (places[:, None] >= places[None, :]) & (row_ids[:, None] == row_ids[None, :])
    spread = running.T[:, :, None] - running.T[:, None, :]
    decay_matrix = jnp.where(allowed[None], jnp.exp(jnp.where(allowed[None], spread, 0.0)), 0.0)
    intersection = jnp.dot(c_matrix, b_matrix.T, precision=HIGH, preferred_element_type=jnp.float32)
    driven = step_size[:, :, None] * states_x
    y_part = jnp.einsum('hts,shp->thp', decay_matrix * intersection[None], driven, precision=HIGH)
    to_end = jnp.where((row_ids == row_ids[-1])[:, None], jnp.exp(running[-1][None, :] - running), 0.0)
    local_state = jnp.einsum('sh,shp,sn->hpn', to_end, driven, b_matrix, precision=HIGH)
    return (y_part, local_state)

def ssm_carry(c_matrix, log_decay, row_ids, prev_id, state_in):
    kept_mask = (row_ids == prev_id).astype(jnp.float32)
    weight = jnp.exp(jnp.cumsum(log_decay, axis=0)) * kept_mask[:, None]
    return weight[:, :, None] * jnp.einsum('hpn,tn->thp', state_in, c_matrix, precision=HIGH)

def block_decay(log_decay, row_ids, prev_id):
    return jnp.exp(lax.optimization_barrier(jnp.sum(log_decay, axis=0))) * (row_ids[-1] == prev_id).astype(jnp.float32)

def attend(queries, key_rows, value_rows, row_ids):
    length = queries.shape[0]
    width = min(length, 512)
    places = jnp.arange(length, dtype=jnp.int32)
    key_all = jnp.repeat(key_rows, HQ // HK, axis=1)
    value_all = jnp.repeat(value_rows, HQ // HK, axis=1)

    def block_fn(first_row):
        query_block = lax.dynamic_slice_in_dim(queries, first_row, width, 0)
        query_places = lax.dynamic_slice_in_dim(places, first_row, width, 0)
        query_ids = lax.dynamic_slice_in_dim(row_ids, first_row, width, 0)
        scores = low_back(jnp.einsum('qhd,khd->hqk', query_block, key_all, precision=HIGH) * HA ** (-0.5))
        allowed = (query_places[:, None] >= places[None, :]) & (query_ids[:, None] == row_ids[None, :])
        scores = jnp.where(allowed[None], scores, -1e+30)
        weights = low(jax.nn.softmax(scores, axis=-1))
        return jnp.einsum('hqk,khd->qhd', weights, value_all, precision=HIGH)
    blocks = lax.map(jax.checkpoint(block_fn), jnp.arange(length // width, dtype=jnp.int32) * width)
    return blocks.reshape(length, HQ, HA)

def layer(hidden, row_ids, params):
    in_proj, dt_proj, conv_weight, conv_bias, dt_bias, a_log, d_skip, mixer_gain, out_proj, qkv_proj, o_proj, first_gain, second_gain, gate_up, down_proj = params
    length = hidden.shape[0]
    places = jnp.arange(length, dtype=jnp.int32)
    normed_in = low(normed(hidden, first_gain))
    projected = low_back(product(normed_in, in_proj))
    step_raw = low_back(product(normed_in, dt_proj))
    attn_in = low_back(product(normed_in, qkv_proj))
    gate_z = projected[:, :DS]
    conv_in = low(projected[:, DS:])
    padded = jnp.concatenate([jnp.zeros((KC - 1, CH), jnp.float32), conv_in], 0)
    pad_ids = jnp.concatenate([jnp.full((KC - 1,), -1, jnp.int32), row_ids], 0)
    activated = jax.nn.silu(convolve(padded, pad_ids, row_ids, conv_weight, conv_bias))
    states_x = activated[:, :DS].reshape(length, NH, HP)
    b_matrix = activated[:, DS:DS + NS]
    c_matrix = activated[:, DS + NS:]
    step_size = jax.nn.softplus(step_raw + dt_bias)
    log_decay = -step_size * jnp.exp(a_log)

    def block_fn(carried, block_index):
        state_now, prev_id = carried
        first_row = block_index * TOK_DEV

        def take_rows(operand):
            return lax.dynamic_slice_in_dim(operand, first_row, TOK_DEV, 0)
        ids_here = take_rows(row_ids)
        y_part, local_state = ssm_local(take_rows(states_x), take_rows(step_size), take_rows(log_decay), take_rows(b_matrix), take_rows(c_matrix), ids_here)
        y_carry = ssm_carry(take_rows(c_matrix), take_rows(log_decay), ids_here, prev_id, state_now)
        new_state = block_decay(take_rows(log_decay), ids_here, prev_id)[:, None, None] * state_now + local_state
        return ((new_state, ids_here[-1]), y_part + y_carry)
    start_state = (jnp.zeros((NH, HP, NS), jnp.float32), jnp.array(-1, jnp.int32))
    ignored, y_blocks = lax.scan(jax.checkpoint(block_fn), start_state, jnp.arange(length // TOK_DEV, dtype=jnp.int32))
    core = y_blocks.reshape(length, NH, HP) + d_skip[None, :, None] * states_x
    gated = core.reshape(length, DS) * jax.nn.silu(gate_z)
    mixer_out = low_back(product(low(normed(gated, mixer_gain)), out_proj))
    queries = low(rotate(attn_in[:, :HQ * HA].reshape(length, HQ, HA), places, 1.0))
    key_rows = low(rotate(attn_in[:, HQ * HA:(HQ + HK) * HA].reshape(length, HK, HA), places, 1.0))
    value_rows = low(attn_in[:, (HQ + HK) * HA:].reshape(length, HK, HA))
    attended = low(low_back(attend(queries, key_rows, value_rows, row_ids).reshape(length, HQ * HA)))
    attn_out = low_back(product(attended, o_proj))
    middle = hidden + mixer_out + attn_out
    normed_mid = low(normed(middle, second_gain))
    gate_up_out = low_back(product(normed_mid, gate_up))
    activation = low(jax.nn.silu(gate_up_out[:, :FF]) * gate_up_out[:, FF:])
    return middle + low_back(product(activation, down_proj))

def reference(tokens, cotangent, doc_ids, in_proj, dt_proj, conv_weight, conv_bias, dt_bias, a_log, d_skip, mixer_gain, out_proj, qkv_proj, o_proj, first_gain, second_gain, gate_up, down_proj):
    params = tuple((operand.astype(jnp.float32) for operand in (in_proj, dt_proj, conv_weight, conv_bias, dt_bias, a_log, d_skip, mixer_gain, out_proj, qkv_proj, o_proj, first_gain, second_gain, gate_up, down_proj)))

    def sequence_fn(totals, inputs):
        hidden, grad_out, row_ids = inputs
        output, pullback = jax.vjp(lambda first_arg, second_arg: layer(first_arg, row_ids, second_arg), hidden.astype(jnp.float32), params)
        d_hidden, d_params = pullback(grad_out.astype(jnp.float32))
        return (jax.tree.map(jnp.add, totals, d_params), (output.astype(jnp.bfloat16), d_hidden))
    zeros_tree = jax.tree.map(jnp.zeros_like, params)
    totals, (mixed, d_tokens) = lax.scan(sequence_fn, zeros_tree, (tokens, cotangent, doc_ids))
    return (mixed, d_tokens, totals[0], totals[1], totals[2], totals[3], totals[4], totals[5], totals[6], totals[7], totals[8], totals[9], totals[10], totals[11], totals[12], totals[13], totals[14])
```

```python
import jax
import jax.numpy as jnp
from jax import lax
from jax.experimental import pallas as pl
from jax.experimental.pallas import tpu as pltpu
from jax.sharding import PartitionSpec as P

D = 2048
FF = 4096
NH = 48
HP = 64
NS = 256
KC = 4
HQ = 8
HK = 2
HA = 128
DS = 3072


HIGH = lax.Precision.HIGHEST
epsilon = 1e-05
rope_base = 100000000000.0


def from_behind(block, axis, distance):
    devices = range(lax.axis_size(axis))
    route = [(i - distance, i) for i in devices if i - distance in devices]
    return lax.ppermute(block, axis, route)


def normed(operand, gain_vec):
    return (
        operand
        * lax.rsqrt(jnp.mean(operand * operand, axis=-1, keepdims=True) + epsilon)
        * gain_vec
    )


def rotate(operand, places, direction):
    half_width = operand.shape[-1] // 2
    frequency = rope_base ** (
        -jnp.arange(half_width, dtype=jnp.float32) * (2.0 / operand.shape[-1])
    )
    angles = places.astype(jnp.float32)[:, None] * frequency[None, :]
    cosine = jnp.cos(angles)[:, None, :]
    sine_part = direction * jnp.sin(angles)[:, None, :]
    first_half = operand[..., :half_width]
    second_half = operand[..., half_width:]
    return jnp.concatenate(
        [
            first_half * cosine - second_half * sine_part,
            second_half * cosine + first_half * sine_part,
        ],
        -1,
    )


def project(left_side, right_side):
    return jnp.dot(left_side, right_side, preferred_element_type=jnp.float32)


def project_back(grad_in, weight):
    return lax.dot_general(
        grad_in, weight, (((1,), (1,)), ((), ())), preferred_element_type=jnp.float32
    )


def convolve(padded, pad_ids, row_ids, kernel_in, bias_in):
    length = row_ids.shape[0]
    total = jnp.zeros((length, padded.shape[1]), jnp.float32) + bias_in[None, :]
    for offset in range(KC):
        same_doc = (pad_ids[offset : offset + length] == row_ids).astype(jnp.float32)
        total = (
            total
            + kernel_in[offset][None, :] * padded[offset : offset + length] * same_doc[:, None]
        )
    return total


def ssm_local(states_x, step_size, log_decay, b_matrix, c_matrix, row_ids):
    length = states_x.shape[0]
    running = jnp.cumsum(log_decay, axis=0)
    places = jnp.arange(length, dtype=jnp.int32)
    allowed = (places[:, None] >= places[None, :]) & (row_ids[:, None] == row_ids[None, :])
    spread = running.T[:, :, None] - running.T[:, None, :]
    decay_matrix = jnp.where(allowed[None], jnp.exp(jnp.where(allowed[None], spread, 0.0)), 0.0)
    intersection = jnp.dot(c_matrix, b_matrix.T, precision=HIGH, preferred_element_type=jnp.float32)
    driven = step_size[:, :, None] * states_x
    y_part = jnp.einsum("hts,shp->thp", decay_matrix * intersection[None], driven, precision=HIGH)
    to_end = jnp.where(
        (row_ids == row_ids[-1])[:, None], jnp.exp(running[-1][None, :] - running), 0.0
    )
    local_state = jnp.einsum("sh,shp,sn->hpn", to_end, driven, b_matrix, precision=HIGH)
    return (y_part, local_state)


def ssm_carry(c_matrix, log_decay, row_ids, prev_id, state_in):
    kept_mask = (row_ids == prev_id).astype(jnp.float32)
    weight = jnp.exp(jnp.cumsum(log_decay, axis=0)) * kept_mask[:, None]
    return weight[:, :, None] * jnp.einsum("hpn,tn->thp", state_in, c_matrix, precision=HIGH)


def block_decay(log_decay, row_ids, prev_id):
    return jnp.exp(jnp.sum(log_decay, axis=0)) * (row_ids[-1] == prev_id).astype(jnp.float32)


def mixer_tail(core_in, states_x, gate_z, skip_in, gain_in):
    length = core_in.shape[0]
    core = core_in + skip_in[None, :, None] * states_x
    gated = core.reshape(length, DS) * jax.nn.silu(gate_z)
    return normed(gated, gain_in)


def swiglu(gate_up_out):
    return jax.nn.silu(gate_up_out[:, :FF]) * gate_up_out[:, FF:]


def swap(block, distance):
    peers = lax.axis_size("ctx")
    return lax.ppermute(block, "ctx", [(i, i ^ distance) for i in range(peers)])


def shifted(block, hops):
    peers = lax.axis_size("fsdp")
    return lax.ppermute(block, "fsdp", [(i, (i + hops) % peers) for i in range(peers)])


def powers(first, limit):
    found = []
    while first < limit:
        found.append(first)
        first *= 2
    return found


def chip_steps():
    return powers(2, lax.axis_size("ctx"))


def ordered(flag, first, second, axis):
    return jnp.where(
        flag,
        jnp.concatenate([second, first], axis),
        jnp.concatenate([first, second], axis),
    )


def halves(flag, array, axis):
    size = array.shape[axis] // 2
    low = lax.slice_in_dim(array, 0, size, axis=axis)
    high = lax.slice_in_dim(array, size, 2 * size, axis=axis)
    return (jnp.where(flag, high, low), jnp.where(flag, low, high))


def join(earlier, later):
    return (earlier[0] * later[0], later[0][:, None, None] * earlier[1] + later[1])


def either(flag, when, otherwise):
    return jax.tree.map(lambda a, b: jnp.where(flag, a, b), when, otherwise)


def entering(decay, state, place, backwards):
    def sent(pair, step):
        return (swap(pair[0], step), swap(pair[1].astype(jnp.bfloat16), step).astype(jnp.float32))

    def is_later(step):
        return (jnp.bitwise_and(place, step) != 0) != backwards

    core = jnp.bitwise_and(place, 1) == 1
    near = sent((decay, state), 1)
    total = either(is_later(1), join(near, (decay, state)), join((decay, state), near))
    total = tuple(halves(core, part, 0)[0] for part in total)
    before = (jnp.ones_like(total[0]), jnp.zeros_like(total[1]))
    steps = chip_steps()
    for step in steps:
        there = sent(total, step)
        before = either(is_later(step), join(there, before), before)
        if step != steps[-1]:
            total = either(is_later(step), join(there, total), join(total, there))
    across = swap(before[1].astype(jnp.bfloat16), 1).astype(jnp.float32)
    whole = ordered(core, before[1], across, 0)
    return jnp.where(is_later(1), near[0][:, None, None] * whole + near[1], whole)


def place_kernel(first_col, found, idx_ref, shard_ref, *refs):
    count = sum(len(side) for side in found)
    part_refs, whole_ref, sems = refs[:count], refs[count], refs[-1]
    chip, core, layer = idx_ref[0], idx_ref[1], idx_ref[2]
    depth, width = shard_ref.shape[0], whole_ref.shape[1]
    layers, rows = whole_ref.shape[0] // depth, part_refs[0].shape[1]
    columns = pl.ds(pl.multiple_of(first_col + core * width, 128), width)
    copies = [
        pltpu.make_async_copy(
            shard_ref.at[:, columns],
            whole_ref.at[pl.ds(pl.multiple_of(layer * depth, depth), depth), :],
            sems.at[0],
        )
    ]
    at = 0
    for side, groups in enumerate(found):
        for group in groups:
            for number, other in enumerate(group):
                for hop in range(layers - 1):
                    owner = lax.rem(layer + 1 + hop, layers)
                    begin = owner * depth + jnp.bitwise_xor(chip, other) * rows
                    copies.append(
                        pltpu.make_async_copy(
                            part_refs[at].at[number * (layers - 1) + hop],
                            whole_ref.at[
                                pl.ds(pl.multiple_of(begin, rows), rows),
                                pl.ds(side * (width // 2), width // 2),
                            ],
                            sems.at[len(copies)],
                        )
                    )
            at += 1
    for copy in copies:
        copy.start()
    for copy in copies:
        copy.wait()


def placed(idx, shard, first_col, found, parts):
    layers = lax.axis_size("fsdp")
    rows, width = parts[0][0].shape[1], 2 * parts[0][0].shape[2]
    depth = shard.shape[0]
    count = 1 + sum((layers - 1) * len(group) for side in found for group in side)
    flat = [part for side in parts for part in side]
    return pl.pallas_call(
        lambda *refs: place_kernel(first_col, found, *refs),
        out_shape=jax.ShapeDtypeStruct((layers * depth, width), shard.dtype),
        in_specs=[pl.BlockSpec(memory_space=pltpu.SMEM)]
        + [pl.BlockSpec(memory_space=pl.ANY)] * (1 + len(flat)),
        out_specs=pl.BlockSpec(memory_space=pltpu.VMEM),
        scratch_shapes=[pltpu.SemaphoreType.DMA((count,))],
        compiler_params=pltpu.CompilerParams(vmem_limit_bytes=32 * 1024 * 1024),
        cost_estimate=pl.CostEstimate(
            flops=0, bytes_accessed=4 * layers * depth * width, transcendentals=0
        ),
        name="place",
    )(idx, shard, *flat)


def gathered(chunks, idx, chip, core, layer):
    steps, layers = chip_steps(), lax.axis_size("fsdp")
    stages = len(steps) + 1
    pieces, along = [], {}
    for shard, first_col, width in chunks:
        rows = shard.shape[0] // (lax.axis_size("ctx") // 2)
        cut = lax.dynamic_slice_in_dim(
            shard[:, first_col : first_col + width], chip * rows, rows, 0
        )
        pieces.append(halves(core == 1, cut, 1)[0])
    along[0] = lax.all_gather(pieces[0], "fsdp")

    def others(block):
        return jnp.stack(
            [
                lax.dynamic_index_in_dim(block, lax.rem(layer + 1 + hop, layers), 0, False)
                for hop in range(layers - 1)
            ]
        )

    state, found, done = {}, {}, [None] * len(chunks)
    pieces = dict(enumerate(pieces))
    for turn in range(len(chunks) + stages - 1):
        live = [at for at in range(len(chunks)) if 0 <= turn - at < stages]
        held = ([state[at] for at in live if at in state], along, pieces)
        held, along, pieces = lax.optimization_barrier(held)
        state.update(zip([at for at in live if at in state], held, strict=True))
        if turn + 1 < len(chunks):
            along[turn + 1] = lax.all_gather(pieces[turn + 1], "fsdp")
        if turn in along:
            rest, width = others(along.pop(turn)), chunks[turn][2] // 2
            state[turn] = [[rest[:, :, : width // 2]], [rest[:, :, width // 2 :]]]
            found[turn] = [[[0]], [[0]]]
        for at in live:
            stage = turn - at
            if stage < len(steps):
                for side in range(2):
                    step = (steps[side:] + steps[:side])[stage]
                    have = state[at][side]
                    block = jnp.concatenate(have, 0) if len(have) > 1 else have[0]
                    state[at][side] = have + [swap(block, step)]
                    reached = [other for group in found[at][side] for other in group]
                    found[at][side] = found[at][side] + [
                        [other ^ (step // 2) for other in reached]
                    ]
            else:
                own = placed(idx, chunks[at][0], chunks[at][1], found[at], state[at])
                done[at] = (own, swap(own, 1))
    return done


def tile_of(width):
    return max(tile for tile in range(128, 1025, 128) if width % tile == 0)


def forth_kernel(idx_ref, left_ref, own_ref, other_ref, out_ref):
    for side, part_ref in enumerate((own_ref, other_ref)):

        @pl.when(pl.program_id(0) == side)
        def _():
            out_ref[...] = jnp.dot(
                left_ref[...], part_ref[...], preferred_element_type=jnp.float32
            ).astype(out_ref.dtype)


def back_kernel(idx_ref, grad_ref, own_ref, other_ref, out_ref):
    @pl.when((pl.program_id(0) == 0) & (pl.program_id(1) == 0))
    def _():
        out_ref[...] = jnp.zeros_like(out_ref)

    for side, part_ref in enumerate((own_ref, other_ref)):

        @pl.when(pl.program_id(0) == side)
        def _():
            out_ref[...] += lax.dot_general(
                grad_ref[...],
                part_ref[...],
                (((1,), (1,)), ((), ())),
                preferred_element_type=jnp.float32,
            )


def product_specs(depth, width):
    tile = tile_of(width)
    count = width // tile
    return (
        tile,
        count,
        pl.BlockSpec((depth, tile), lambda s, t, idx: (0, jnp.where(s == 0, t, count - 1))),
        pl.BlockSpec((depth, tile), lambda s, t, idx: (0, jnp.where(s == 0, 0, t))),
        lambda s, t, idx: (0, jnp.bitwise_xor(idx[1], s) * count + t),
    )


def forth(idx, left_side, chunk, kind=jnp.float32):
    rows, (depth, width) = left_side.shape[0], chunk[0].shape
    tile, count, own_spec, other_spec, place = product_specs(depth, width)
    return pl.pallas_call(
        forth_kernel,
        grid_spec=pltpu.PrefetchScalarGridSpec(
            num_scalar_prefetch=1,
            grid=(2, count),
            in_specs=[pl.BlockSpec((rows, depth), lambda s, t, idx: (0, 0)), own_spec, other_spec],
            out_specs=pl.BlockSpec((rows, tile), place),
        ),
        out_shape=jax.ShapeDtypeStruct((rows, 2 * width), kind),
        compiler_params=pltpu.CompilerParams(vmem_limit_bytes=40 * 1024 * 1024),
        cost_estimate=pl.CostEstimate(
            flops=4 * rows * depth * width, bytes_accessed=4 * depth * width, transcendentals=0
        ),
        name="forth",
    )(idx, left_side, *chunk)


def back(idx, grad_in, chunk):
    rows, (depth, width) = grad_in.shape[0], chunk[0].shape
    tile, count, own_spec, other_spec, place = product_specs(depth, width)
    return pl.pallas_call(
        back_kernel,
        grid_spec=pltpu.PrefetchScalarGridSpec(
            num_scalar_prefetch=1,
            grid=(2, count),
            in_specs=[pl.BlockSpec((rows, tile), place), own_spec, other_spec],
            out_specs=pl.BlockSpec((rows, depth), lambda s, t, idx: (0, 0)),
        ),
        out_shape=jax.ShapeDtypeStruct((rows, depth), jnp.float32),
        compiler_params=pltpu.CompilerParams(vmem_limit_bytes=40 * 1024 * 1024),
        cost_estimate=pl.CostEstimate(
            flops=4 * rows * depth * width, bytes_accessed=4 * depth * width, transcendentals=0
        ),
        name="back",
    )(idx, grad_in, *chunk)


def dealt(array, layer):
    peers = lax.axis_size("fsdp")
    width = array.shape[1] // peers

    def cut(hops):
        return lax.dynamic_slice_in_dim(array, lax.rem(layer + hops, peers) * width, width, 1)

    ahead = [cut(0)] + [shifted(cut(peers - hops), peers - hops) for hops in range(1, peers)]
    twice = jnp.concatenate(ahead + ahead, 0)
    length = array.shape[0]
    return lax.dynamic_slice_in_dim(
        twice, lax.rem(peers - layer, peers) * length, peers * length, 0
    )


def every(block):
    return lax.all_gather(block, "fsdp", axis=0, tiled=True)


def added(left_side, right_side):
    return (left_side.astype(jnp.float32) + right_side.astype(jnp.float32)).astype(jnp.bfloat16)


def plane_sum(part, place, core):
    steps = chip_steps()
    own, other = halves(core == 1, part, 1)
    own = added(own, swap(other, 1))
    size = own.shape[0] // 2
    sides = []
    for side in range(2):
        order = steps[side:] + steps[:side]
        block = own[side * size : (side + 1) * size]
        for step in order:
            keep, send = halves(jnp.bitwise_and(place, step) != 0, block, 0)
            block = added(keep, swap(send, step))
        for step in order[::-1]:
            block = ordered(jnp.bitwise_and(place, step) != 0, block, swap(block, step), 0)
        sides.append(block)
    own = jnp.concatenate(sides, 0)
    return (own, swap(own, 1))


def finish_kernel(widths, idx_ref, *refs):
    out_ref = refs[-1]
    for flag in (0, 1):

        @pl.when(idx_ref[1] == flag)
        def _():
            at = 0
            for number, width in enumerate(widths):
                pair = refs[2 * number : 2 * number + 2]
                low, high = pair[flag], pair[1 - flag]
                half = low.shape[1]
                out_ref[:, at : at + half] = low[...].astype(jnp.float32)
                out_ref[:, at + half : at + width] = high[:, : width - half].astype(jnp.float32)
                at += width


def finished(idx, pairs, widths, first_row=0, rows=None):
    rows = rows or pairs[0][0].shape[0]
    block = 32
    while block < 256 and rows % (2 * block) == 0 and first_row % (2 * block) == 0:
        block *= 2
    while block > 32 and block * sum(widths) > 1024 * 1024:
        block //= 2
    skip = first_row // block
    flat = [part for pair in pairs for part in pair]
    return pl.pallas_call(
        lambda *refs: finish_kernel(widths, *refs),
        grid=(rows // block,),
        out_shape=jax.ShapeDtypeStruct((rows, sum(widths)), jnp.float32),
        in_specs=[pl.BlockSpec(memory_space=pltpu.SMEM)]
        + [pl.BlockSpec((block, part.shape[1]), lambda i: (i + skip, 0)) for part in flat],
        out_specs=pl.BlockSpec((block, sum(widths)), lambda i: (i, 0)),
        compiler_params=pltpu.CompilerParams(vmem_limit_bytes=32 * 1024 * 1024),
        cost_estimate=pl.CostEstimate(
            flops=0, bytes_accessed=6 * rows * sum(widths), transcendentals=0
        ),
        name="finish",
    )(idx, *flat)


def sum_of_all(arrays):
    flat = jnp.concatenate([array.reshape(-1) for array in arrays])
    size = flat.shape[0]
    flat = jnp.pad(flat, (0, -size % 1024)).reshape(-1, 128)
    for axis in ("ctx", "fsdp"):
        peers = lax.axis_size(axis)
        for step in powers(1, peers):
            flat = flat + lax.ppermute(flat, axis, [(i, i ^ step) for i in range(peers)])
    flat, found, at = flat.reshape(-1), [], 0
    for array in arrays:
        found.append(flat[at : at + array.size].reshape(array.shape))
        at += array.size
    return found


def body(
    tokens,
    cotangent,
    doc_ids,
    in_proj,
    dt_proj,
    conv_weight,
    conv_bias,
    dt_bias,
    a_log,
    d_skip,
    mixer_gain,
    out_proj,
    qkv_proj,
    o_proj,
    first_gain,
    second_gain,
    gate_up,
    down_proj,
):
    hidden = tokens[0].astype(jnp.float32)
    grad_out = cotangent[0].astype(jnp.float32)
    own_ids = doc_ids[0]
    length = hidden.shape[0]
    my_index = lax.axis_index("ctx")
    all_ids = own_ids.reshape(1, length)
    for step in powers(1, lax.axis_size("ctx")):
        all_ids = ordered(
            jnp.bitwise_and(my_index, step) != 0, all_ids, swap(all_ids, step), 0
        )
    all_ids = all_ids.reshape(-1)
    first_row = my_index * length
    places = first_row + jnp.arange(length, dtype=jnp.int32)
    before = first_row - (KC - 1) + jnp.arange(KC - 1, dtype=jnp.int32)
    earlier_ids = lax.dynamic_slice_in_dim(all_ids, jnp.maximum(first_row - (KC - 1), 0), KC - 1, 0)
    earlier_ids = jnp.where(before >= 0, earlier_ids, -1)
    pad_ids = jnp.concatenate([earlier_ids, own_ids], 0)
    prev_id = jnp.where(my_index > 0, all_ids[jnp.maximum(first_row - 1, 0)], -1)
    core = jnp.bitwise_and(my_index, 1)
    layer = lax.axis_index("fsdp")
    layers = lax.axis_size("fsdp")
    idx = jnp.stack([my_index // 2, core, layer]).astype(jnp.int32)
    z_qkv_dt = jnp.concatenate(
        [
            in_proj[:, :DS],
            qkv_proj,
            dt_proj,
            jnp.zeros((qkv_proj.shape[0], 512 - NH), jnp.bfloat16),
        ],
        1,
    )
    out_o = jnp.concatenate([out_proj, o_proj], 0)
    conv_w, zqd_w, oo_w, gate_w, up_w, down_w = gathered(
        [
            (in_proj, DS, DS + 2 * NS),
            (z_qkv_dt, 0, z_qkv_dt.shape[1]),
            (out_o, 0, D),
            (gate_up, 0, FF),
            (gate_up, FF, FF),
            (down_proj, 0, D),
        ],
        idx,
        my_index // 2,
        core,
        layer,
    )
    qkv_end = DS + (HQ + 2 * HK) * HA

    def interleaved(mixed_in, attended_in):
        return jnp.concatenate(
            [
                mixed_in.reshape(length, layers, DS // layers),
                attended_in.reshape(length, layers, HQ * HA // layers),
            ],
            2,
        ).reshape(length, DS + HQ * HA)

    def parted(both):
        both = both.reshape(length, layers, (DS + HQ * HA) // layers)
        return (
            both[:, :, : DS // layers].reshape(length, DS),
            both[:, :, DS // layers :].reshape(length, HQ * HA),
        )

    normed_in, norm_pull = jax.vjp(normed, hidden, first_gain)
    input_low = normed_in.astype(jnp.bfloat16)
    conv_low = forth(idx, input_low, conv_w, jnp.bfloat16)
    zqd_out = forth(idx, input_low, zqd_w)
    gate_z = zqd_out[:, :DS]
    attn_in = zqd_out[:, DS:qkv_end]
    step_raw = zqd_out[:, qkv_end : qkv_end + NH]
    tail_low = from_behind(conv_low[length - (KC - 1) :], "ctx", 1)

    def front_fn(conv_in, tail_in, shift_in, kernel_in, bias_in, bias_step, log_rate):
        padded = jnp.concatenate([tail_in, conv_in], 0)
        activated = jax.nn.silu(convolve(padded, pad_ids, own_ids, kernel_in, bias_in))
        states_x = activated[:, :DS].reshape(length, NH, HP)
        b_matrix = activated[:, DS : DS + NS]
        c_matrix = activated[:, DS + NS :]
        step_size = jax.nn.softplus(shift_in + bias_step)
        log_decay = -step_size * jnp.exp(log_rate)
        y_part, local_state = ssm_local(states_x, step_size, log_decay, b_matrix, c_matrix, own_ids)
        return (y_part, local_state, states_x, c_matrix, log_decay)

    front_out, front_pull = jax.vjp(
        front_fn,
        conv_low.astype(jnp.float32),
        tail_low.astype(jnp.float32),
        step_raw,
        conv_weight,
        conv_bias,
        dt_bias,
        a_log,
    )
    y_part, local_state, states_x, c_matrix, log_decay = front_out
    decay_now, decay_pull = jax.vjp(lambda log_in: block_decay(log_in, own_ids, prev_id), log_decay)
    state_in = entering(decay_now, local_state, my_index, False)
    y_carry, carry_pull = jax.vjp(
        lambda c_in, log_in, state_arg: ssm_carry(c_in, log_in, own_ids, prev_id, state_arg),
        c_matrix,
        log_decay,
        state_in,
    )
    mixer_normed, tail_pull = jax.vjp(
        mixer_tail, y_part + y_carry, states_x, gate_z, d_skip, mixer_gain
    )
    mixer_low = mixer_normed.astype(jnp.bfloat16)
    groups = HQ // HK
    scale = HA ** (-0.5)
    query_low = rotate(attn_in[:, : HQ * HA].reshape(length, HQ, HA), places, 1.0).astype(
        jnp.bfloat16
    )
    key_low = rotate(
        attn_in[:, HQ * HA : (HQ + HK) * HA].reshape(length, HK, HA), places, 1.0
    ).astype(jnp.bfloat16)
    value_low = attn_in[:, (HQ + HK) * HA :].reshape(length, HK, HA).astype(jnp.bfloat16)
    query_groups = query_low.reshape(length, HK, groups, HA)
    top_now = jnp.full((HK, groups, length), -1e30, jnp.float32)
    both_all = lax.all_gather(
        jnp.concatenate([key_low, value_low], 1), "ctx", axis=0, tiled=True
    )
    key_piece, value_piece = both_all[:, :HK], both_all[:, HK:]
    key_ids = all_ids
    width = key_piece.shape[0]
    key_places = jnp.arange(width, dtype=jnp.int32)
    score = (
        jnp.einsum("qkgd,rkd->kgqr", query_groups, key_piece, preferred_element_type=jnp.float32)
        * scale
    )
    allowed = (places[:, None] >= key_places[None, :]) & (own_ids[:, None] == key_ids[None, :])
    score = jnp.where(allowed[None, None], score, -1e30)
    new_top = jnp.maximum(top_now, jnp.max(score, axis=-1))
    weight = jnp.where(allowed[None, None], jnp.exp(score - new_top[..., None]), 0.0)
    total = jnp.sum(weight, axis=-1)
    accum = jnp.einsum(
        "kgqr,rkd->qkgd",
        weight.astype(jnp.bfloat16),
        value_piece,
        preferred_element_type=jnp.float32,
    )
    accum, top_now, total = (accum, new_top, total)
    attended = accum / jnp.transpose(total, (2, 0, 1))[..., None]
    log_total = top_now + jnp.log(total)
    attended_low = attended.reshape(length, HQ * HA).astype(jnp.bfloat16)
    branches_low = interleaved(mixer_low, attended_low)
    middle = hidden + forth(idx, branches_low, oo_w)
    normed_mid, mid_pull = jax.vjp(normed, middle, second_gain)
    mid_low = normed_mid.astype(jnp.bfloat16)
    gate_up_out = jnp.concatenate([forth(idx, mid_low, gate_w), forth(idx, mid_low, up_w)], 1)
    act_value, act_pull = jax.vjp(swiglu, gate_up_out)
    act_low = act_value.astype(jnp.bfloat16)
    mixed = middle + forth(idx, act_low, down_w)
    grad_low = grad_out.astype(jnp.bfloat16)
    d_act = back(idx, grad_low, down_w)
    gu_low = act_pull(d_act)[0].astype(jnp.bfloat16)
    d_mid_norm = back(idx, gu_low[:, :FF], gate_w) + back(idx, gu_low[:, FF:], up_w)
    d_middle_part, d_second_gain = mid_pull(d_mid_norm)
    d_middle = grad_out + d_middle_part
    branch_low = d_middle.astype(jnp.bfloat16)
    d_mixer_norm, d_attended = parted(back(idx, branch_low, oo_w))
    d_out_low = d_attended.reshape(length, HK, groups, HA).astype(jnp.bfloat16)
    delta = jnp.transpose(jnp.sum(d_out_low.astype(jnp.float32) * attended, axis=-1), (1, 2, 0))
    keys_all, values_all = key_piece, value_piece
    seq_len = keys_all.shape[0]
    block = min(seq_len, 512)

    def key_block(d_query, block_index):
        begin = block_index * block
        key_part = lax.dynamic_slice_in_dim(keys_all, begin, block, 0)
        value_part = lax.dynamic_slice_in_dim(values_all, begin, block, 0)
        key_ids = lax.dynamic_slice_in_dim(all_ids, begin, block, 0)
        key_places = begin + jnp.arange(block, dtype=jnp.int32)
        score = (
            jnp.einsum("qkgd,rkd->kgqr", query_groups, key_part, preferred_element_type=jnp.float32)
            * scale
        )
        allowed = (places[:, None] >= key_places[None, :]) & (own_ids[:, None] == key_ids[None, :])
        prob = jnp.where(
            allowed[None, None],
            jnp.exp(jnp.where(allowed[None, None], score, 0.0) - log_total[..., None]),
            0.0,
        )
        d_prob = jnp.einsum(
            "qkgd,rkd->kgqr", d_out_low, value_part, preferred_element_type=jnp.float32
        )
        score_grad = (prob * (d_prob - delta[..., None])).astype(jnp.bfloat16)
        d_query = (
            d_query
            + jnp.einsum("kgqr,rkd->qkgd", score_grad, key_part, preferred_element_type=jnp.float32)
            * scale
        )
        d_keys = (
            jnp.einsum(
                "kgqr,qkgd->rkd", score_grad, query_groups, preferred_element_type=jnp.float32
            )
            * scale
        )
        d_values = jnp.einsum(
            "kgqr,qkgd->rkd",
            prob.astype(jnp.bfloat16),
            d_out_low,
            preferred_element_type=jnp.float32,
        )
        return (d_query, jnp.concatenate([d_keys, d_values], 1).reshape(block, 2 * HK * HA))

    d_query, kv_terms = lax.scan(
        key_block,
        jnp.zeros((length, HK, groups, HA), jnp.float32),
        jnp.arange(seq_len // block, dtype=jnp.int32),
    )
    d_kv = lax.psum_scatter(
        kv_terms.reshape(seq_len, 2 * HK * HA).astype(jnp.bfloat16),
        "ctx",
        scatter_dimension=0,
        tiled=True,
    ).astype(jnp.float32)
    d_attn_in = jnp.concatenate(
        [
            rotate(d_query.reshape(length, HQ, HA), places, -1.0).reshape(length, HQ * HA),
            rotate(d_kv[:, : HK * HA].reshape(length, HK, HA), places, -1.0).reshape(
                length, HK * HA
            ),
            d_kv[:, HK * HA :],
        ],
        1,
    )
    qkv_low = d_attn_in.astype(jnp.bfloat16)
    d_core, d_states_tail, d_gate_z, d_d_skip, d_mixer_gain = tail_pull(d_mixer_norm)
    d_c_carry, d_log_carry, d_state_in = carry_pull(d_core)
    later_grad = entering(decay_now, d_state_in, my_index, True)
    d_decay = jnp.sum(later_grad * state_in, axis=(1, 2))
    d_log_decay = decay_pull(d_decay)[0]
    d_conv_in, d_tail, d_step_raw, d_conv_weight, d_conv_bias, d_dt_bias, d_a_log = front_pull(
        (d_core, later_grad, d_states_tail, d_c_carry, d_log_carry + d_log_decay)
    )
    from_next = from_behind(d_tail.astype(jnp.bfloat16), "ctx", -1).astype(d_tail.dtype)
    d_conv_in = jnp.concatenate(
        [d_conv_in[: length - (KC - 1)], d_conv_in[length - (KC - 1) :] + from_next], 0
    )
    z_low = d_gate_z.astype(jnp.bfloat16)
    blank = jnp.zeros((length, 512 - NH), jnp.bfloat16)
    conv_grad_low = d_conv_in.astype(jnp.bfloat16)
    step_low = d_step_raw.astype(jnp.bfloat16)
    d_normed_in = back(idx, conv_grad_low, conv_w) + back(
        idx, jnp.concatenate([z_low, qkv_low, step_low, blank], 1), zqd_w
    )
    d_hidden_part, d_first_gain = norm_pull(d_normed_in)
    d_tokens = d_middle + d_hidden_part

    def weight_grad(act_in, grad_in):
        part = lax.dot_general(
            act_in, grad_in, (((0,), (0,)), ((), ())), preferred_element_type=jnp.float32
        ).astype(jnp.bfloat16)
        return plane_sum(part, my_index, core)

    input_mine = dealt(input_low, layer)
    down_pair = weight_grad(dealt(act_low, layer), every(grad_low))
    gate_up_pair = weight_grad(dealt(mid_low, layer), every(gu_low))
    oo_pair = weight_grad(dealt(branches_low, layer), every(branch_low))
    z_pair = weight_grad(input_mine, every(z_low))
    qkv_pair = weight_grad(input_mine, every(qkv_low))
    tail_cols = DS + 2 * NS
    tail_pair = weight_grad(
        input_mine, every(jnp.concatenate([conv_grad_low, step_low, blank[:, : 256 - NH]], 1))
    )
    tail_half = tail_pair[0].shape[1]
    summed = (
        finished(idx, [z_pair, tail_pair], [DS, tail_cols]),
        jnp.where(core == 1, tail_pair[0], tail_pair[1])[
            :, tail_cols - tail_half : tail_cols - tail_half + NH
        ].astype(jnp.float32),
        finished(idx, [oo_pair], [D], 0, DS // layers),
        finished(idx, [qkv_pair], [(HQ + 2 * HK) * HA]),
        finished(idx, [oo_pair], [D], DS // layers, HQ * HA // layers),
        finished(idx, [gate_up_pair], [2 * FF]),
        finished(idx, [down_pair], [D]),
    )
    smalls = sum_of_all(
        (
            d_conv_weight,
            d_conv_bias,
            d_dt_bias,
            d_a_log,
            d_d_skip,
            d_mixer_gain,
            d_first_gain,
            d_second_gain,
        )
    )
    return (
        mixed[None].astype(jnp.bfloat16),
        d_tokens[None],
        summed[0],
        summed[1],
        smalls[0],
        smalls[1],
        smalls[2],
        smalls[3],
        smalls[4],
        smalls[5],
        summed[2],
        summed[3],
        summed[4],
        smalls[6],
        smalls[7],
        summed[5],
        summed[6],
    )


def solution(mesh):
    return jax.shard_map(
        body,
        mesh=mesh,
        in_specs=(
            P("fsdp", "ctx", None),
            P("fsdp", "ctx", None),
            P("fsdp", "ctx"),
            P("fsdp", None),
            P("fsdp", None),
            P(),
            P(),
            P(),
            P(),
            P(),
            P(),
            P("fsdp", None),
            P("fsdp", None),
            P("fsdp", None),
            P(),
            P(),
            P("fsdp", None),
            P("fsdp", None),
        ),
        out_specs=(
            P("fsdp", "ctx", None),
            P("fsdp", "ctx", None),
            P("fsdp", None),
            P("fsdp", None),
            P(),
            P(),
            P(),
            P(),
            P(),
            P(),
            P("fsdp", None),
            P("fsdp", None),
            P("fsdp", None),
            P(),
            P(),
            P("fsdp", None),
            P("fsdp", None),
        ),
        check_vma=False,
    )
```

```python
import jax
import jax.numpy as jnp
from jax import lax
from jax.experimental import pallas as pl
from jax.experimental.pallas import tpu as pltpu
from jax.sharding import PartitionSpec as P

D = 2048
FF = 4096
NH = 48
HP = 64
NS = 256
KC = 4
HQ = 8
HK = 2
HA = 128
DS = 3072


HIGH = lax.Precision.HIGHEST
epsilon = 1e-05
rope_base = 100000000000.0


def from_behind(block, axis, distance):
    devices = range(lax.axis_size(axis))
    route = [(i - distance, i) for i in devices if i - distance in devices]
    return lax.ppermute(block, axis, route)


def normed(operand, gain_vec):
    return (
        operand
        * lax.rsqrt(jnp.mean(operand * operand, axis=-1, keepdims=True) + epsilon)
        * gain_vec
    )


def rotate(operand, places, direction):
    half_width = operand.shape[-1] // 2
    frequency = rope_base ** (
        -jnp.arange(half_width, dtype=jnp.float32) * (2.0 / operand.shape[-1])
    )
    angles = places.astype(jnp.float32)[:, None] * frequency[None, :]
    cosine = jnp.cos(angles)[:, None, :]
    sine_part = direction * jnp.sin(angles)[:, None, :]
    first_half = operand[..., :half_width]
    second_half = operand[..., half_width:]
    return jnp.concatenate(
        [
            first_half * cosine - second_half * sine_part,
            second_half * cosine + first_half * sine_part,
        ],
        -1,
    )


def project(left_side, right_side):
    return jnp.dot(left_side, right_side, preferred_element_type=jnp.float32)


def project_back(grad_in, weight):
    return lax.dot_general(
        grad_in, weight, (((1,), (1,)), ((), ())), preferred_element_type=jnp.float32
    )


def convolve(padded, pad_ids, row_ids, kernel_in, bias_in):
    length = row_ids.shape[0]
    total = jnp.zeros((length, padded.shape[1]), jnp.float32) + bias_in[None, :]
    for offset in range(KC):
        same_doc = (pad_ids[offset : offset + length] == row_ids).astype(jnp.float32)
        total = (
            total
            + kernel_in[offset][None, :] * padded[offset : offset + length] * same_doc[:, None]
        )
    return total


def ssm_local(states_x, step_size, log_decay, b_matrix, c_matrix, row_ids):
    length = states_x.shape[0]
    running = jnp.cumsum(log_decay, axis=0)
    places = jnp.arange(length, dtype=jnp.int32)
    allowed = (places[:, None] >= places[None, :]) & (row_ids[:, None] == row_ids[None, :])
    spread = running.T[:, :, None] - running.T[:, None, :]
    decay_matrix = jnp.where(allowed[None], jnp.exp(jnp.where(allowed[None], spread, 0.0)), 0.0)
    intersection = jnp.dot(c_matrix, b_matrix.T, precision=HIGH, preferred_element_type=jnp.float32)
    driven = step_size[:, :, None] * states_x
    y_part = jnp.einsum("hts,shp->thp", decay_matrix * intersection[None], driven, precision=HIGH)
    to_end = jnp.where(
        (row_ids == row_ids[-1])[:, None], jnp.exp(running[-1][None, :] - running), 0.0
    )
    local_state = jnp.einsum("sh,shp,sn->hpn", to_end, driven, b_matrix, precision=HIGH)
    return (y_part, local_state)


def ssm_carry(c_matrix, log_decay, row_ids, prev_id, state_in):
    kept_mask = (row_ids == prev_id).astype(jnp.float32)
    weight = jnp.exp(jnp.cumsum(log_decay, axis=0)) * kept_mask[:, None]
    return weight[:, :, None] * jnp.einsum("hpn,tn->thp", state_in, c_matrix, precision=HIGH)


def block_decay(log_decay, row_ids, prev_id):
    return jnp.exp(jnp.sum(log_decay, axis=0)) * (row_ids[-1] == prev_id).astype(jnp.float32)


def mixer_tail(core_in, states_x, gate_z, skip_in, gain_in):
    length = core_in.shape[0]
    core = core_in + skip_in[None, :, None] * states_x
    gated = core.reshape(length, DS) * jax.nn.silu(gate_z)
    return normed(gated, gain_in)


def swiglu(gate_up_out):
    return jax.nn.silu(gate_up_out[:, :FF]) * gate_up_out[:, FF:]


def swap(block, distance):
    peers = lax.axis_size("ctx")
    return lax.ppermute(block, "ctx", [(i, i ^ distance) for i in range(peers)])


def shifted(block, hops):
    peers = lax.axis_size("fsdp")
    return lax.ppermute(block, "fsdp", [(i, (i + hops) % peers) for i in range(peers)])


def powers(first, limit):
    found = []
    while first < limit:
        found.append(first)
        first *= 2
    return found


def chip_steps():
    return powers(2, lax.axis_size("ctx"))


def ordered(flag, first, second, axis):
    return jnp.where(
        flag,
        jnp.concatenate([second, first], axis),
        jnp.concatenate([first, second], axis),
    )


def halves(flag, array, axis):
    size = array.shape[axis] // 2
    low = lax.slice_in_dim(array, 0, size, axis=axis)
    high = lax.slice_in_dim(array, size, 2 * size, axis=axis)
    return (jnp.where(flag, high, low), jnp.where(flag, low, high))


def join(earlier, later):
    return (earlier[0] * later[0], later[0][:, None, None] * earlier[1] + later[1])


def either(flag, when, otherwise):
    return jax.tree.map(lambda a, b: jnp.where(flag, a, b), when, otherwise)


class Last:
    def __init__(self, value):
        self.value = value


class Task:
    def __init__(self, steps):
        self.steps, self.ready, self.result = steps, None, None


class Rounds:
    def __init__(self):
        self.tasks = []

    def start(self, steps):
        self.tasks.append(Task(steps))
        return self.tasks[-1]

    def turn(self, values=()):
        found = []
        for task in self.tasks:
            try:
                found.append(task.steps.send(task.ready))
            except StopIteration:
                found.append(Last(()))
        held = [step.value if isinstance(step, Last) else step for step in found]
        values, held = lax.optimization_barrier((values, held))
        going = []
        for task, step, ready in zip(self.tasks, found, held, strict=True):
            task.ready = ready
            if isinstance(step, Last):
                task.result = ready
            else:
                going.append(task)
        self.tasks = going
        return values

    def until(self, *tasks):
        while any(task.result is None for task in tasks):
            self.turn()

    def until_ready(self, *weights):
        while any(weight.ready is None for weight in weights):
            self.turn()


def entering_steps(decay, state, place, backwards):
    def sent(pair, step):
        return (swap(pair[0], step), swap(pair[1].astype(jnp.bfloat16), step))

    def read(pair):
        return (pair[0], pair[1].astype(jnp.float32))

    def is_later(step):
        return (jnp.bitwise_and(place, step) != 0) != backwards

    core = jnp.bitwise_and(place, 1) == 1
    near = read(sent((decay, state), 1))
    total = either(is_later(1), join(near, (decay, state)), join((decay, state), near))
    total = tuple(halves(core, part, 0)[0] for part in total)
    before = (jnp.ones_like(total[0]), jnp.zeros_like(total[1]))
    steps = chip_steps()
    for step in steps:
        there = read(sent(total, step))
        before = either(is_later(step), join(there, before), before)
        if step != steps[-1]:
            total = either(is_later(step), join(there, total), join(total, there))
            total, before, near = yield total, before, near
    across = swap(before[1].astype(jnp.bfloat16), 1).astype(jnp.float32)
    whole = ordered(core, before[1], across, 0)
    yield Last(jnp.where(is_later(1), near[0][:, None, None] * whole + near[1], whole))


class Weight:
    def __init__(self, shard, width):
        self.shard, self.width, self.chunks, self.ready = shard, width, [], None

    def cuts(self, idx, rows, columns):
        chip, core = idx[0], idx[1]
        per = rows * (lax.axis_size("ctx") // 2)
        for first_row in range(0, self.shard.shape[0], per):
            for first_col in range(0, self.width // 2, columns):
                piece = lax.dynamic_slice(
                    self.shard,
                    (first_row + chip * rows, first_col + core * (self.width // 2)),
                    (rows, columns),
                )
                self.chunks.append((first_row, first_col, []))
                yield piece, self.chunks[-1][2]


class Box:
    def __init__(self, value):
        self.value = value


def copy_all(copies):
    for copy in copies:
        copy.start()
    for copy in copies:
        copy.wait()


def place_kernel(chunks, idx_ref, shard_ref, *refs):
    whole_ref, sems = refs[-2], refs[-1]
    chip, core, layer = idx_ref[0], idx_ref[1], idx_ref[2]
    depth, width = shard_ref.shape[0], whole_ref.shape[1]
    layers = whole_ref.shape[0] // depth
    copies = [
        pltpu.make_async_copy(
            shard_ref.at[:, pl.ds(pl.multiple_of(core * width, 128), width)],
            whole_ref.at[pl.ds(pl.multiple_of(layer * depth, depth), depth), :],
            sems.at[0],
        )
    ]
    for first_row, first_col, found in chunks:
        for side, others, source, first in found:
            rows, columns = refs[source].shape[1:]
            for number, other in enumerate(others):
                for hop in range(layers - 1):
                    owner = lax.rem(layer + 1 + hop, layers)
                    begin = owner * depth + first_row + jnp.bitwise_xor(chip, other) * rows
                    copies.append(
                        pltpu.make_async_copy(
                            refs[source].at[first + number * (layers - 1) + hop],
                            whole_ref.at[
                                pl.ds(pl.multiple_of(begin, rows), rows),
                                pl.ds(first_col + side * columns, columns),
                            ],
                            sems.at[len(copies)],
                        )
                    )
    copy_all(copies)


def placed(idx, weight):
    layers = lax.axis_size("fsdp")
    depth, width = weight.shard.shape[0], weight.width // 2
    boxes = list({id(box): box for _, _, found in weight.chunks for _, _, box, _ in found}.values())
    chunks = [
        (
            first_row,
            first_col,
            [(side, others, boxes.index(box), first) for side, others, box, first in found],
        )
        for first_row, first_col, found in weight.chunks
    ]
    count = 1 + sum(
        (layers - 1) * len(others) for _, _, found in chunks for _, others, _, _ in found
    )
    return pl.pallas_call(
        lambda *refs: place_kernel(chunks, *refs),
        out_shape=jax.ShapeDtypeStruct((layers * depth, width), weight.shard.dtype),
        in_specs=[pl.BlockSpec(memory_space=pltpu.SMEM)]
        + [pl.BlockSpec(memory_space=pl.ANY)] * (1 + len(boxes)),
        out_specs=pl.BlockSpec(memory_space=pltpu.VMEM),
        scratch_shapes=[pltpu.SemaphoreType.DMA((count,))],
        compiler_params=pltpu.CompilerParams(vmem_limit_bytes=32 * 1024 * 1024),
        cost_estimate=pl.CostEstimate(
            flops=0, bytes_accessed=4 * layers * depth * width, transcendentals=0
        ),
        name="place",
    )(idx, weight.shard, *[box.value for box in boxes])


def pack_kernel(fresh, plan, inputs, idx_ref, *refs):
    layer = idx_ref[2]
    outs, sems = refs[inputs:-1], refs[-1]
    copies = []
    for out, first, side in fresh:
        layers, columns = refs[0].shape[0], outs[out].shape[2]
        for hop in range(layers - 1):
            owner = lax.rem(layer + 1 + hop, layers)
            copies.append(
                pltpu.make_async_copy(
                    refs[0].at[owner, :, pl.ds(side * columns, columns)],
                    outs[out].at[first + hop],
                    sems.at[len(copies)],
                )
            )
    for out, first, source, begin, size in plan:
        copies.append(
            pltpu.make_async_copy(
                refs[source].at[pl.ds(begin, size)],
                outs[out].at[pl.ds(first, size)],
                sems.at[len(copies)],
            )
        )
    copy_all(copies)


def packed(idx, along, fresh, plan, sizes, rows, columns):
    boxes = list({id(entry[2]): entry[2] for entry in plan}.values())
    arrays = ([] if along is None else [along]) + [box.value for box in boxes]
    skip = len(arrays) - len(boxes)
    plan = [(out, row, skip + boxes.index(box), begin, size) for out, row, box, begin, size in plan]
    count = len(fresh) * (lax.axis_size("fsdp") - 1) + len(plan)
    return pl.pallas_call(
        lambda *refs: pack_kernel(fresh, plan, len(arrays), *refs),
        out_shape=[jax.ShapeDtypeStruct((size, rows, columns), jnp.bfloat16) for size in sizes],
        in_specs=[pl.BlockSpec(memory_space=pltpu.SMEM)]
        + [pl.BlockSpec(memory_space=pl.ANY)] * len(arrays),
        out_specs=[pl.BlockSpec(memory_space=pltpu.VMEM)] * len(sizes),
        scratch_shapes=[pltpu.SemaphoreType.DMA((count,))],
        compiler_params=pltpu.CompilerParams(vmem_limit_bytes=32 * 1024 * 1024),
        cost_estimate=pl.CostEstimate(
            flops=0, bytes_accessed=4 * sum(sizes) * rows * columns, transcendentals=0
        ),
        name="pack",
    )(idx, *arrays)


def gather_steps(idx, weights, rows, columns):
    steps, layers = chip_steps(), lax.axis_size("fsdp")
    half, near = columns // 2, layers - 1
    pieces, sinks, owners = [], [], []
    for weight in weights:
        for piece, sink in weight.cuts(idx, rows, columns):
            pieces.append(piece)
            sinks.append(sink)
            owners.append(weight)
    along, flying = {}, []
    for turn in range(len(pieces) + 2 * len(steps) + 2):
        if turn < len(pieces):
            along[turn] = lax.all_gather(pieces[turn], "fsdp")
        fresh, plan, sizes, comes = [], [], {step: 0 for step in steps}, []
        used = []
        for stage in range(len(steps)):
            at = turn - 1 - 2 * stage
            if not 0 <= at < len(pieces):
                continue
            for side in range(2):
                step = (steps[side:] + steps[:side])[stage]
                out = steps.index(step)
                first = sizes[step]
                reached = []
                if stage == 0:
                    fresh.append((out, first, side))
                    used.append((at, side, [0], step, first))
                    reached, sizes[step] = [0], first + near
                for _, others, box, begin in [e for e in sinks[at] if e[0] == side]:
                    plan.append((out, sizes[step], box, begin, near * len(others)))
                    sizes[step] += near * len(others)
                    reached = reached + others
                comes.append((at, side, [other ^ (step // 2) for other in reached], step, first))
        active = [step for step in steps if sizes[step]]
        blocks = {}
        if active:
            rank = {steps.index(step): number for number, step in enumerate(active)}
            made = packed(
                idx,
                along.pop(turn - 1, None) if fresh else None,
                [(rank[out], first, side) for out, first, side in fresh],
                [(rank[out], *rest) for out, *rest in plan],
                [sizes[step] for step in active],
                rows,
                half,
            )
            blocks = dict(zip(active, made, strict=True))
        blocks, pieces = lax.optimization_barrier((blocks, pieces))
        got = {step: swap(block, step) for step, block in blocks.items()}
        whole = [
            weight
            for at, weight in enumerate(owners)
            if at == turn - 1 - 2 * len(steps) and weight not in owners[at + 1 :]
        ]
        for weight in whole:
            mine = placed(idx, weight)
            weight.ready = (mine, swap(mine, 1))
            for sink, owner in zip(sinks, owners, strict=True):
                if owner is weight:
                    sink.clear()
        kept = {step: Box(block) for step, block in blocks.items()}
        sent = {step: Box(block) for step, block in got.items()}
        for at, side, others, step, first in used:
            sinks[at].append((side, others, kept[step], first))
        for at, side, others, step, first in comes:
            sinks[at].append((side, others, sent[step], first))
        late, pieces, now, ready = yield (
            [box.value for box in flying],
            pieces,
            {turn: along[turn]} if turn in along else {},
            [weight.ready for weight in whole],
        )
        for box, value in zip(flying, late, strict=True):
            box.value = value
        flying = list(sent.values())
        along.update(now)
        for weight, pair in zip(whole, ready, strict=True):
            weight.ready = pair


def ring_steps(block, layer):
    peers, length = lax.axis_size("fsdp"), block.shape[0]
    found = [block]
    for _ in range(peers - 1):
        found.append((yield shifted(found[-1], 1)))
    ahead = found[:1] + found[:0:-1]
    twice = jnp.concatenate(ahead + ahead, 0)
    whole = lax.dynamic_slice_in_dim(
        twice, lax.rem(peers - layer, peers) * length, peers * length, 0
    )
    yield Last(whole)


def deal_steps(array, layer):
    peers = lax.axis_size("fsdp")
    width = array.shape[1] // peers

    def cut(hops):
        return lax.dynamic_slice_in_dim(array, lax.rem(layer + hops, peers) * width, width, 1)

    ahead = [cut(0)]
    for hops in range(1, peers):
        ahead.append((yield shifted(cut(peers - hops), peers - hops)))
    twice = jnp.concatenate(ahead + ahead, 0)
    length = array.shape[0]
    yield Last(
        lax.dynamic_slice_in_dim(
            twice, lax.rem(peers - layer, peers) * length, peers * length, 0
        )
    )


def every_steps(block, wait):
    found = lax.all_gather(block, "fsdp", axis=0, tiled=True)
    for _ in range(wait):
        yield ()
    yield Last(found)


def added(left_side, right_side):
    return (left_side.astype(jnp.float32) + right_side.astype(jnp.float32)).astype(jnp.bfloat16)


def weight_steps(act, grad, place, finish):
    steps, core = chip_steps(), jnp.bitwise_and(place, 1) == 1
    while any(task.result is None for task in act + grad):
        yield ()
    part = lax.dot_general(
        act[0].result, grad[0].result, (((0,), (0,)), ((), ())), preferred_element_type=jnp.float32
    ).astype(jnp.bfloat16)
    own, other = halves(core, part, 1)
    own, got = yield own, swap(other, 1)
    own = added(own, got)
    size = own.shape[0] // 2
    blocks = [own[:size], own[size:]]
    orders = [steps[side:] + steps[:side] for side in range(2)]
    for stage in range(len(steps)):
        sent = []
        for side in range(2):
            step = orders[side][stage]
            keep, send = halves(jnp.bitwise_and(place, step) != 0, blocks[side], 0)
            sent.append((keep, swap(send, step)))
        sent = yield sent
        blocks = [added(*pair) for pair in sent]
    for stage in range(len(steps))[::-1]:
        sent = yield [(blocks[side], swap(blocks[side], orders[side][stage])) for side in range(2)]
        blocks = [
            ordered(jnp.bitwise_and(place, orders[side][stage]) != 0, *sent[side], 0)
            for side in range(2)
        ]
    own = jnp.concatenate(blocks, 0)
    pair = yield own, swap(own, 1)
    yield Last(finish(pair))


def finish_kernel(segments, idx_ref, *refs):
    out_ref = refs[-1]
    for flag in (0, 1):

        @pl.when(idx_ref[1] == flag)
        def _():
            at = 0
            for number, first, last in segments:
                pair = refs[2 * number : 2 * number + 2]
                half = pair[0].shape[1]
                for part, begin, end in (
                    (pair[flag], first, min(last, half)),
                    (pair[1 - flag], max(first, half) - half, last - half),
                ):
                    if begin < end:
                        out_ref[:, at : at + end - begin] = part[:, begin:end].astype(jnp.float32)
                        at += end - begin


def finished(idx, pairs, segments, first_row=0, rows=None):
    rows = rows or pairs[0][0].shape[0]
    width = sum(last - first for _, first, last in segments)
    block = 32
    while block < 256 and rows % (2 * block) == 0 and first_row % (2 * block) == 0:
        block *= 2
    while block > 32 and block * width > 1024 * 1024:
        block //= 2
    skip = first_row // block
    flat = [part for pair in pairs for part in pair]
    return pl.pallas_call(
        lambda *refs: finish_kernel(segments, *refs),
        grid=(rows // block,),
        out_shape=jax.ShapeDtypeStruct((rows, width), jnp.float32),
        in_specs=[pl.BlockSpec(memory_space=pltpu.SMEM)]
        + [pl.BlockSpec((block, part.shape[1]), lambda i: (i + skip, 0)) for part in flat],
        out_specs=pl.BlockSpec((block, width), lambda i: (i, 0)),
        compiler_params=pltpu.CompilerParams(vmem_limit_bytes=32 * 1024 * 1024),
        cost_estimate=pl.CostEstimate(
            flops=0, bytes_accessed=6 * rows * width, transcendentals=0
        ),
        name="finish",
    )(idx, *flat)


def finish_steps(tasks, finish):
    while any(task.result is None for task in tasks):
        yield ()
    yield Last(finish(*[task.result for task in tasks]))


def along_ctx(block, place):
    for step in powers(1, lax.axis_size("ctx")):
        block = ordered(jnp.bitwise_and(place, step) != 0, block, swap(block, step), 0)
    return block


def along_ctx_steps(block, place):
    for step in powers(1, lax.axis_size("ctx")):
        got = yield swap(block, step)
        block = ordered(jnp.bitwise_and(place, step) != 0, block, got, 0)
    yield Last(block)


def summed_rows(block, place):
    for step in powers(1, lax.axis_size("ctx"))[::-1]:
        keep, send = halves(jnp.bitwise_and(place, step) != 0, block, 0)
        block = added(keep, swap(send, step))
    return block


def tile_of(width):
    return max(tile for tile in range(128, 1025, 128) if width % tile == 0)


def forth_kernel(idx_ref, left_ref, own_ref, other_ref, out_ref):
    for side, part_ref in enumerate((own_ref, other_ref)):

        @pl.when(pl.program_id(0) == side)
        def _():
            out_ref[...] = jnp.dot(
                left_ref[...], part_ref[...], preferred_element_type=jnp.float32
            ).astype(out_ref.dtype)


def back_kernel(idx_ref, grad_ref, own_ref, other_ref, out_ref):
    @pl.when((pl.program_id(0) == 0) & (pl.program_id(1) == 0))
    def _():
        out_ref[...] = jnp.zeros_like(out_ref)

    for side, part_ref in enumerate((own_ref, other_ref)):

        @pl.when(pl.program_id(0) == side)
        def _():
            out_ref[...] += lax.dot_general(
                grad_ref[...],
                part_ref[...],
                (((1,), (1,)), ((), ())),
                preferred_element_type=jnp.float32,
            )


def product_specs(depth, width):
    tile = tile_of(width)
    count = width // tile
    return (
        tile,
        count,
        pl.BlockSpec((depth, tile), lambda s, t, idx: (0, jnp.where(s == 0, t, count - 1))),
        pl.BlockSpec((depth, tile), lambda s, t, idx: (0, jnp.where(s == 0, 0, t))),
        lambda s, t, idx: (0, jnp.bitwise_xor(idx[1], s) * count + t),
    )


def forth(idx, left_side, chunk, kind=jnp.float32):
    rows, (depth, width) = left_side.shape[0], chunk[0].shape
    tile, count, own_spec, other_spec, place = product_specs(depth, width)
    return pl.pallas_call(
        forth_kernel,
        grid_spec=pltpu.PrefetchScalarGridSpec(
            num_scalar_prefetch=1,
            grid=(2, count),
            in_specs=[pl.BlockSpec((rows, depth), lambda s, t, idx: (0, 0)), own_spec, other_spec],
            out_specs=pl.BlockSpec((rows, tile), place),
        ),
        out_shape=jax.ShapeDtypeStruct((rows, 2 * width), kind),
        compiler_params=pltpu.CompilerParams(vmem_limit_bytes=40 * 1024 * 1024),
        cost_estimate=pl.CostEstimate(
            flops=4 * rows * depth * width, bytes_accessed=4 * depth * width, transcendentals=0
        ),
        name="forth",
    )(idx, left_side, *chunk)


def back(idx, grad_in, chunk):
    rows, (depth, width) = grad_in.shape[0], chunk[0].shape
    tile, count, own_spec, other_spec, place = product_specs(depth, width)
    return pl.pallas_call(
        back_kernel,
        grid_spec=pltpu.PrefetchScalarGridSpec(
            num_scalar_prefetch=1,
            grid=(2, count),
            in_specs=[pl.BlockSpec((rows, tile), place), own_spec, other_spec],
            out_specs=pl.BlockSpec((rows, depth), lambda s, t, idx: (0, 0)),
        ),
        out_shape=jax.ShapeDtypeStruct((rows, depth), jnp.float32),
        compiler_params=pltpu.CompilerParams(vmem_limit_bytes=40 * 1024 * 1024),
        cost_estimate=pl.CostEstimate(
            flops=4 * rows * depth * width, bytes_accessed=4 * depth * width, transcendentals=0
        ),
        name="back",
    )(idx, grad_in, *chunk)


def sum_steps(arrays):
    flat = jnp.concatenate([array.reshape(-1) for array in arrays])
    size = flat.shape[0]
    flat = jnp.pad(flat, (0, -size % 1024)).reshape(-1, 128)
    for axis in ("ctx", "fsdp"):
        peers = lax.axis_size(axis)
        for step in powers(1, peers):
            flat = yield flat + lax.ppermute(flat, axis, [(i, i ^ step) for i in range(peers)])
    flat, found, at = flat.reshape(-1), [], 0
    for array in arrays:
        found.append(flat[at : at + array.size].reshape(array.shape))
        at += array.size
    yield Last(found)


def body(
    tokens,
    cotangent,
    doc_ids,
    in_proj,
    dt_proj,
    conv_weight,
    conv_bias,
    dt_bias,
    a_log,
    d_skip,
    mixer_gain,
    out_proj,
    qkv_proj,
    o_proj,
    first_gain,
    second_gain,
    gate_up,
    down_proj,
):
    my_index, layer = lax.axis_index("ctx"), lax.axis_index("fsdp")
    layers = lax.axis_size("fsdp")
    core, chip = jnp.bitwise_and(my_index, 1), my_index // 2
    idx = jnp.stack([chip, core, layer]).astype(jnp.int32)
    conv_cols, qkv_cols = DS + 2 * NS, (HQ + 2 * HK) * HA
    kv_bc = jnp.concatenate([qkv_proj, in_proj[:, 2 * DS :]], 1)
    z_x = in_proj[:, : 2 * DS]
    out_o = jnp.concatenate([out_proj, o_proj], 0)
    rounds = Rounds()

    def dealt(array):
        return rounds.start(deal_steps(array, layer))

    def every(block, wait):
        return rounds.start(every_steps(block, wait))

    def weight_grad(act, grad, finish):
        return rounds.start(weight_steps(act, grad, my_index, finish))

    part = 2048
    qb_w = Weight(kv_bc, part)
    x_w = Weight(in_proj[:, DS : DS + part], part)
    xz_w = Weight(
        jnp.concatenate([in_proj[:, DS + part : 2 * DS], in_proj[:, : DS - part]], 1), part
    )
    z_w = Weight(in_proj[:, DS - part : DS], part)
    oo_w, down_w = Weight(out_o, D), Weight(down_proj, D)
    gate_w, up_w = Weight(gate_up[:, :FF], FF), Weight(gate_up[:, FF:], FF)
    rows = gate_up.shape[0] // (lax.axis_size("ctx") // 2)
    rounds.start(
        gather_steps(idx, [qb_w, x_w, xz_w, z_w, oo_w, gate_w, up_w, down_w], rows, part // 2)
    )
    dt_task = rounds.start(ring_steps(dt_proj, layer))

    hidden = tokens[0].astype(jnp.float32)
    grad_out = cotangent[0].astype(jnp.float32)
    own_ids = doc_ids[0]
    length = hidden.shape[0]
    all_ids = along_ctx(own_ids.reshape(1, length), my_index).reshape(-1)
    first_row = my_index * length
    places = first_row + jnp.arange(length, dtype=jnp.int32)
    before = first_row - (KC - 1) + jnp.arange(KC - 1, dtype=jnp.int32)
    earlier_ids = lax.dynamic_slice_in_dim(all_ids, jnp.maximum(first_row - (KC - 1), 0), KC - 1, 0)
    earlier_ids = jnp.where(before >= 0, earlier_ids, -1)
    pad_ids = jnp.concatenate([earlier_ids, own_ids], 0)
    prev_id = jnp.where(my_index > 0, all_ids[jnp.maximum(first_row - 1, 0)], -1)
    normed_in, norm_pull = jax.vjp(normed, hidden, first_gain)
    input_low = normed_in.astype(jnp.bfloat16)
    input_low, all_ids, pad_ids, prev_id = rounds.turn((input_low, all_ids, pad_ids, prev_id))
    input_dealt = dealt(input_low)
    rounds.until_ready(qb_w)
    rounds.until(dt_task)

    qb_out = forth(idx, input_low, qb_w.ready)
    attn_in, bc_out = qb_out[:, :qkv_cols], qb_out[:, qkv_cols:]
    step_raw = project(input_low, dt_task.result)
    groups = HQ // HK
    scale = HA ** (-0.5)
    query_low = rotate(attn_in[:, : HQ * HA].reshape(length, HQ, HA), places, 1.0).astype(
        jnp.bfloat16
    )
    key_low = rotate(
        attn_in[:, HQ * HA : (HQ + HK) * HA].reshape(length, HK, HA), places, 1.0
    ).astype(jnp.bfloat16)
    value_low = attn_in[:, (HQ + HK) * HA :].astype(jnp.bfloat16)
    both_low = jnp.concatenate([key_low.reshape(length, HK * HA), value_low], 1)
    query_low, both_low, step_raw, bc_out = rounds.turn((query_low, both_low, step_raw, bc_out))
    both_task = rounds.start(along_ctx_steps(both_low, my_index))
    rounds.until_ready(x_w)
    x_out = forth(idx, input_low, x_w.ready)
    x_out = rounds.turn(x_out)
    rounds.until_ready(xz_w)
    xz_out = forth(idx, input_low, xz_w.ready)
    conv_low = jnp.concatenate([x_out, xz_out[:, : DS - part], bc_out], 1).astype(jnp.bfloat16)
    tail_low = from_behind(conv_low[length - (KC - 1) :], "ctx", 1)
    conv_low, tail_low, xz_out = rounds.turn((conv_low, tail_low, xz_out))

    def front_fn(conv_in, tail_in, shift_in, kernel_in, bias_in, bias_step, log_rate):
        padded = jnp.concatenate([tail_in, conv_in], 0)
        activated = jax.nn.silu(convolve(padded, pad_ids, own_ids, kernel_in, bias_in))
        states_x = activated[:, :DS].reshape(length, NH, HP)
        b_matrix = activated[:, DS : DS + NS]
        c_matrix = activated[:, DS + NS :]
        step_size = jax.nn.softplus(shift_in + bias_step)
        log_decay = -step_size * jnp.exp(log_rate)
        y_part, local_state = ssm_local(states_x, step_size, log_decay, b_matrix, c_matrix, own_ids)
        return (y_part, local_state, states_x, c_matrix, log_decay)

    front_out, front_pull = jax.vjp(
        front_fn,
        conv_low.astype(jnp.float32),
        tail_low.astype(jnp.float32),
        step_raw,
        conv_weight,
        conv_bias,
        dt_bias,
        a_log,
    )
    y_part, local_state, states_x, c_matrix, log_decay = front_out
    decay_now, decay_pull = jax.vjp(lambda log_in: block_decay(log_in, own_ids, prev_id), log_decay)
    y_part, local_state, decay_now = rounds.turn((y_part, local_state, decay_now))
    state_task = rounds.start(entering_steps(decay_now, local_state, my_index, False))
    rounds.until(both_task)
    both_all = both_task.result
    query_groups = query_low.reshape(length, HK, groups, HA)
    seq_len = both_all.shape[0]
    keys_all = both_all[:, : HK * HA].reshape(seq_len, HK, HA)
    values_all = both_all[:, HK * HA :].reshape(seq_len, HK, HA)
    key_places = jnp.arange(seq_len, dtype=jnp.int32)
    allowed = (places[:, None] >= key_places[None, :]) & (own_ids[:, None] == all_ids[None, :])

    score = (
        jnp.einsum("qkgd,rkd->kgqr", query_groups, keys_all, preferred_element_type=jnp.float32)
        * scale
    )
    score = jnp.where(allowed[None, None], score, -1e30)
    new_top = jnp.maximum(-1e30, jnp.max(score, axis=-1))
    soft = jnp.where(allowed[None, None], jnp.exp(score - new_top[..., None]), 0.0)
    total = jnp.sum(soft, axis=-1)
    accum = jnp.einsum(
        "kgqr,rkd->qkgd",
        soft.astype(jnp.bfloat16),
        values_all,
        preferred_element_type=jnp.float32,
    )
    attended = accum / jnp.transpose(total, (2, 0, 1))[..., None]
    log_total = new_top + jnp.log(total)
    attended_low = attended.reshape(length, HQ * HA).astype(jnp.bfloat16)
    attended, log_total, attended_low = rounds.turn((attended, log_total, attended_low))

    rounds.until_ready(z_w)
    gate_z = jnp.concatenate(
        [xz_out[:, DS - part :], forth(idx, input_low, z_w.ready)], 1
    )
    gate_z = rounds.turn(gate_z)
    rounds.until(state_task)
    rounds.until_ready(oo_w)
    state_in = state_task.result
    y_carry, carry_pull = jax.vjp(
        lambda c_in, log_in, state_arg: ssm_carry(c_in, log_in, own_ids, prev_id, state_arg),
        c_matrix,
        log_decay,
        state_in,
    )
    mixer_normed, tail_pull = jax.vjp(
        mixer_tail, y_part + y_carry, states_x, gate_z, d_skip, mixer_gain
    )
    mixer_low = mixer_normed.astype(jnp.bfloat16)

    def interleaved(mixed_in, attended_in):
        return jnp.concatenate(
            [
                mixed_in.reshape(length, layers, DS // layers),
                attended_in.reshape(length, layers, HQ * HA // layers),
            ],
            2,
        ).reshape(length, DS + HQ * HA)

    def parted(both):
        both = both.reshape(length, layers, (DS + HQ * HA) // layers)
        return (
            both[:, :, : DS // layers].reshape(length, DS),
            both[:, :, DS // layers :].reshape(length, HQ * HA),
        )

    branches_low = interleaved(mixer_low, attended_low)
    middle = hidden + forth(idx, branches_low, oo_w.ready)
    normed_mid, mid_pull = jax.vjp(normed, middle, second_gain)
    mid_low = normed_mid.astype(jnp.bfloat16)
    grad_low = grad_out.astype(jnp.bfloat16)
    middle, mid_low, branches_low = rounds.turn((middle, mid_low, branches_low))
    branches_dealt = dealt(branches_low)
    rounds.until_ready(gate_w)
    gate_out = forth(idx, mid_low, gate_w.ready)
    gate_out = rounds.turn(gate_out)
    rounds.until_ready(up_w)
    cotangent_all = every(grad_low, 2)
    mid_dealt = dealt(mid_low)
    up_out = forth(idx, mid_low, up_w.ready)
    act_value, act_pull = jax.vjp(
        lambda gate_in, up_in: jax.nn.silu(gate_in) * up_in, gate_out, up_out
    )
    act_low = act_value.astype(jnp.bfloat16)
    act_low = rounds.turn(act_low)

    rounds.until_ready(down_w)
    act_dealt = dealt(act_low)
    d_act = back(idx, grad_low, down_w.ready)
    d_gate, d_up = act_pull(d_act)
    gate_low, up_low = d_gate.astype(jnp.bfloat16), d_up.astype(jnp.bfloat16)
    gate_low, up_low = rounds.turn((gate_low, up_low))
    rounds.until(cotangent_all)
    gate_all = every(gate_low, 4)
    up_all = every(up_low, 7)
    down_grad = weight_grad(
        [act_dealt], [cotangent_all], lambda pair: finished(idx, [pair], [(0, 0, D)])
    )
    d_mid_norm = back(idx, gate_low, gate_w.ready)
    mixed, d_mid_norm = rounds.turn((middle + forth(idx, act_low, down_w.ready), d_mid_norm))
    d_mid_norm = d_mid_norm + back(idx, up_low, up_w.ready)
    d_middle_part, d_second_gain = mid_pull(d_mid_norm)
    d_middle = grad_out + d_middle_part
    branch_low = d_middle.astype(jnp.bfloat16)
    branch_low, d_middle = rounds.turn((branch_low, d_middle))
    branch_all = every(branch_low, 7)
    d_mixer_norm, d_attended = parted(back(idx, branch_low, oo_w.ready))
    d_core, d_states_tail, d_gate_z, d_d_skip, d_mixer_gain = tail_pull(d_mixer_norm)
    z_low = d_gate_z.astype(jnp.bfloat16)
    z_low, d_attended, d_core = rounds.turn((z_low, d_attended, d_core))
    d_c_carry, d_log_carry, d_state_in = carry_pull(d_core)
    later_task = rounds.start(entering_steps(decay_now, d_state_in, my_index, True))
    d_out_low = d_attended.reshape(length, HK, groups, HA).astype(jnp.bfloat16)
    delta = jnp.transpose(jnp.sum(d_out_low.astype(jnp.float32) * attended, axis=-1), (1, 2, 0))
    score = (
        jnp.einsum("qkgd,rkd->kgqr", query_groups, keys_all, preferred_element_type=jnp.float32)
        * scale
    )
    prob = jnp.where(
        allowed[None, None],
        jnp.exp(jnp.where(allowed[None, None], score, 0.0) - log_total[..., None]),
        0.0,
    )
    d_prob = jnp.einsum(
        "qkgd,rkd->kgqr", d_out_low, values_all, preferred_element_type=jnp.float32
    )
    score_grad = (prob * (d_prob - delta[..., None])).astype(jnp.bfloat16)
    d_query = (
        jnp.einsum("kgqr,rkd->qkgd", score_grad, keys_all, preferred_element_type=jnp.float32)
        * scale
    )
    d_keys = (
        jnp.einsum("kgqr,qkgd->rkd", score_grad, query_groups, preferred_element_type=jnp.float32)
        * scale
    )
    d_values = jnp.einsum(
        "kgqr,qkgd->rkd", prob.astype(jnp.bfloat16), d_out_low, preferred_element_type=jnp.float32
    )
    kv_terms = jnp.concatenate(
        [d_keys.reshape(seq_len, HK * HA), d_values.reshape(seq_len, HK * HA)], 1
    ).astype(jnp.bfloat16)
    kv_terms, d_query = rounds.turn((kv_terms, d_query))
    d_kv = summed_rows(kv_terms, my_index).astype(jnp.float32)
    qkv_low = jnp.concatenate(
        [
            rotate(d_query.reshape(length, HQ, HA), places, -1.0).reshape(length, HQ * HA),
            rotate(d_kv[:, : HK * HA].reshape(length, HK, HA), places, -1.0).reshape(
                length, HK * HA
            ),
            d_kv[:, HK * HA :],
        ],
        1,
    ).astype(jnp.bfloat16)
    qkv_low = rounds.turn(qkv_low)
    zq_all = every(jnp.concatenate([z_low, qkv_low], 1), 5)
    rounds.until(later_task)
    later_grad = later_task.result
    d_decay = jnp.sum(later_grad * state_in, axis=(1, 2))
    d_log_decay = decay_pull(d_decay)[0]
    d_conv_in, d_tail, d_step_raw, d_conv_weight, d_conv_bias, d_dt_bias, d_a_log = front_pull(
        (d_core, later_grad, d_states_tail, d_c_carry, d_log_carry + d_log_decay)
    )
    d_conv_in, d_tail, d_step_raw = rounds.turn((d_conv_in, d_tail, d_step_raw))
    from_next = from_behind(d_tail.astype(jnp.bfloat16), "ctx", -1).astype(d_tail.dtype)
    d_conv_in = jnp.concatenate(
        [d_conv_in[: length - (KC - 1)], d_conv_in[length - (KC - 1) :] + from_next], 0
    )
    conv_grad_low = d_conv_in.astype(jnp.bfloat16)
    step_low = d_step_raw.astype(jnp.bfloat16)
    blank = jnp.zeros((length, 512 - NH), jnp.bfloat16)
    conv_grad_low, step_low = rounds.turn((conv_grad_low, step_low))
    tail_all = every(jnp.concatenate([conv_grad_low, step_low, blank[:, : 256 - NH]], 1), 5)
    pending = {
        "gate": (mid_dealt, gate_all, lambda pair: pair),
        "up": (mid_dealt, up_all, lambda pair: pair),
        "oo": (
            branches_dealt,
            branch_all,
            lambda pair: (
                finished(idx, [pair], [(0, 0, D)], 0, DS // layers),
                finished(idx, [pair], [(0, 0, D)], DS // layers, HQ * HA // layers),
            ),
        ),
        "zq": (input_dealt, zq_all, lambda pair: pair),
        "tail": (input_dealt, tail_all, lambda pair: pair),
    }
    grads = {
        name: weight_grad([act], [grad], finish) for name, (act, grad, finish) in pending.items()
    }
    gate_up_grad = rounds.start(
        finish_steps(
            [grads["gate"], grads["up"]],
            lambda *pairs: finished(idx, pairs, [(0, 0, FF), (1, 0, FF)]),
        )
    )
    d_normed_in = (
        back(idx, conv_grad_low[:, :part], x_w.ready)
        + back(
            idx,
            jnp.concatenate([conv_grad_low[:, part:DS], z_low[:, : DS - part]], 1),
            xz_w.ready,
        )
    )
    d_normed_in = rounds.turn(d_normed_in)
    d_normed_in = (
        d_normed_in
        + back(idx, z_low[:, DS - part :], z_w.ready)
        + back(idx, jnp.concatenate([qkv_low, conv_grad_low[:, DS:]], 1), qb_w.ready)
        + project_back(step_low, dt_task.result)
    )
    d_hidden_part, d_first_gain = norm_pull(d_normed_in)
    d_tokens = d_middle + d_hidden_part
    d_tokens, d_first_gain = rounds.turn((d_tokens, d_first_gain))
    smalls_task = rounds.start(
        sum_steps(
            (
                d_conv_weight,
                d_conv_bias,
                d_dt_bias,
                d_a_log,
                d_d_skip,
                d_mixer_gain,
                d_first_gain,
                d_second_gain,
            )
        )
    )
    rounds.until(smalls_task, gate_up_grad, down_grad, *grads.values())
    smalls = smalls_task.result
    tail_pair, zq_pair = grads["tail"].result, grads["zq"].result
    tail_half = tail_pair[0].shape[1]
    step_grad = jnp.where(core == 1, tail_pair[0], tail_pair[1])
    return (
        mixed[None].astype(jnp.bfloat16),
        d_tokens[None],
        finished(idx, [zq_pair, tail_pair], [(0, 0, DS), (1, 0, conv_cols)]),
        step_grad[:, conv_cols - tail_half : conv_cols - tail_half + NH].astype(jnp.float32),
        smalls[0],
        smalls[1],
        smalls[2],
        smalls[3],
        smalls[4],
        smalls[5],
        grads["oo"].result[0],
        finished(idx, [zq_pair], [(0, DS, DS + qkv_cols)]),
        grads["oo"].result[1],
        smalls[6],
        smalls[7],
        gate_up_grad.result,
        down_grad.result,
    )


def solution(mesh):
    return jax.shard_map(
        body,
        mesh=mesh,
        in_specs=(
            P("fsdp", "ctx", None),
            P("fsdp", "ctx", None),
            P("fsdp", "ctx"),
            P("fsdp", None),
            P("fsdp", None),
            P(),
            P(),
            P(),
            P(),
            P(),
            P(),
            P("fsdp", None),
            P("fsdp", None),
            P("fsdp", None),
            P(),
            P(),
            P("fsdp", None),
            P("fsdp", None),
        ),
        out_specs=(
            P("fsdp", "ctx", None),
            P("fsdp", "ctx", None),
            P("fsdp", None),
            P("fsdp", None),
            P(),
            P(),
            P(),
            P(),
            P(),
            P(),
            P("fsdp", None),
            P("fsdp", None),
            P("fsdp", None),
            P(),
            P(),
            P("fsdp", None),
            P("fsdp", None),
        ),
        check_vma=False,
    )
```

```python
import jax
import jax.numpy as jnp
from jax import lax
from jax.experimental import pallas as pl
from jax.experimental.pallas import tpu as pltpu
from jax.sharding import PartitionSpec as P

D = 2048
FF = 4096
NH = 48
HP = 64
NS = 256
KC = 4
HQ = 8
HK = 2
HA = 128
DS = 3072


HIGH = lax.Precision.HIGHEST
epsilon = 1e-05
rope_base = 100000000000.0


def from_behind(block, axis, distance):
    devices = range(lax.axis_size(axis))
    route = [(i - distance, i) for i in devices if i - distance in devices]
    return lax.ppermute(block, axis, route)


def normed(operand, gain_vec):
    return (
        operand
        * lax.rsqrt(jnp.mean(operand * operand, axis=-1, keepdims=True) + epsilon)
        * gain_vec
    )


def rotate(operand, places, direction):
    half_width = operand.shape[-1] // 2
    frequency = rope_base ** (
        -jnp.arange(half_width, dtype=jnp.float32) * (2.0 / operand.shape[-1])
    )
    angles = places.astype(jnp.float32)[:, None] * frequency[None, :]
    cosine = jnp.cos(angles)[:, None, :]
    sine_part = direction * jnp.sin(angles)[:, None, :]
    first_half = operand[..., :half_width]
    second_half = operand[..., half_width:]
    return jnp.concatenate(
        [
            first_half * cosine - second_half * sine_part,
            second_half * cosine + first_half * sine_part,
        ],
        -1,
    )


def project(left_side, right_side):
    return jnp.dot(left_side, right_side, preferred_element_type=jnp.float32)


def project_back(grad_in, weight):
    return lax.dot_general(
        grad_in, weight, (((1,), (1,)), ((), ())), preferred_element_type=jnp.float32
    )


def convolve(padded, pad_ids, row_ids, kernel_in, bias_in):
    length = row_ids.shape[0]
    total = jnp.zeros((length, padded.shape[1]), jnp.float32) + bias_in[None, :]
    for offset in range(KC):
        same_doc = (pad_ids[offset : offset + length] == row_ids).astype(jnp.float32)
        total = (
            total
            + kernel_in[offset][None, :] * padded[offset : offset + length] * same_doc[:, None]
        )
    return total


def ssm_local(states_x, step_size, log_decay, b_matrix, c_matrix, row_ids):
    length = states_x.shape[0]
    running = jnp.cumsum(log_decay, axis=0)
    places = jnp.arange(length, dtype=jnp.int32)
    allowed = (places[:, None] >= places[None, :]) & (row_ids[:, None] == row_ids[None, :])
    spread = running.T[:, :, None] - running.T[:, None, :]
    decay_matrix = jnp.where(allowed[None], jnp.exp(jnp.where(allowed[None], spread, 0.0)), 0.0)
    intersection = jnp.dot(c_matrix, b_matrix.T, precision=HIGH, preferred_element_type=jnp.float32)
    driven = step_size[:, :, None] * states_x
    y_part = jnp.einsum("hts,shp->thp", decay_matrix * intersection[None], driven, precision=HIGH)
    to_end = jnp.where(
        (row_ids == row_ids[-1])[:, None], jnp.exp(running[-1][None, :] - running), 0.0
    )
    local_state = jnp.einsum("sh,shp,sn->hpn", to_end, driven, b_matrix, precision=HIGH)
    return (y_part, local_state)


def ssm_carry(c_matrix, log_decay, row_ids, prev_id, state_in):
    kept_mask = (row_ids == prev_id).astype(jnp.float32)
    weight = jnp.exp(jnp.cumsum(log_decay, axis=0)) * kept_mask[:, None]
    return weight[:, :, None] * jnp.einsum("hpn,tn->thp", state_in, c_matrix, precision=HIGH)


def block_decay(log_decay, row_ids, prev_id):
    return jnp.exp(jnp.sum(log_decay, axis=0)) * (row_ids[-1] == prev_id).astype(jnp.float32)


def mixer_tail(core_in, states_x, gate_z, skip_in, gain_in):
    length = core_in.shape[0]
    core = core_in + skip_in[None, :, None] * states_x
    gated = core.reshape(length, DS) * jax.nn.silu(gate_z)
    return normed(gated, gain_in)


def swiglu(gate_up_out):
    return jax.nn.silu(gate_up_out[:, :FF]) * gate_up_out[:, FF:]


def swap(block, distance):
    peers = lax.axis_size("ctx")
    return lax.ppermute(block, "ctx", [(i, i ^ distance) for i in range(peers)])


def shifted(block, hops):
    peers = lax.axis_size("fsdp")
    return lax.ppermute(block, "fsdp", [(i, (i + hops) % peers) for i in range(peers)])


def powers(first, limit):
    found = []
    while first < limit:
        found.append(first)
        first *= 2
    return found


def chip_steps():
    return powers(2, lax.axis_size("ctx"))


def ordered(flag, first, second, axis):
    return jnp.where(
        flag,
        jnp.concatenate([second, first], axis),
        jnp.concatenate([first, second], axis),
    )


def halves(flag, array, axis):
    size = array.shape[axis] // 2
    low = lax.slice_in_dim(array, 0, size, axis=axis)
    high = lax.slice_in_dim(array, size, 2 * size, axis=axis)
    return (jnp.where(flag, high, low), jnp.where(flag, low, high))


def join(earlier, later):
    return (earlier[0] * later[0], later[0][:, None, None] * earlier[1] + later[1])


def either(flag, when, otherwise):
    return jax.tree.map(lambda a, b: jnp.where(flag, a, b), when, otherwise)


class Last:
    def __init__(self, value):
        self.value = value


class Task:
    def __init__(self, steps):
        self.steps, self.ready, self.result = steps, None, None


class Rounds:
    def __init__(self):
        self.tasks = []

    def start(self, steps):
        self.tasks.append(Task(steps))
        return self.tasks[-1]

    def turn(self, values=()):
        found = []
        for task in self.tasks:
            try:
                found.append(task.steps.send(task.ready))
            except StopIteration:
                found.append(Last(()))
        held = [step.value if isinstance(step, Last) else step for step in found]
        values, held = lax.optimization_barrier((values, held))
        going = []
        for task, step, ready in zip(self.tasks, found, held, strict=True):
            task.ready = ready
            if isinstance(step, Last):
                task.result = ready
            else:
                going.append(task)
        self.tasks = going
        return values

    def until(self, *tasks):
        while any(task.result is None for task in tasks):
            self.turn()

    def until_ready(self, *weights):
        while any(weight.ready is None for weight in weights):
            self.turn()


def entering_steps(decay, state, place, backwards):
    def sent(pair, step):
        return (swap(pair[0], step), swap(pair[1].astype(jnp.bfloat16), step))

    def read(pair):
        return (pair[0], pair[1].astype(jnp.float32))

    def is_later(step):
        return (jnp.bitwise_and(place, step) != 0) != backwards

    core = jnp.bitwise_and(place, 1) == 1
    near = read(sent((decay, state), 1))
    total = either(is_later(1), join(near, (decay, state)), join((decay, state), near))
    total = tuple(halves(core, part, 0)[0] for part in total)
    before = (jnp.ones_like(total[0]), jnp.zeros_like(total[1]))
    steps = chip_steps()
    for step in steps:
        there = read(sent(total, step))
        before = either(is_later(step), join(there, before), before)
        if step != steps[-1]:
            total = either(is_later(step), join(there, total), join(total, there))
            total, before, near = yield total, before, near
    across = swap(before[1].astype(jnp.bfloat16), 1).astype(jnp.float32)
    whole = ordered(core, before[1], across, 0)
    yield Last(jnp.where(is_later(1), near[0][:, None, None] * whole + near[1], whole))


class Weight:
    def __init__(self, shard, width):
        self.shard, self.width, self.chunks, self.ready = shard, width, [], None

    def cuts(self, idx, rows, columns):
        chip, core = idx[0], idx[1]
        per = rows * (lax.axis_size("ctx") // 2)
        for first_row in range(0, self.shard.shape[0], per):
            for first_col in range(0, self.width // 2, columns):
                piece = lax.dynamic_slice(
                    self.shard,
                    (first_row + chip * rows, first_col + core * (self.width // 2)),
                    (rows, columns),
                )
                self.chunks.append((first_row, first_col, []))
                yield piece, self.chunks[-1][2]


class Box:
    def __init__(self, value):
        self.value = value


def copy_all(copies):
    for copy in copies:
        copy.start()
    for copy in copies:
        copy.wait()


def place_kernel(chunks, idx_ref, shard_ref, *refs):
    whole_ref, sems = refs[-2], refs[-1]
    chip, core, layer = idx_ref[0], idx_ref[1], idx_ref[2]
    depth, width = shard_ref.shape[0], whole_ref.shape[1]
    layers = whole_ref.shape[0] // depth
    copies = [
        pltpu.make_async_copy(
            shard_ref.at[:, pl.ds(pl.multiple_of(core * width, 128), width)],
            whole_ref.at[pl.ds(pl.multiple_of(layer * depth, depth), depth), :],
            sems.at[0],
        )
    ]
    for first_row, first_col, found in chunks:
        for side, others, source, first in found:
            rows, columns = refs[source].shape[1:]
            for number, other in enumerate(others):
                for hop in range(layers - 1):
                    owner = lax.rem(layer + 1 + hop, layers)
                    begin = owner * depth + first_row + jnp.bitwise_xor(chip, other) * rows
                    copies.append(
                        pltpu.make_async_copy(
                            refs[source].at[first + number * (layers - 1) + hop],
                            whole_ref.at[
                                pl.ds(pl.multiple_of(begin, rows), rows),
                                pl.ds(first_col + side * columns, columns),
                            ],
                            sems.at[len(copies)],
                        )
                    )
    copy_all(copies)


def placed(idx, weight):
    layers = lax.axis_size("fsdp")
    depth, width = weight.shard.shape[0], weight.width // 2
    boxes = list({id(box): box for _, _, found in weight.chunks for _, _, box, _ in found}.values())
    chunks = [
        (
            first_row,
            first_col,
            [(side, others, boxes.index(box), first) for side, others, box, first in found],
        )
        for first_row, first_col, found in weight.chunks
    ]
    count = 1 + sum(
        (layers - 1) * len(others) for _, _, found in chunks for _, others, _, _ in found
    )
    return pl.pallas_call(
        lambda *refs: place_kernel(chunks, *refs),
        out_shape=jax.ShapeDtypeStruct((layers * depth, width), weight.shard.dtype),
        in_specs=[pl.BlockSpec(memory_space=pltpu.SMEM)]
        + [pl.BlockSpec(memory_space=pl.ANY)] * (1 + len(boxes)),
        out_specs=pl.BlockSpec(memory_space=pltpu.VMEM),
        scratch_shapes=[pltpu.SemaphoreType.DMA((count,))],
        compiler_params=pltpu.CompilerParams(vmem_limit_bytes=56 * 1024 * 1024),
        cost_estimate=pl.CostEstimate(flops=1024, bytes_accessed=1024, transcendentals=0),
        name="place",
    )(idx, weight.shard, *[box.value for box in boxes])


def pack_kernel(fresh, plan, inputs, idx_ref, *refs):
    layer = idx_ref[2]
    outs, sems = refs[inputs:-1], refs[-1]
    copies = []
    for out, first, side in fresh:
        layers, columns = refs[0].shape[0], outs[out].shape[2]
        for hop in range(layers - 1):
            owner = lax.rem(layer + 1 + hop, layers)
            copies.append(
                pltpu.make_async_copy(
                    refs[0].at[owner, :, pl.ds(side * columns, columns)],
                    outs[out].at[first + hop],
                    sems.at[len(copies)],
                )
            )
    for out, first, source, begin, size in plan:
        copies.append(
            pltpu.make_async_copy(
                refs[source].at[pl.ds(begin, size)],
                outs[out].at[pl.ds(first, size)],
                sems.at[len(copies)],
            )
        )
    copy_all(copies)


def packed(idx, along, fresh, plan, sizes, rows, columns):
    boxes = list({id(entry[2]): entry[2] for entry in plan}.values())
    arrays = ([] if along is None else [along]) + [box.value for box in boxes]
    skip = len(arrays) - len(boxes)
    plan = [(out, row, skip + boxes.index(box), begin, size) for out, row, box, begin, size in plan]
    count = len(fresh) * (lax.axis_size("fsdp") - 1) + len(plan)
    return pl.pallas_call(
        lambda *refs: pack_kernel(fresh, plan, len(arrays), *refs),
        out_shape=[jax.ShapeDtypeStruct((size, rows, columns), jnp.bfloat16) for size in sizes],
        in_specs=[pl.BlockSpec(memory_space=pltpu.SMEM)]
        + [pl.BlockSpec(memory_space=pl.ANY)] * len(arrays),
        out_specs=[pl.BlockSpec(memory_space=pltpu.VMEM)] * len(sizes),
        scratch_shapes=[pltpu.SemaphoreType.DMA((count,))],
        compiler_params=pltpu.CompilerParams(vmem_limit_bytes=56 * 1024 * 1024),
        cost_estimate=pl.CostEstimate(flops=1024, bytes_accessed=1024, transcendentals=0),
        name="pack",
    )(idx, *arrays)


def whole_steps(piece, turns, wait):
    for _ in range(turns):
        piece = yield piece
    whole = lax.all_gather(piece, ("fsdp", "ctx"), axis=0, tiled=True)
    for _ in range(wait):
        yield ()
    yield Last(whole)


def gather_steps(idx, weights, rows, columns):
    steps, layers = chip_steps(), lax.axis_size("fsdp")
    half, near = columns // 2, layers - 1
    pieces, sinks, owners = [], [], []
    for weight in weights:
        for piece, sink in weight.cuts(idx, rows, columns):
            pieces.append(piece)
            sinks.append(sink)
            owners.append(weight)
    along, halved = {}, []
    for turn in range(len(pieces) + len(steps) + 3):
        if turn < len(pieces):
            along[turn] = lax.all_gather(pieces[turn], "fsdp")
        fresh, plan, sizes, comes = [], [], {step: 0 for step in steps}, []
        used = []
        for stage in range(len(steps)):
            at = turn - 1 - stage
            if not 0 <= at < len(pieces):
                continue
            for side in range(2):
                step = (steps[side:] + steps[:side])[stage]
                out = steps.index(step)
                first = sizes[step]
                reached = []
                if stage == 0:
                    fresh.append((out, first, side))
                    used.append((at, side, [0], step, first))
                    reached, sizes[step] = [0], first + near
                for _, others, box, begin in [e for e in sinks[at] if e[0] == side]:
                    plan.append((out, sizes[step], box, begin, near * len(others)))
                    sizes[step] += near * len(others)
                    reached = reached + others
                comes.append((at, side, [other ^ (step // 2) for other in reached], step, first))
        active = [step for step in steps if sizes[step]]
        blocks = {}
        if active:
            rank = {steps.index(step): number for number, step in enumerate(active)}
            made = packed(
                idx,
                along.pop(turn - 1, None) if fresh else None,
                [(rank[out], first, side) for out, first, side in fresh],
                [(rank[out], *rest) for out, *rest in plan],
                [sizes[step] for step in active],
                rows,
                half,
            )
            blocks = dict(zip(active, made, strict=True))
        blocks, pieces = lax.optimization_barrier((blocks, pieces))
        got = {step: swap(block, step) for step, block in blocks.items()}
        whole = [
            weight
            for at, weight in enumerate(owners)
            if at == turn - 1 - len(steps) and weight not in owners[at + 1 :]
        ]
        ready = [(weight, mine, swap(mine, 1)) for weight, mine in halved]
        halved = [(weight, placed(idx, weight)) for weight in whole]
        for weight in whole:
            for sink, owner in zip(sinks, owners, strict=True):
                if owner is weight:
                    sink.clear()
        kept = {step: Box(block) for step, block in blocks.items()}
        sent = {step: Box(block) for step, block in got.items()}
        flying = list(sent.values())
        for at, side, others, step, first in used:
            sinks[at].append((side, others, kept[step], first))
        for at, side, others, step, first in comes:
            sinks[at].append((side, others, sent[step], first))
        now_ready = [weight for weight, _, _ in ready]
        for weight, mine, other in ready:
            weight.ready = (mine, other)
        late, pieces, now, ready, mines = yield (
            [box.value for box in flying],
            pieces,
            {turn: along[turn]} if turn in along else {},
            [(mine, other) for _, mine, other in ready],
            [mine for _, mine in halved],
        )
        for box, value in zip(flying, late, strict=True):
            box.value = value
        along.update(now)
        for weight, pair in zip(now_ready, ready, strict=True):
            weight.ready = pair
        halved = [(weight, mine) for (weight, _), mine in zip(halved, mines, strict=True)]


def ring_steps(block, layer):
    peers, length = lax.axis_size("fsdp"), block.shape[0]
    found = [block]
    for _ in range(peers - 1):
        found.append((yield shifted(found[-1], 1)))
    ahead = found[:1] + found[:0:-1]
    twice = jnp.concatenate(ahead + ahead, 0)
    whole = lax.dynamic_slice_in_dim(
        twice, lax.rem(peers - layer, peers) * length, peers * length, 0
    )
    yield Last(whole)


def deal_steps(arrays, layer):
    peers = lax.axis_size("fsdp")
    widths = [array.shape[1] // peers for array in arrays]

    def cut(hops):
        to = lax.rem(layer + hops, peers)
        return jnp.concatenate(
            [
                lax.dynamic_slice_in_dim(array, to * width, width, 1)
                for array, width in zip(arrays, widths, strict=True)
            ],
            1,
        )

    ahead = [cut(0)]
    for hops in range(1, peers):
        ahead.append((yield shifted(cut(peers - hops), peers - hops)))
    whole = jnp.concatenate(
        [lax.select_n(lax.rem(at + peers - layer, peers), *ahead) for at in range(peers)], 0
    )
    found, at = [], 0
    for width in widths:
        found.append(whole[:, at : at + width])
        at += width
    yield Last(found)


def every_steps(block, wait):
    found = lax.all_gather(block, "fsdp", axis=0, tiled=True)
    for _ in range(wait):
        yield ()
    yield Last(found)


def added(left_side, right_side):
    return (left_side.astype(jnp.float32) + right_side.astype(jnp.float32)).astype(jnp.bfloat16)


def weight_steps(products, place, finish, after):
    steps, core = chip_steps(), jnp.bitwise_and(place, 1) == 1
    while any(task.result is None for act, _, grad in products for task in (act, grad)) or any(
        task.result is None for task in after
    ):
        yield ()
    rows = min(act.result[which].shape[1] for act, which, _ in products)
    parts = []
    for act, which, grad in products:
        array = act.result[which]
        for first in range(0, array.shape[1], rows):
            parts.append(
                lax.dot_general(
                    array[:, first : first + rows],
                    grad.result,
                    (((0,), (0,)), ((), ())),
                    preferred_element_type=jnp.float32,
                ).astype(jnp.bfloat16)
            )
    part = jnp.concatenate(parts, 1) if len(parts) > 1 else parts[0]
    own, other = halves(core, part, 1)
    own, got = yield own, swap(other, 1)
    own = added(own, got)
    size = own.shape[0] // 2
    blocks = [own[:size], own[size:]]
    orders = [steps[side:] + steps[:side] for side in range(2)]
    for stage in range(len(steps)):
        sent = []
        for side in range(2):
            step = orders[side][stage]
            keep, send = halves(jnp.bitwise_and(place, step) != 0, blocks[side], 0)
            sent.append((keep, swap(send, step)))
        sent = yield sent
        blocks = [added(*pair) for pair in sent]
    for stage in range(len(steps))[::-1]:
        sent = yield [(blocks[side], swap(blocks[side], orders[side][stage])) for side in range(2)]
        blocks = [
            ordered(jnp.bitwise_and(place, orders[side][stage]) != 0, *sent[side], 0)
            for side in range(2)
        ]
    own = jnp.concatenate(blocks, 0)
    pair = yield own, swap(own, 1)
    yield Last(finish(pair))


def finish_kernel(segments, idx_ref, *refs):
    out_ref = refs[-1]
    for flag in (0, 1):

        @pl.when(idx_ref[1] == flag)
        def _():
            at = 0
            for number, first, last in segments:
                pair = refs[2 * number : 2 * number + 2]
                half = pair[0].shape[1]
                for part, begin, end in (
                    (pair[flag], first, min(last, half)),
                    (pair[1 - flag], max(first, half) - half, last - half),
                ):
                    if begin < end:
                        out_ref[:, at : at + end - begin] = part[:, begin:end].astype(jnp.float32)
                        at += end - begin


def finished(idx, pairs, segments, first_row=0, rows=None):
    rows = rows or pairs[0][0].shape[0]
    width = sum(last - first for _, first, last in segments)
    block = 32
    while block < 256 and rows % (2 * block) == 0 and first_row % (2 * block) == 0:
        block *= 2
    while block > 32 and block * width > 1024 * 1024:
        block //= 2
    skip = first_row // block
    flat = [part for pair in pairs for part in pair]
    return pl.pallas_call(
        lambda *refs: finish_kernel(segments, *refs),
        grid=(rows // block,),
        out_shape=jax.ShapeDtypeStruct((rows, width), jnp.float32),
        in_specs=[pl.BlockSpec(memory_space=pltpu.SMEM)]
        + [pl.BlockSpec((block, part.shape[1]), lambda i: (i + skip, 0)) for part in flat],
        out_specs=pl.BlockSpec((block, width), lambda i: (i, 0)),
        compiler_params=pltpu.CompilerParams(vmem_limit_bytes=56 * 1024 * 1024),
        cost_estimate=pl.CostEstimate(flops=1024, bytes_accessed=1024, transcendentals=0),
        name="finish",
    )(idx, *flat)


def finish_steps(tasks, finish):
    while any(task.result is None for task in tasks):
        yield ()
    yield Last(finish(*[task.result for task in tasks]))


def along_ctx(block, place):
    for step in powers(1, lax.axis_size("ctx")):
        block = ordered(jnp.bitwise_and(place, step) != 0, block, swap(block, step), 0)
    return block


def along_ctx_steps(block, place):
    for step in powers(1, lax.axis_size("ctx")):
        got = yield swap(block, step)
        block = ordered(jnp.bitwise_and(place, step) != 0, block, got, 0)
    yield Last(block)


def sum_rows_steps(block, place):
    for step in powers(1, lax.axis_size("ctx"))[::-1]:
        keep, send = halves(jnp.bitwise_and(place, step) != 0, block, 0)
        got, keep = yield swap(send, step), keep
        block = added(keep, got)
    yield Last(block)


def summed_rows(block, place):
    for step in powers(1, lax.axis_size("ctx"))[::-1]:
        keep, send = halves(jnp.bitwise_and(place, step) != 0, block, 0)
        block = added(keep, swap(send, step))
    return block


def tile_of(width):
    return max(tile for tile in range(128, 1025, 128) if width % tile == 0)


def forth_kernel(idx_ref, left_ref, own_ref, other_ref, out_ref):
    for side, part_ref in enumerate((own_ref, other_ref)):

        @pl.when(pl.program_id(0) == side)
        def _():
            out_ref[...] = jnp.dot(
                left_ref[...], part_ref[...], preferred_element_type=jnp.float32
            ).astype(out_ref.dtype)


def back_kernel(idx_ref, grad_ref, own_ref, other_ref, out_ref):
    @pl.when((pl.program_id(0) == 0) & (pl.program_id(1) == 0))
    def _():
        out_ref[...] = jnp.zeros_like(out_ref)

    for side, part_ref in enumerate((own_ref, other_ref)):

        @pl.when(pl.program_id(0) == side)
        def _():
            out_ref[...] += lax.dot_general(
                grad_ref[...],
                part_ref[...],
                (((1,), (1,)), ((), ())),
                preferred_element_type=jnp.float32,
            )


def product_specs(depth, width):
    tile = tile_of(width)
    count = width // tile
    return (
        tile,
        count,
        pl.BlockSpec((depth, tile), lambda s, t, idx: (0, jnp.where(s == 0, t, count - 1))),
        pl.BlockSpec((depth, tile), lambda s, t, idx: (0, jnp.where(s == 0, 0, t))),
        lambda s, t, idx: (0, jnp.bitwise_xor(idx[1], s) * count + t),
    )


def forth(idx, left_side, chunk, kind=jnp.float32):
    rows, (depth, width) = left_side.shape[0], chunk[0].shape
    tile, count, own_spec, other_spec, place = product_specs(depth, width)
    return pl.pallas_call(
        forth_kernel,
        grid_spec=pltpu.PrefetchScalarGridSpec(
            num_scalar_prefetch=1,
            grid=(2, count),
            in_specs=[pl.BlockSpec((rows, depth), lambda s, t, idx: (0, 0)), own_spec, other_spec],
            out_specs=pl.BlockSpec((rows, tile), place),
        ),
        out_shape=jax.ShapeDtypeStruct((rows, 2 * width), kind),
        compiler_params=pltpu.CompilerParams(vmem_limit_bytes=56 * 1024 * 1024),
        cost_estimate=pl.CostEstimate(flops=1024, bytes_accessed=1024, transcendentals=0),
        name="forth",
    )(idx, left_side, *chunk)


def back(idx, grad_in, chunk):
    rows, (depth, width) = grad_in.shape[0], chunk[0].shape
    tile, count, own_spec, other_spec, place = product_specs(depth, width)
    return pl.pallas_call(
        back_kernel,
        grid_spec=pltpu.PrefetchScalarGridSpec(
            num_scalar_prefetch=1,
            grid=(2, count),
            in_specs=[pl.BlockSpec((rows, tile), place), own_spec, other_spec],
            out_specs=pl.BlockSpec((rows, depth), lambda s, t, idx: (0, 0)),
        ),
        out_shape=jax.ShapeDtypeStruct((rows, depth), jnp.float32),
        compiler_params=pltpu.CompilerParams(vmem_limit_bytes=56 * 1024 * 1024),
        cost_estimate=pl.CostEstimate(flops=1024, bytes_accessed=1024, transcendentals=0),
        name="back",
    )(idx, grad_in, *chunk)


def sum_steps(arrays):
    flat = jnp.concatenate([array.reshape(-1) for array in arrays])
    size = flat.shape[0]
    flat = jnp.pad(flat, (0, -size % 1024)).reshape(-1, 128)
    for axis in ("ctx", "fsdp"):
        peers = lax.axis_size(axis)
        for step in powers(1, peers):
            flat = yield flat + lax.ppermute(flat, axis, [(i, i ^ step) for i in range(peers)])
    flat, found, at = flat.reshape(-1), [], 0
    for array in arrays:
        found.append(flat[at : at + array.size].reshape(array.shape))
        at += array.size
    yield Last(found)


def body(
    tokens,
    cotangent,
    doc_ids,
    in_proj,
    dt_proj,
    conv_weight,
    conv_bias,
    dt_bias,
    a_log,
    d_skip,
    mixer_gain,
    out_proj,
    qkv_proj,
    o_proj,
    first_gain,
    second_gain,
    gate_up,
    down_proj,
):
    my_index, layer = lax.axis_index("ctx"), lax.axis_index("fsdp")
    layers = lax.axis_size("fsdp")
    core, chip = jnp.bitwise_and(my_index, 1), my_index // 2
    idx = jnp.stack([chip, core, layer]).astype(jnp.int32)
    conv_cols, qkv_cols = DS + 2 * NS, (HQ + 2 * HK) * HA
    kv_bc = jnp.concatenate([qkv_proj, in_proj[:, 2 * DS :]], 1)
    z_x = in_proj[:, : 2 * DS]
    out_o = jnp.concatenate([out_proj, o_proj], 0)
    rounds = Rounds()

    def dealt(*arrays):
        return rounds.start(deal_steps(arrays, layer))

    def every(block, wait):
        return rounds.start(every_steps(block, wait))

    def weight_grad(products, finish, *after):
        return rounds.start(weight_steps(products, my_index, finish, list(after)))

    part = 2048
    qb_w = Weight(kv_bc, part)
    x_w = Weight(in_proj[:, DS : DS + part], part)
    xz_w = Weight(
        jnp.concatenate([in_proj[:, DS + part : 2 * DS], in_proj[:, : DS - part]], 1), part
    )
    z_w = Weight(in_proj[:, DS - part : DS], part)
    oo_w, down_w = Weight(out_o, D), Weight(down_proj, D)
    gate_w, up_w = Weight(gate_up[:, :FF], FF), Weight(gate_up[:, FF:], FF)
    rows = gate_up.shape[0] // (lax.axis_size("ctx") // 2)
    rounds.start(
        gather_steps(idx, [qb_w, x_w, xz_w, z_w, oo_w, gate_w, up_w, down_w], rows, part // 2)
    )
    dt_task = rounds.start(ring_steps(dt_proj, layer))

    hidden = tokens[0].astype(jnp.float32)
    grad_out = cotangent[0].astype(jnp.float32)
    own_ids = doc_ids[0]
    length = hidden.shape[0]
    all_ids = along_ctx(own_ids.reshape(1, length), my_index).reshape(-1)
    first_row = my_index * length
    places = first_row + jnp.arange(length, dtype=jnp.int32)
    before = first_row - (KC - 1) + jnp.arange(KC - 1, dtype=jnp.int32)
    earlier_ids = lax.dynamic_slice_in_dim(all_ids, jnp.maximum(first_row - (KC - 1), 0), KC - 1, 0)
    earlier_ids = jnp.where(before >= 0, earlier_ids, -1)
    pad_ids = jnp.concatenate([earlier_ids, own_ids], 0)
    prev_id = jnp.where(my_index > 0, all_ids[jnp.maximum(first_row - 1, 0)], -1)
    normed_in, norm_pull = jax.vjp(normed, hidden, first_gain)
    input_low = normed_in.astype(jnp.bfloat16)
    input_low, all_ids, pad_ids, prev_id = rounds.turn((input_low, all_ids, pad_ids, prev_id))
    rounds.until_ready(qb_w)
    rounds.until(dt_task)

    qb_out = forth(idx, input_low, qb_w.ready)
    attn_in, bc_out = qb_out[:, :qkv_cols], qb_out[:, qkv_cols:]
    step_raw = project(input_low, dt_task.result)
    groups = HQ // HK
    scale = HA ** (-0.5)
    query_low = rotate(attn_in[:, : HQ * HA].reshape(length, HQ, HA), places, 1.0).astype(
        jnp.bfloat16
    )
    key_low = rotate(
        attn_in[:, HQ * HA : (HQ + HK) * HA].reshape(length, HK, HA), places, 1.0
    ).astype(jnp.bfloat16)
    value_low = attn_in[:, (HQ + HK) * HA :].astype(jnp.bfloat16)
    both_low = jnp.concatenate([key_low.reshape(length, HK * HA), value_low], 1)
    query_low, both_low, step_raw, bc_out = rounds.turn((query_low, both_low, step_raw, bc_out))
    both_task = rounds.start(along_ctx_steps(both_low, my_index))
    rounds.until_ready(x_w)
    x_out = forth(idx, input_low, x_w.ready)
    x_out = rounds.turn(x_out)
    rounds.until_ready(xz_w)
    xz_out = forth(idx, input_low, xz_w.ready)
    conv_low = jnp.concatenate([x_out, xz_out[:, : DS - part], bc_out], 1).astype(jnp.bfloat16)
    tail_low = from_behind(conv_low[length - (KC - 1) :], "ctx", 1)
    conv_low, tail_low, xz_out = rounds.turn((conv_low, tail_low, xz_out))

    def conv_fn(conv_in, tail_in, kernel_in, bias_in):
        padded = jnp.concatenate([tail_in, conv_in], 0)
        activated = jax.nn.silu(convolve(padded, pad_ids, own_ids, kernel_in, bias_in))
        states_x = activated[:, :DS].reshape(length, NH, HP)
        return (states_x, activated[:, DS : DS + NS], activated[:, DS + NS :])

    def step_fn(shift_in, bias_step, log_rate):
        step_size = jax.nn.softplus(shift_in + bias_step)
        return (step_size, -step_size * jnp.exp(log_rate))

    (states_x, b_matrix, c_matrix), conv_pull = jax.vjp(
        conv_fn, conv_low.astype(jnp.float32), tail_low.astype(jnp.float32), conv_weight, conv_bias
    )
    (step_size, log_decay), step_pull = jax.vjp(step_fn, step_raw, dt_bias, a_log)
    own_parts = (states_x, step_size, log_decay, b_matrix, c_matrix)
    y_part, y_pull = jax.vjp(lambda *parts: ssm_local(*parts, own_ids)[0], *own_parts)
    local_state, state_pull = jax.vjp(lambda *parts: ssm_local(*parts, own_ids)[1], *own_parts)
    decay_now, decay_pull = jax.vjp(lambda log_in: block_decay(log_in, own_ids, prev_id), log_decay)
    y_part, local_state, decay_now = rounds.turn((y_part, local_state, decay_now))
    state_task = rounds.start(entering_steps(decay_now, local_state, my_index, False))
    rounds.until(both_task)
    both_all = both_task.result
    query_groups = query_low.reshape(length, HK, groups, HA)
    seq_len = both_all.shape[0]
    keys_all = both_all[:, : HK * HA].reshape(seq_len, HK, HA)
    values_all = both_all[:, HK * HA :].reshape(seq_len, HK, HA)
    key_places = jnp.arange(seq_len, dtype=jnp.int32)
    allowed = (places[:, None] >= key_places[None, :]) & (own_ids[:, None] == all_ids[None, :])

    score = (
        jnp.einsum("qkgd,rkd->kgqr", query_groups, keys_all, preferred_element_type=jnp.float32)
        * scale
    )
    score = jnp.where(allowed[None, None], score, -1e30)
    new_top = jnp.maximum(-1e30, jnp.max(score, axis=-1))
    soft = jnp.where(allowed[None, None], jnp.exp(score - new_top[..., None]), 0.0)
    total = jnp.sum(soft, axis=-1)
    accum = jnp.einsum(
        "kgqr,rkd->qkgd",
        soft.astype(jnp.bfloat16),
        values_all,
        preferred_element_type=jnp.float32,
    )
    attended = accum / jnp.transpose(total, (2, 0, 1))[..., None]
    log_total = new_top + jnp.log(total)
    attended_low = attended.reshape(length, HQ * HA).astype(jnp.bfloat16)
    attended, log_total, attended_low = rounds.turn((attended, log_total, attended_low))

    rounds.until_ready(z_w)
    gate_z = jnp.concatenate(
        [xz_out[:, DS - part :], forth(idx, input_low, z_w.ready)], 1
    )
    gate_z, grad_low = rounds.turn((gate_z, grad_out.astype(jnp.bfloat16)))
    cotangent_all = every(grad_low, 0)
    rounds.until(state_task)
    rounds.until_ready(oo_w)
    state_in = state_task.result
    y_carry, carry_pull = jax.vjp(
        lambda c_in, log_in, state_arg: ssm_carry(c_in, log_in, own_ids, prev_id, state_arg),
        c_matrix,
        log_decay,
        state_in,
    )
    mixer_normed, tail_pull = jax.vjp(
        mixer_tail, y_part + y_carry, states_x, gate_z, d_skip, mixer_gain
    )
    mixer_low = mixer_normed.astype(jnp.bfloat16)

    def interleaved(mixed_in, attended_in):
        return jnp.concatenate(
            [
                mixed_in.reshape(length, layers, DS // layers),
                attended_in.reshape(length, layers, HQ * HA // layers),
            ],
            2,
        ).reshape(length, DS + HQ * HA)

    def parted(both):
        both = both.reshape(length, layers, (DS + HQ * HA) // layers)
        return (
            both[:, :, : DS // layers].reshape(length, DS),
            both[:, :, DS // layers :].reshape(length, HQ * HA),
        )

    branches_low = interleaved(mixer_low, attended_low)
    middle = hidden + forth(idx, branches_low, oo_w.ready)
    normed_mid, mid_pull = jax.vjp(normed, middle, second_gain)
    mid_low = normed_mid.astype(jnp.bfloat16)
    middle, mid_low, branches_low = rounds.turn((middle, mid_low, branches_low))
    early_deal = dealt(branches_low, input_low)
    rounds.until_ready(gate_w)
    gate_out = forth(idx, mid_low, gate_w.ready)
    gate_out = rounds.turn(gate_out)
    rounds.until_ready(up_w)
    up_out = forth(idx, mid_low, up_w.ready)
    act_value, act_pull = jax.vjp(
        lambda gate_in, up_in: jax.nn.silu(gate_in) * up_in, gate_out, up_out
    )
    act_low = act_value.astype(jnp.bfloat16)
    act_low = rounds.turn(act_low)

    rounds.until_ready(down_w)
    late_deal = dealt(act_low, mid_low)
    d_act = rounds.turn(back(idx, grad_low, down_w.ready))
    d_gate, d_up = act_pull(d_act)
    gate_low, up_low = d_gate.astype(jnp.bfloat16), d_up.astype(jnp.bfloat16)
    gate_low, up_low = rounds.turn((gate_low, up_low))
    gate_all, up_all = every(gate_low, 3), every(up_low, 6)
    shard_rows = mid_low.shape[1] // layers

    down_grad = weight_grad(
        [(late_deal, 0, cotangent_all)],
        lambda pair: finished(idx, [pair], [(0, 0, D)]),
    )
    gate_up_grad = weight_grad(
        [(late_deal, 1, gate_all), (late_deal, 1, up_all)],
        lambda pair: finished(idx, [pair], [(0, 0, 2 * FF)]),
        down_grad,
    )
    d_mid_norm = back(idx, gate_low, gate_w.ready)
    d_mid_norm = rounds.turn(d_mid_norm)
    d_mid_norm = d_mid_norm + back(idx, up_low, up_w.ready)
    d_middle_part, d_second_gain = mid_pull(d_mid_norm)
    d_middle = grad_out + d_middle_part
    branch_low = d_middle.astype(jnp.bfloat16)
    branch_low, d_middle = rounds.turn((branch_low, d_middle))
    branch_all = every(branch_low, 6)
    d_mixer_norm, d_attended = parted(back(idx, branch_low, oo_w.ready))
    d_mixer_norm, d_attended = rounds.turn((d_mixer_norm, d_attended))
    d_core, d_states_tail, d_gate_z, d_d_skip, d_mixer_gain = tail_pull(d_mixer_norm)
    z_low = d_gate_z.astype(jnp.bfloat16)
    z_low, d_core, d_states_tail = rounds.turn((z_low, d_core, d_states_tail))
    z_all = every(z_low, 6)
    oo_z_grad = weight_grad(
        [(early_deal, 0, branch_all), (early_deal, 1, z_all)], lambda pair: pair, gate_up_grad
    )
    d_c_carry, d_log_carry, d_state_in = carry_pull(d_core)
    mixed = middle + forth(idx, act_low, down_w.ready)
    d_c_carry, d_log_carry, d_state_in, mixed = rounds.turn(
        (d_c_carry, d_log_carry, d_state_in, mixed)
    )
    later_task = rounds.start(entering_steps(decay_now, d_state_in, my_index, True))
    d_out_low = d_attended.reshape(length, HK, groups, HA).astype(jnp.bfloat16)
    delta = jnp.transpose(jnp.sum(d_out_low.astype(jnp.float32) * attended, axis=-1), (1, 2, 0))
    score = (
        jnp.einsum("qkgd,rkd->kgqr", query_groups, keys_all, preferred_element_type=jnp.float32)
        * scale
    )
    prob = jnp.where(
        allowed[None, None],
        jnp.exp(jnp.where(allowed[None, None], score, 0.0) - log_total[..., None]),
        0.0,
    )
    d_prob = jnp.einsum(
        "qkgd,rkd->kgqr", d_out_low, values_all, preferred_element_type=jnp.float32
    )
    score_grad = (prob * (d_prob - delta[..., None])).astype(jnp.bfloat16)
    d_query = (
        jnp.einsum("kgqr,rkd->qkgd", score_grad, keys_all, preferred_element_type=jnp.float32)
        * scale
    )
    d_keys = (
        jnp.einsum("kgqr,qkgd->rkd", score_grad, query_groups, preferred_element_type=jnp.float32)
        * scale
    )
    d_values = jnp.einsum(
        "kgqr,qkgd->rkd", prob.astype(jnp.bfloat16), d_out_low, preferred_element_type=jnp.float32
    )
    kv_terms = jnp.concatenate(
        [d_keys.reshape(seq_len, HK * HA), d_values.reshape(seq_len, HK * HA)], 1
    ).astype(jnp.bfloat16)
    kv_terms, d_query = rounds.turn((kv_terms, d_query))
    kv_task = rounds.start(sum_rows_steps(kv_terms, my_index))
    y_grads = rounds.turn(y_pull(d_core))
    rounds.until(later_task)
    later_grad = later_task.result
    state_grads = rounds.turn(state_pull(later_grad))
    d_decay = jnp.sum(later_grad * state_in, axis=(1, 2))
    d_log_decay = decay_pull(d_decay)[0]
    d_states, d_step, d_log, d_b, d_c = jax.tree.map(jnp.add, y_grads, state_grads)
    d_conv_in, d_tail, d_conv_weight, d_conv_bias = conv_pull(
        (d_states + d_states_tail, d_b, d_c + d_c_carry)
    )
    d_step_raw, d_dt_bias, d_a_log = step_pull((d_step, d_log + d_log_carry + d_log_decay))
    d_conv_in, d_tail, d_step_raw = rounds.turn((d_conv_in, d_tail, d_step_raw))
    rounds.until(kv_task)
    d_kv = kv_task.result.astype(jnp.float32)
    qkv_low = jnp.concatenate(
        [
            rotate(d_query.reshape(length, HQ, HA), places, -1.0).reshape(length, HQ * HA),
            rotate(d_kv[:, : HK * HA].reshape(length, HK, HA), places, -1.0).reshape(
                length, HK * HA
            ),
            d_kv[:, HK * HA :],
        ],
        1,
    ).astype(jnp.bfloat16)
    from_next = from_behind(d_tail.astype(jnp.bfloat16), "ctx", -1).astype(d_tail.dtype)
    d_conv_in = jnp.concatenate(
        [d_conv_in[: length - (KC - 1)], d_conv_in[length - (KC - 1) :] + from_next], 0
    )
    conv_grad_low = d_conv_in.astype(jnp.bfloat16)
    step_low = d_step_raw.astype(jnp.bfloat16)
    blank = jnp.zeros((length, 512 - NH), jnp.bfloat16)
    tail_low = jnp.concatenate([conv_grad_low, step_low, blank[:, : 256 - NH], qkv_low], 1)
    conv_grad_low, step_low, qkv_low, tail_low = rounds.turn(
        (conv_grad_low, step_low, qkv_low, tail_low)
    )
    tail_grad = weight_grad(
        [(early_deal, 1, every(tail_low, 4))], lambda pair: pair
    )
    d_normed_in = (
        back(idx, conv_grad_low[:, :part], x_w.ready)
        + back(
            idx,
            jnp.concatenate([conv_grad_low[:, part:DS], z_low[:, : DS - part]], 1),
            xz_w.ready,
        )
    )
    d_normed_in = rounds.turn(d_normed_in)
    d_normed_in = (
        d_normed_in
        + back(idx, z_low[:, DS - part :], z_w.ready)
        + back(idx, jnp.concatenate([qkv_low, conv_grad_low[:, DS:]], 1), qb_w.ready)
        + project_back(step_low, dt_task.result)
    )
    d_hidden_part, d_first_gain = norm_pull(d_normed_in)
    d_tokens = d_middle + d_hidden_part
    d_tokens, d_first_gain = rounds.turn((d_tokens, d_first_gain))
    smalls_task = rounds.start(
        sum_steps(
            (
                d_conv_weight,
                d_conv_bias,
                d_dt_bias,
                d_a_log,
                d_d_skip,
                d_mixer_gain,
                d_first_gain,
                d_second_gain,
            )
        )
    )
    rounds.until(smalls_task, gate_up_grad, down_grad, oo_z_grad, tail_grad)
    smalls = smalls_task.result
    tail_pair, oo_z_pair = tail_grad.result, oo_z_grad.result
    blocks = branches_low.shape[1] // layers // shard_rows
    z_first = blocks * D
    oo = [
        finished(idx, [oo_z_pair], [(0, at * D, (at + 1) * D)]) for at in range(blocks)
    ]
    tail_half = tail_pair[0].shape[1]
    step_grad = jnp.where(core == 1, tail_pair[0], tail_pair[1])
    return (
        mixed[None].astype(jnp.bfloat16),
        d_tokens[None],
        finished(idx, [oo_z_pair, tail_pair], [(0, z_first, z_first + DS), (1, 0, conv_cols)]),
        step_grad[:, conv_cols - tail_half : conv_cols - tail_half + NH].astype(jnp.float32),
        smalls[0],
        smalls[1],
        smalls[2],
        smalls[3],
        smalls[4],
        smalls[5],
        jnp.concatenate(oo, 0)[: DS // layers],
        finished(idx, [tail_pair], [(0, conv_cols + 256, conv_cols + 256 + qkv_cols)]),
        jnp.concatenate(oo, 0)[DS // layers :],
        smalls[6],
        smalls[7],
        gate_up_grad.result,
        down_grad.result,
    )


def solution(mesh):
    return jax.shard_map(
        body,
        mesh=mesh,
        in_specs=(
            P("fsdp", "ctx", None),
            P("fsdp", "ctx", None),
            P("fsdp", "ctx"),
            P("fsdp", None),
            P("fsdp", None),
            P(),
            P(),
            P(),
            P(),
            P(),
            P(),
            P("fsdp", None),
            P("fsdp", None),
            P("fsdp", None),
            P(),
            P(),
            P("fsdp", None),
            P("fsdp", None),
        ),
        out_specs=(
            P("fsdp", "ctx", None),
            P("fsdp", "ctx", None),
            P("fsdp", None),
            P("fsdp", None),
            P(),
            P(),
            P(),
            P(),
            P(),
            P(),
            P("fsdp", None),
            P("fsdp", None),
            P("fsdp", None),
            P(),
            P(),
            P("fsdp", None),
            P("fsdp", None),
        ),
        check_vma=False,
    )
```

```python
import jax
import jax.numpy as jnp
from jax import lax
from jax.experimental import pallas as pl
from jax.experimental.pallas import tpu as pltpu
from jax.sharding import PartitionSpec as P

D = 2048
FF = 4096
NH = 48
HP = 64
NS = 256
KC = 4
HQ = 8
HK = 2
HA = 128
DS = 3072


HIGH = lax.Precision.HIGHEST
epsilon = 1e-05
rope_base = 100000000000.0


def from_behind(block, axis, distance):
    devices = range(lax.axis_size(axis))
    route = [(i - distance, i) for i in devices if i - distance in devices]
    return lax.ppermute(block, axis, route)


def normed(operand, gain_vec):
    return (
        operand
        * lax.rsqrt(jnp.mean(operand * operand, axis=-1, keepdims=True) + epsilon)
        * gain_vec
    )


def rotate(operand, places, direction):
    half_width = operand.shape[-1] // 2
    frequency = rope_base ** (
        -jnp.arange(half_width, dtype=jnp.float32) * (2.0 / operand.shape[-1])
    )
    angles = places.astype(jnp.float32)[:, None] * frequency[None, :]
    cosine = jnp.cos(angles)[:, None, :]
    sine_part = direction * jnp.sin(angles)[:, None, :]
    first_half = operand[..., :half_width]
    second_half = operand[..., half_width:]
    return jnp.concatenate(
        [
            first_half * cosine - second_half * sine_part,
            second_half * cosine + first_half * sine_part,
        ],
        -1,
    )


def project(left_side, right_side):
    return jnp.dot(left_side, right_side, preferred_element_type=jnp.float32)


def project_back(grad_in, weight):
    return lax.dot_general(
        grad_in, weight, (((1,), (1,)), ((), ())), preferred_element_type=jnp.float32
    )


def convolve(padded, pad_ids, row_ids, kernel_in, bias_in):
    length = row_ids.shape[0]
    total = jnp.zeros((length, padded.shape[1]), jnp.float32) + bias_in[None, :]
    for offset in range(KC):
        same_doc = (pad_ids[offset : offset + length] == row_ids).astype(jnp.float32)
        total = (
            total
            + kernel_in[offset][None, :] * padded[offset : offset + length] * same_doc[:, None]
        )
    return total


def ssm_local(states_x, step_size, log_decay, b_matrix, c_matrix, row_ids):
    length = states_x.shape[0]
    running = jnp.cumsum(log_decay, axis=0)
    places = jnp.arange(length, dtype=jnp.int32)
    allowed = (places[:, None] >= places[None, :]) & (row_ids[:, None] == row_ids[None, :])
    spread = running.T[:, :, None] - running.T[:, None, :]
    decay_matrix = jnp.where(allowed[None], jnp.exp(jnp.where(allowed[None], spread, 0.0)), 0.0)
    intersection = jnp.dot(c_matrix, b_matrix.T, precision=HIGH, preferred_element_type=jnp.float32)
    driven = step_size[:, :, None] * states_x
    y_part = jnp.einsum("hts,shp->thp", decay_matrix * intersection[None], driven, precision=HIGH)
    to_end = jnp.where(
        (row_ids == row_ids[-1])[:, None], jnp.exp(running[-1][None, :] - running), 0.0
    )
    local_state = jnp.einsum("sh,shp,sn->hpn", to_end, driven, b_matrix, precision=HIGH)
    return (y_part, local_state)


def ssm_carry(c_matrix, log_decay, row_ids, prev_id, state_in):
    kept_mask = (row_ids == prev_id).astype(jnp.float32)
    weight = jnp.exp(jnp.cumsum(log_decay, axis=0)) * kept_mask[:, None]
    return weight[:, :, None] * jnp.einsum("hpn,tn->thp", state_in, c_matrix, precision=HIGH)


def block_decay(log_decay, row_ids, prev_id):
    return jnp.exp(jnp.sum(log_decay, axis=0)) * (row_ids[-1] == prev_id).astype(jnp.float32)


def mixer_tail(core_in, states_x, gate_z, skip_in, gain_in):
    length = core_in.shape[0]
    core = core_in + skip_in[None, :, None] * states_x
    gated = core.reshape(length, DS) * jax.nn.silu(gate_z)
    return normed(gated, gain_in)


def swiglu(gate_up_out):
    return jax.nn.silu(gate_up_out[:, :FF]) * gate_up_out[:, FF:]


def swap(block, distance):
    peers = lax.axis_size("ctx")
    return lax.ppermute(block, "ctx", [(i, i ^ distance) for i in range(peers)])


def shifted(block, hops):
    peers = lax.axis_size("fsdp")
    return lax.ppermute(block, "fsdp", [(i, (i + hops) % peers) for i in range(peers)])


def powers(first, limit):
    found = []
    while first < limit:
        found.append(first)
        first *= 2
    return found


def chip_steps():
    return powers(2, lax.axis_size("ctx"))


def ordered(flag, first, second, axis):
    return jnp.where(
        flag,
        jnp.concatenate([second, first], axis),
        jnp.concatenate([first, second], axis),
    )


def halves(flag, array, axis):
    size = array.shape[axis] // 2
    low = lax.slice_in_dim(array, 0, size, axis=axis)
    high = lax.slice_in_dim(array, size, 2 * size, axis=axis)
    return (jnp.where(flag, high, low), jnp.where(flag, low, high))


def join(earlier, later):
    return (earlier[0] * later[0], later[0][:, None, None] * earlier[1] + later[1])


def either(flag, when, otherwise):
    return jax.tree.map(lambda a, b: jnp.where(flag, a, b), when, otherwise)


class Last:
    def __init__(self, value):
        self.value = value


class Task:
    def __init__(self, steps):
        self.steps, self.ready, self.result = steps, None, None


class Rounds:
    def __init__(self):
        self.tasks = []

    def start(self, steps):
        self.tasks.append(Task(steps))
        return self.tasks[-1]

    def turn(self, values=()):
        found = []
        for task in self.tasks:
            try:
                found.append(task.steps.send(task.ready))
            except StopIteration:
                found.append(Last(()))
        held = [step.value if isinstance(step, Last) else step for step in found]
        values, held = lax.optimization_barrier((values, held))
        going = []
        for task, step, ready in zip(self.tasks, found, held, strict=True):
            task.ready = ready
            if isinstance(step, Last):
                task.result = ready
            else:
                going.append(task)
        self.tasks = going
        return values

    def until(self, *tasks):
        while any(task.result is None for task in tasks):
            self.turn()

    def until_ready(self, *weights):
        while any(weight.ready is None for weight in weights):
            self.turn()


def entering_steps(decay, state, place, backwards):
    def sent(pair, step):
        return (swap(pair[0], step), swap(pair[1].astype(jnp.bfloat16), step))

    def read(pair):
        return (pair[0], pair[1].astype(jnp.float32))

    def is_later(step):
        return (jnp.bitwise_and(place, step) != 0) != backwards

    core = jnp.bitwise_and(place, 1) == 1
    near = read(sent((decay, state), 1))
    total = either(is_later(1), join(near, (decay, state)), join((decay, state), near))
    total = tuple(halves(core, part, 0)[0] for part in total)
    before = (jnp.ones_like(total[0]), jnp.zeros_like(total[1]))
    steps = chip_steps()
    for step in steps:
        there = read(sent(total, step))
        before = either(is_later(step), join(there, before), before)
        if step != steps[-1]:
            total = either(is_later(step), join(there, total), join(total, there))
            total, before, near = yield total, before, near
    across = swap(before[1].astype(jnp.bfloat16), 1).astype(jnp.float32)
    whole = ordered(core, before[1], across, 0)
    yield Last(jnp.where(is_later(1), near[0][:, None, None] * whole + near[1], whole))


class Weight:
    def __init__(self, shard, width):
        self.shard, self.width, self.chunks, self.ready = shard, width, [], None

    def cuts(self, idx, rows, columns):
        chip, core = idx[0], idx[1]
        per = rows * (lax.axis_size("ctx") // 2)
        for first_row in range(0, self.shard.shape[0], per):
            for first_col in range(0, self.width // 2, columns):
                piece = lax.dynamic_slice(
                    self.shard,
                    (first_row + chip * rows, first_col + core * (self.width // 2)),
                    (rows, columns),
                )
                self.chunks.append((first_row, first_col, []))
                yield piece, self.chunks[-1][2]


class Box:
    def __init__(self, value):
        self.value = value


def copy_all(copies):
    for copy in copies:
        copy.start()
    for copy in copies:
        copy.wait()


def place_kernel(chunks, idx_ref, shard_ref, *refs):
    whole_ref, sems = refs[-2], refs[-1]
    chip, core, layer = idx_ref[0], idx_ref[1], idx_ref[2]
    depth, width = shard_ref.shape[0], whole_ref.shape[1]
    layers = whole_ref.shape[0] // depth
    copies = [
        pltpu.make_async_copy(
            shard_ref.at[:, pl.ds(pl.multiple_of(core * width, 128), width)],
            whole_ref.at[pl.ds(pl.multiple_of(layer * depth, depth), depth), :],
            sems.at[0],
        )
    ]
    for first_row, first_col, found in chunks:
        for side, others, source, first in found:
            rows, columns = refs[source].shape[1:]
            for number, other in enumerate(others):
                for hop in range(layers - 1):
                    owner = lax.rem(layer + 1 + hop, layers)
                    begin = owner * depth + first_row + jnp.bitwise_xor(chip, other) * rows
                    copies.append(
                        pltpu.make_async_copy(
                            refs[source].at[first + number * (layers - 1) + hop],
                            whole_ref.at[
                                pl.ds(pl.multiple_of(begin, rows), rows),
                                pl.ds(first_col + side * columns, columns),
                            ],
                            sems.at[len(copies)],
                        )
                    )
    copy_all(copies)


def placed(idx, weight):
    layers = lax.axis_size("fsdp")
    depth, width = weight.shard.shape[0], weight.width // 2
    boxes = list({id(box): box for _, _, found in weight.chunks for _, _, box, _ in found}.values())
    chunks = [
        (
            first_row,
            first_col,
            [(side, others, boxes.index(box), first) for side, others, box, first in found],
        )
        for first_row, first_col, found in weight.chunks
    ]
    count = 1 + sum(
        (layers - 1) * len(others) for _, _, found in chunks for _, others, _, _ in found
    )
    return pl.pallas_call(
        lambda *refs: place_kernel(chunks, *refs),
        out_shape=jax.ShapeDtypeStruct((layers * depth, width), weight.shard.dtype),
        in_specs=[pl.BlockSpec(memory_space=pltpu.SMEM)]
        + [pl.BlockSpec(memory_space=pl.ANY)] * (1 + len(boxes)),
        out_specs=pl.BlockSpec(memory_space=pltpu.VMEM),
        scratch_shapes=[pltpu.SemaphoreType.DMA((count,))],
        compiler_params=pltpu.CompilerParams(vmem_limit_bytes=56 * 1024 * 1024),
        cost_estimate=pl.CostEstimate(flops=1024, bytes_accessed=1024, transcendentals=0),
        name="place",
    )(idx, weight.shard, *[box.value for box in boxes])


def pack_kernel(fresh, plan, inputs, idx_ref, *refs):
    layer = idx_ref[2]
    outs, sems = refs[inputs:-1], refs[-1]
    copies = []
    for out, first, side in fresh:
        layers, columns = refs[0].shape[0], outs[out].shape[2]
        for hop in range(layers - 1):
            owner = lax.rem(layer + 1 + hop, layers)
            copies.append(
                pltpu.make_async_copy(
                    refs[0].at[owner, :, pl.ds(side * columns, columns)],
                    outs[out].at[first + hop],
                    sems.at[len(copies)],
                )
            )
    for out, first, source, begin, size in plan:
        copies.append(
            pltpu.make_async_copy(
                refs[source].at[pl.ds(begin, size)],
                outs[out].at[pl.ds(first, size)],
                sems.at[len(copies)],
            )
        )
    copy_all(copies)


def packed(idx, along, fresh, plan, sizes, rows, columns):
    boxes = list({id(entry[2]): entry[2] for entry in plan}.values())
    arrays = ([] if along is None else [along]) + [box.value for box in boxes]
    skip = len(arrays) - len(boxes)
    plan = [(out, row, skip + boxes.index(box), begin, size) for out, row, box, begin, size in plan]
    count = len(fresh) * (lax.axis_size("fsdp") - 1) + len(plan)
    return pl.pallas_call(
        lambda *refs: pack_kernel(fresh, plan, len(arrays), *refs),
        out_shape=[jax.ShapeDtypeStruct((size, rows, columns), jnp.bfloat16) for size in sizes],
        in_specs=[pl.BlockSpec(memory_space=pltpu.SMEM)]
        + [pl.BlockSpec(memory_space=pl.ANY)] * len(arrays),
        out_specs=[pl.BlockSpec(memory_space=pltpu.VMEM)] * len(sizes),
        scratch_shapes=[pltpu.SemaphoreType.DMA((count,))],
        compiler_params=pltpu.CompilerParams(vmem_limit_bytes=56 * 1024 * 1024),
        cost_estimate=pl.CostEstimate(flops=1024, bytes_accessed=1024, transcendentals=0),
        name="pack",
    )(idx, *arrays)


def whole_steps(piece, turns, wait):
    for _ in range(turns):
        piece = yield piece
    whole = lax.all_gather(piece, ("fsdp", "ctx"), axis=0, tiled=True)
    for _ in range(wait):
        yield ()
    yield Last(whole)


def gather_steps(idx, weights, rows, columns):
    steps, layers = chip_steps(), lax.axis_size("fsdp")
    half, near = columns // 2, layers - 1
    pieces, sinks, owners = [], [], []
    for weight in weights:
        for piece, sink in weight.cuts(idx, rows, columns):
            pieces.append(piece)
            sinks.append(sink)
            owners.append(weight)
    along, halved = {}, []
    for turn in range(len(pieces) + len(steps) + 3):
        if turn < len(pieces):
            along[turn] = lax.all_gather(pieces[turn], "fsdp")
        fresh, plan, sizes, comes = [], [], {step: 0 for step in steps}, []
        used = []
        for stage in range(len(steps)):
            at = turn - 1 - stage
            if not 0 <= at < len(pieces):
                continue
            for side in range(2):
                step = (steps[side:] + steps[:side])[stage]
                out = steps.index(step)
                first = sizes[step]
                reached = []
                if stage == 0:
                    fresh.append((out, first, side))
                    used.append((at, side, [0], step, first))
                    reached, sizes[step] = [0], first + near
                for _, others, box, begin in [e for e in sinks[at] if e[0] == side]:
                    plan.append((out, sizes[step], box, begin, near * len(others)))
                    sizes[step] += near * len(others)
                    reached = reached + others
                comes.append((at, side, [other ^ (step // 2) for other in reached], step, first))
        active = [step for step in steps if sizes[step]]
        blocks = {}
        if active:
            rank = {steps.index(step): number for number, step in enumerate(active)}
            made = packed(
                idx,
                along.pop(turn - 1, None) if fresh else None,
                [(rank[out], first, side) for out, first, side in fresh],
                [(rank[out], *rest) for out, *rest in plan],
                [sizes[step] for step in active],
                rows,
                half,
            )
            blocks = dict(zip(active, made, strict=True))
        blocks, pieces = lax.optimization_barrier((blocks, pieces))
        got = {step: swap(block, step) for step, block in blocks.items()}
        whole = [
            weight
            for at, weight in enumerate(owners)
            if at == turn - 1 - len(steps) and weight not in owners[at + 1 :]
        ]
        ready = [(weight, mine, swap(mine, 1)) for weight, mine in halved]
        halved = [(weight, placed(idx, weight)) for weight in whole]
        for weight in whole:
            for sink, owner in zip(sinks, owners, strict=True):
                if owner is weight:
                    sink.clear()
        kept = {step: Box(block) for step, block in blocks.items()}
        sent = {step: Box(block) for step, block in got.items()}
        flying = list(sent.values())
        for at, side, others, step, first in used:
            sinks[at].append((side, others, kept[step], first))
        for at, side, others, step, first in comes:
            sinks[at].append((side, others, sent[step], first))
        now_ready = [weight for weight, _, _ in ready]
        for weight, mine, other in ready:
            weight.ready = (mine, other)
        late, pieces, now, ready, mines = yield (
            [box.value for box in flying],
            pieces,
            {turn: along[turn]} if turn in along else {},
            [(mine, other) for _, mine, other in ready],
            [mine for _, mine in halved],
        )
        for box, value in zip(flying, late, strict=True):
            box.value = value
        along.update(now)
        for weight, pair in zip(now_ready, ready, strict=True):
            weight.ready = pair
        halved = [(weight, mine) for (weight, _), mine in zip(halved, mines, strict=True)]


def ring_steps(block, layer):
    peers, length = lax.axis_size("fsdp"), block.shape[0]
    found = [block]
    for _ in range(peers - 1):
        found.append((yield shifted(found[-1], 1)))
    ahead = found[:1] + found[:0:-1]
    twice = jnp.concatenate(ahead + ahead, 0)
    whole = lax.dynamic_slice_in_dim(
        twice, lax.rem(peers - layer, peers) * length, peers * length, 0
    )
    yield Last(whole)


def deal_steps(arrays, layer):
    peers = lax.axis_size("fsdp")
    widths = [array.shape[1] // peers for array in arrays]

    def cut(hops):
        to = lax.rem(layer + hops, peers)
        return jnp.concatenate(
            [
                lax.dynamic_slice_in_dim(array, to * width, width, 1)
                for array, width in zip(arrays, widths, strict=True)
            ],
            1,
        )

    ahead = [cut(0)]
    for hops in range(1, peers):
        ahead.append((yield shifted(cut(peers - hops), peers - hops)))
    whole = jnp.concatenate(
        [lax.select_n(lax.rem(at + peers - layer, peers), *ahead) for at in range(peers)], 0
    )
    found, at = [], 0
    for width in widths:
        found.append(whole[:, at : at + width])
        at += width
    yield Last(found)


def every_steps(block, wait):
    found = lax.all_gather(block, "fsdp", axis=0, tiled=True)
    for _ in range(wait):
        yield ()
    yield Last(found)


def added(left_side, right_side):
    return (left_side.astype(jnp.float32) + right_side.astype(jnp.float32)).astype(jnp.bfloat16)


def weight_steps(products, place, finish, after):
    steps, core = chip_steps(), jnp.bitwise_and(place, 1) == 1
    while any(task.result is None for act, _, grad in products for task in (act, grad)) or any(
        task.result is None for task in after
    ):
        yield ()
    rows = min(act.result[which].shape[1] for act, which, _ in products)
    parts = []
    for act, which, grad in products:
        array = act.result[which]
        for first in range(0, array.shape[1], rows):
            parts.append(
                lax.dot_general(
                    array[:, first : first + rows],
                    grad.result,
                    (((0,), (0,)), ((), ())),
                    preferred_element_type=jnp.float32,
                ).astype(jnp.bfloat16)
            )
    part = jnp.concatenate(parts, 1) if len(parts) > 1 else parts[0]
    own, other = halves(core, part, 1)
    own = added(own, swap(other, 1))
    size = own.shape[0] // 2
    blocks = [own[:size], own[size:]]
    orders = [steps[side:] + steps[:side] for side in range(2)]
    moves = [(stage, True) for stage in range(len(steps))]
    moves += [(stage, False) for stage in range(len(steps))[::-1]]
    for number, (stage, adds) in enumerate(moves):
        for side in range(2):
            step = orders[side][stage]
            flag = jnp.bitwise_and(place, step) != 0
            if adds:
                keep, send = halves(flag, blocks[side], 0)
                blocks[side] = added(keep, swap(send, step))
            else:
                blocks[side] = ordered(flag, blocks[side], swap(blocks[side], step), 0)
        if number % 2 == 0:
            blocks = list((yield blocks))
    own = jnp.concatenate(blocks, 0)
    pair = yield own, swap(own, 1)
    yield Last(finish(pair))


def finish_kernel(segments, idx_ref, *refs):
    out_ref = refs[-1]
    for flag in (0, 1):

        @pl.when(idx_ref[1] == flag)
        def _():
            at = 0
            for number, first, last in segments:
                pair = refs[2 * number : 2 * number + 2]
                half = pair[0].shape[1]
                for part, begin, end in (
                    (pair[flag], first, min(last, half)),
                    (pair[1 - flag], max(first, half) - half, last - half),
                ):
                    if begin < end:
                        out_ref[:, at : at + end - begin] = part[:, begin:end].astype(jnp.float32)
                        at += end - begin


def finished(idx, pairs, segments, first_row=0, rows=None):
    rows = rows or pairs[0][0].shape[0]
    width = sum(last - first for _, first, last in segments)
    block = 32
    while block < 256 and rows % (2 * block) == 0 and first_row % (2 * block) == 0:
        block *= 2
    while block > 32 and block * width > 1024 * 1024:
        block //= 2
    skip = first_row // block
    flat = [part for pair in pairs for part in pair]
    return pl.pallas_call(
        lambda *refs: finish_kernel(segments, *refs),
        grid=(rows // block,),
        out_shape=jax.ShapeDtypeStruct((rows, width), jnp.float32),
        in_specs=[pl.BlockSpec(memory_space=pltpu.SMEM)]
        + [pl.BlockSpec((block, part.shape[1]), lambda i: (i + skip, 0)) for part in flat],
        out_specs=pl.BlockSpec((block, width), lambda i: (i, 0)),
        compiler_params=pltpu.CompilerParams(vmem_limit_bytes=56 * 1024 * 1024),
        cost_estimate=pl.CostEstimate(flops=1024, bytes_accessed=1024, transcendentals=0),
        name="finish",
    )(idx, *flat)


def finish_steps(tasks, finish):
    while any(task.result is None for task in tasks):
        yield ()
    yield Last(finish(*[task.result for task in tasks]))


def rows_kernel(cases, idx_ref, low_ref, high_ref, out_ref):
    half = low_ref.shape[1]
    for number, (_, first, last) in enumerate(cases):
        for flag in (0, 1):
            low, high = (low_ref, high_ref) if flag == 0 else (high_ref, low_ref)

            @pl.when((pl.program_id(0) == number) & (idx_ref[1] == flag))
            def _():
                at = 0
                for part, begin, end in (
                    (low, first, min(last, half)),
                    (high, max(first, half) - half, last - half),
                ):
                    if begin < end:
                        out_ref[:, at : at + end - begin] = part[:, begin:end].astype(jnp.float32)
                        at += end - begin


def finished_rows(idx, pair, cases, rows):
    width, numbers = cases[0][2] - cases[0][1], [number for number, _, _ in cases]

    def place(i, idx):
        return (sum((i == at) * number for at, number in enumerate(numbers)), 0)

    return pl.pallas_call(
        lambda *refs: rows_kernel(cases, *refs),
        grid_spec=pltpu.PrefetchScalarGridSpec(
            num_scalar_prefetch=1,
            grid=(len(cases),),
            in_specs=[pl.BlockSpec((rows, part.shape[1]), place) for part in pair],
            out_specs=pl.BlockSpec((rows, width), lambda i, idx: (i, 0)),
        ),
        out_shape=jax.ShapeDtypeStruct((len(cases) * rows, width), jnp.float32),
        compiler_params=pltpu.CompilerParams(vmem_limit_bytes=56 * 1024 * 1024),
        cost_estimate=pl.CostEstimate(flops=1024, bytes_accessed=1024, transcendentals=0),
        name="finish_rows",
    )(idx, *pair)


def along_ctx(block, place):
    for step in powers(1, lax.axis_size("ctx")):
        block = ordered(jnp.bitwise_and(place, step) != 0, block, swap(block, step), 0)
    return block


def along_ctx_steps(block, place):
    for step in powers(1, lax.axis_size("ctx")):
        got = yield swap(block, step)
        block = ordered(jnp.bitwise_and(place, step) != 0, block, got, 0)
    yield Last(block)


def sum_rows_steps(block, place):
    for step in powers(1, lax.axis_size("ctx"))[::-1]:
        keep, send = halves(jnp.bitwise_and(place, step) != 0, block, 0)
        got, keep = yield swap(send, step), keep
        block = added(keep, got)
    yield Last(block)


def summed_rows(block, place):
    for step in powers(1, lax.axis_size("ctx"))[::-1]:
        keep, send = halves(jnp.bitwise_and(place, step) != 0, block, 0)
        block = added(keep, swap(send, step))
    return block


def forth_kernel(idx_ref, left_ref, own_ref, other_ref, out_ref):
    width = own_ref.shape[1]
    for part_ref, half in ((own_ref, idx_ref[1]), (other_ref, 1 - idx_ref[1])):
        columns = pl.ds(pl.multiple_of(half * width, 128), width)
        term = jnp.dot(left_ref[...], part_ref[...], preferred_element_type=jnp.float32)

        @pl.when(pl.program_id(0) == 0)
        def _():
            out_ref[:, columns] = term

        @pl.when(pl.program_id(0) != 0)
        def _():
            out_ref[:, columns] += term


def back_kernel(idx_ref, grad_ref, own_ref, other_ref, out_ref):
    width, total = own_ref.shape[1], None
    for part_ref, half in ((own_ref, idx_ref[1]), (other_ref, 1 - idx_ref[1])):
        term = lax.dot_general(
            grad_ref[:, pl.ds(pl.multiple_of(half * width, 128), width)],
            part_ref[...],
            (((1,), (1,)), ((), ())),
            preferred_element_type=jnp.float32,
        )
        total = term if total is None else total + term
    out_ref[...] = total


def product(kernel, name, idx, operand, chunk, in_spec, out_spec, columns):
    rows, (depth, width) = operand.shape[0], chunk[0].shape
    part = pl.BlockSpec((depth // 4, width), lambda t, idx: (t, 0))
    return pl.pallas_call(
        kernel,
        grid_spec=pltpu.PrefetchScalarGridSpec(
            num_scalar_prefetch=1, grid=(4,), in_specs=[in_spec, part, part], out_specs=out_spec
        ),
        out_shape=jax.ShapeDtypeStruct((rows, columns), jnp.float32),
        compiler_params=pltpu.CompilerParams(vmem_limit_bytes=56 * 1024 * 1024),
        cost_estimate=pl.CostEstimate(flops=1024, bytes_accessed=1024, transcendentals=0),
        name=name,
    )(idx, operand, *chunk)


def forth(idx, left_side, chunk):
    rows, (depth, width) = left_side.shape[0], chunk[0].shape
    in_spec = pl.BlockSpec((rows, depth // 4), lambda t, idx: (0, t))
    out_spec = pl.BlockSpec((rows, 2 * width), lambda t, idx: (0, 0))
    return product(forth_kernel, "forth", idx, left_side, chunk, in_spec, out_spec, 2 * width)


def back(idx, grad_in, chunk):
    rows, (depth, width) = grad_in.shape[0], chunk[0].shape
    in_spec = pl.BlockSpec((rows, 2 * width), lambda t, idx: (0, 0))
    out_spec = pl.BlockSpec((rows, depth // 4), lambda t, idx: (0, t))
    return product(back_kernel, "back", idx, grad_in, chunk, in_spec, out_spec, depth)


def sum_steps(arrays):
    flat = jnp.concatenate([array.reshape(-1) for array in arrays])
    size = flat.shape[0]
    flat = jnp.pad(flat, (0, -size % 1024)).reshape(-1, 128)
    for axis in ("ctx", "fsdp"):
        peers = lax.axis_size(axis)
        for step in powers(1, peers):
            flat = yield flat + lax.ppermute(flat, axis, [(i, i ^ step) for i in range(peers)])
    flat, found, at = flat.reshape(-1), [], 0
    for array in arrays:
        found.append(flat[at : at + array.size].reshape(array.shape))
        at += array.size
    yield Last(found)


def body(
    tokens,
    cotangent,
    doc_ids,
    in_proj,
    dt_proj,
    conv_weight,
    conv_bias,
    dt_bias,
    a_log,
    d_skip,
    mixer_gain,
    out_proj,
    qkv_proj,
    o_proj,
    first_gain,
    second_gain,
    gate_up,
    down_proj,
):
    my_index, layer = lax.axis_index("ctx"), lax.axis_index("fsdp")
    layers = lax.axis_size("fsdp")
    core, chip = jnp.bitwise_and(my_index, 1), my_index // 2
    idx = jnp.stack([chip, core, layer]).astype(jnp.int32)
    conv_cols, qkv_cols = DS + 2 * NS, (HQ + 2 * HK) * HA
    kv_bc = jnp.concatenate([qkv_proj, in_proj[:, 2 * DS :]], 1)
    z_x = in_proj[:, : 2 * DS]
    out_o = jnp.concatenate([out_proj, o_proj], 0)
    rounds = Rounds()

    def dealt(*arrays):
        return rounds.start(deal_steps(arrays, layer))

    def every(block, wait):
        return rounds.start(every_steps(block, wait))

    def weight_grad(products, finish, *after):
        return rounds.start(weight_steps(products, my_index, finish, list(after)))

    part = 2048
    qb_w = Weight(kv_bc, part)
    x_w = Weight(in_proj[:, DS : DS + part], part)
    xz_w = Weight(
        jnp.concatenate([in_proj[:, DS + part : 2 * DS], in_proj[:, : DS - part]], 1), part
    )
    z_w = Weight(in_proj[:, DS - part : DS], part)
    oo_w, down_w = Weight(out_o, D), Weight(down_proj, D)
    gate_w, up_w = Weight(gate_up[:, :FF], FF), Weight(gate_up[:, FF:], FF)
    rows = gate_up.shape[0] // (lax.axis_size("ctx") // 2)
    rounds.start(
        gather_steps(idx, [qb_w, x_w, xz_w, z_w, oo_w, gate_w, up_w, down_w], rows, part // 2)
    )
    dt_task = rounds.start(ring_steps(dt_proj, layer))

    hidden = tokens[0].astype(jnp.float32)
    grad_out = cotangent[0].astype(jnp.float32)
    own_ids = doc_ids[0]
    length = hidden.shape[0]
    all_ids = along_ctx(own_ids.reshape(1, length), my_index).reshape(-1)
    first_row = my_index * length
    places = first_row + jnp.arange(length, dtype=jnp.int32)
    before = first_row - (KC - 1) + jnp.arange(KC - 1, dtype=jnp.int32)
    earlier_ids = lax.dynamic_slice_in_dim(all_ids, jnp.maximum(first_row - (KC - 1), 0), KC - 1, 0)
    earlier_ids = jnp.where(before >= 0, earlier_ids, -1)
    pad_ids = jnp.concatenate([earlier_ids, own_ids], 0)
    prev_id = jnp.where(my_index > 0, all_ids[jnp.maximum(first_row - 1, 0)], -1)
    normed_in, norm_pull = jax.vjp(normed, hidden, first_gain)
    input_low = normed_in.astype(jnp.bfloat16)
    input_low, all_ids, pad_ids, prev_id = rounds.turn((input_low, all_ids, pad_ids, prev_id))
    rounds.until_ready(qb_w)
    rounds.until(dt_task)

    qb_out = forth(idx, input_low, qb_w.ready)
    attn_in, bc_out = qb_out[:, :qkv_cols], qb_out[:, qkv_cols:]
    step_raw = project(input_low, dt_task.result)
    groups = HQ // HK
    scale = HA ** (-0.5)
    query_low = rotate(attn_in[:, : HQ * HA].reshape(length, HQ, HA), places, 1.0).astype(
        jnp.bfloat16
    )
    key_low = rotate(
        attn_in[:, HQ * HA : (HQ + HK) * HA].reshape(length, HK, HA), places, 1.0
    ).astype(jnp.bfloat16)
    value_low = attn_in[:, (HQ + HK) * HA :].astype(jnp.bfloat16)
    both_low = jnp.concatenate([key_low.reshape(length, HK * HA), value_low], 1)
    query_low, both_low, step_raw, bc_out = rounds.turn((query_low, both_low, step_raw, bc_out))
    both_task = rounds.start(along_ctx_steps(both_low, my_index))
    rounds.until_ready(x_w)
    x_out = forth(idx, input_low, x_w.ready)
    x_out = rounds.turn(x_out)
    rounds.until_ready(xz_w)
    xz_out = forth(idx, input_low, xz_w.ready)
    conv_low = jnp.concatenate([x_out, xz_out[:, : DS - part], bc_out], 1).astype(jnp.bfloat16)
    tail_low = from_behind(conv_low[length - (KC - 1) :], "ctx", 1)
    conv_low, tail_low, xz_out = rounds.turn((conv_low, tail_low, xz_out))

    def conv_fn(conv_in, tail_in, kernel_in, bias_in):
        padded = jnp.concatenate([tail_in, conv_in], 0)
        activated = jax.nn.silu(convolve(padded, pad_ids, own_ids, kernel_in, bias_in))
        states_x = activated[:, :DS].reshape(length, NH, HP)
        return (states_x, activated[:, DS : DS + NS], activated[:, DS + NS :])

    def step_fn(shift_in, bias_step, log_rate):
        step_size = jax.nn.softplus(shift_in + bias_step)
        return (step_size, -step_size * jnp.exp(log_rate))

    (states_x, b_matrix, c_matrix), conv_pull = jax.vjp(
        conv_fn, conv_low.astype(jnp.float32), tail_low.astype(jnp.float32), conv_weight, conv_bias
    )
    (step_size, log_decay), step_pull = jax.vjp(step_fn, step_raw, dt_bias, a_log)
    own_parts = (states_x, step_size, log_decay, b_matrix, c_matrix)
    y_part, y_pull = jax.vjp(lambda *parts: ssm_local(*parts, own_ids)[0], *own_parts)
    local_state, state_pull = jax.vjp(lambda *parts: ssm_local(*parts, own_ids)[1], *own_parts)
    decay_now, decay_pull = jax.vjp(lambda log_in: block_decay(log_in, own_ids, prev_id), log_decay)
    y_part, local_state, decay_now = rounds.turn((y_part, local_state, decay_now))
    state_task = rounds.start(entering_steps(decay_now, local_state, my_index, False))
    rounds.until(both_task)
    both_all = both_task.result
    query_groups = query_low.reshape(length, HK, groups, HA)
    seq_len = both_all.shape[0]
    keys_all = both_all[:, : HK * HA].reshape(seq_len, HK, HA)
    values_all = both_all[:, HK * HA :].reshape(seq_len, HK, HA)
    key_places = jnp.arange(seq_len, dtype=jnp.int32)
    allowed = (places[:, None] >= key_places[None, :]) & (own_ids[:, None] == all_ids[None, :])

    score = (
        jnp.einsum("qkgd,rkd->kgqr", query_groups, keys_all, preferred_element_type=jnp.float32)
        * scale
    )
    score = jnp.where(allowed[None, None], score, -1e30)
    new_top = jnp.maximum(-1e30, jnp.max(score, axis=-1))
    soft = jnp.where(allowed[None, None], jnp.exp(score - new_top[..., None]), 0.0)
    total = jnp.sum(soft, axis=-1)
    accum = jnp.einsum(
        "kgqr,rkd->qkgd",
        soft.astype(jnp.bfloat16),
        values_all,
        preferred_element_type=jnp.float32,
    )
    attended = accum / jnp.transpose(total, (2, 0, 1))[..., None]
    log_total = new_top + jnp.log(total)
    attended_low = attended.reshape(length, HQ * HA).astype(jnp.bfloat16)
    attended, log_total, attended_low = rounds.turn((attended, log_total, attended_low))

    rounds.until_ready(z_w)
    gate_z = jnp.concatenate(
        [xz_out[:, DS - part :], forth(idx, input_low, z_w.ready)], 1
    )
    gate_z, grad_low = rounds.turn((gate_z, grad_out.astype(jnp.bfloat16)))
    cotangent_all = every(grad_low, 0)
    rounds.until(state_task)
    rounds.until_ready(oo_w)
    state_in = state_task.result
    y_carry, carry_pull = jax.vjp(
        lambda c_in, log_in, state_arg: ssm_carry(c_in, log_in, own_ids, prev_id, state_arg),
        c_matrix,
        log_decay,
        state_in,
    )
    mixer_normed, tail_pull = jax.vjp(
        mixer_tail, y_part + y_carry, states_x, gate_z, d_skip, mixer_gain
    )
    mixer_low = mixer_normed.astype(jnp.bfloat16)

    def interleaved(mixed_in, attended_in):
        return jnp.concatenate(
            [
                mixed_in.reshape(length, layers, DS // layers),
                attended_in.reshape(length, layers, HQ * HA // layers),
            ],
            2,
        ).reshape(length, DS + HQ * HA)

    def parted(both):
        both = both.reshape(length, layers, (DS + HQ * HA) // layers)
        return (
            both[:, :, : DS // layers].reshape(length, DS),
            both[:, :, DS // layers :].reshape(length, HQ * HA),
        )

    branches_low = interleaved(mixer_low, attended_low)
    middle = hidden + forth(idx, branches_low, oo_w.ready)
    normed_mid, mid_pull = jax.vjp(normed, middle, second_gain)
    mid_low = normed_mid.astype(jnp.bfloat16)
    middle, mid_low, branches_low = rounds.turn((middle, mid_low, branches_low))
    early_deal = dealt(branches_low, input_low)
    rounds.until_ready(gate_w)
    gate_out = forth(idx, mid_low, gate_w.ready)
    gate_out = rounds.turn(gate_out)
    rounds.until_ready(up_w)
    up_out = forth(idx, mid_low, up_w.ready)
    act_value, act_pull = jax.vjp(
        lambda gate_in, up_in: jax.nn.silu(gate_in) * up_in, gate_out, up_out
    )
    act_low = act_value.astype(jnp.bfloat16)
    act_low = rounds.turn(act_low)

    rounds.until_ready(down_w)
    late_deal = dealt(act_low, mid_low)
    d_act = rounds.turn(back(idx, grad_low, down_w.ready))
    d_gate, d_up = act_pull(d_act)
    gate_low, up_low = d_gate.astype(jnp.bfloat16), d_up.astype(jnp.bfloat16)
    gate_low, up_low = rounds.turn((gate_low, up_low))
    gate_all, up_all = every(gate_low, 3), every(up_low, 5)
    shard_rows = mid_low.shape[1] // layers

    down_grad = weight_grad(
        [(late_deal, 0, cotangent_all)],
        lambda pair: finished(idx, [pair], [(0, 0, D)]),
    )
    gate_up_grad = weight_grad(
        [(late_deal, 1, gate_all), (late_deal, 1, up_all)],
        lambda pair: finished(idx, [pair], [(0, 0, 2 * FF)]),
        down_grad,
    )
    d_mid_norm = back(idx, gate_low, gate_w.ready)
    d_mid_norm = rounds.turn(d_mid_norm)
    d_mid_norm = d_mid_norm + back(idx, up_low, up_w.ready)
    d_middle_part, d_second_gain = mid_pull(d_mid_norm)
    d_middle = grad_out + d_middle_part
    branch_low = d_middle.astype(jnp.bfloat16)
    branch_low, d_middle = rounds.turn((branch_low, d_middle))
    branch_all = every(branch_low, 5)
    d_mixer_norm, d_attended = parted(back(idx, branch_low, oo_w.ready))
    d_mixer_norm, d_attended = rounds.turn((d_mixer_norm, d_attended))
    d_core, d_states_tail, d_gate_z, d_d_skip, d_mixer_gain = tail_pull(d_mixer_norm)
    z_low = d_gate_z.astype(jnp.bfloat16)
    z_low, d_core, d_states_tail = rounds.turn((z_low, d_core, d_states_tail))
    z_all = every(z_low, 6)
    fine = HQ * HA // layers
    cases = [
        (at % (shard_rows // fine), at // (shard_rows // fine) * D, (at // (shard_rows // fine) + 1) * D)
        for at in range((DS + HQ * HA) // layers // fine)
    ]
    oo_z_grad = weight_grad(
        [(early_deal, 0, branch_all), (early_deal, 1, z_all)],
        lambda pair: (
            pair,
            finished_rows(idx, pair, cases[: DS // layers // fine], fine),
            finished_rows(idx, pair, cases[DS // layers // fine :], fine),
        ),
        gate_up_grad,
    )
    d_c_carry, d_log_carry, d_state_in = carry_pull(d_core)
    mixed = middle + forth(idx, act_low, down_w.ready)
    d_c_carry, d_log_carry, d_state_in, mixed = rounds.turn(
        (d_c_carry, d_log_carry, d_state_in, mixed)
    )
    later_task = rounds.start(entering_steps(decay_now, d_state_in, my_index, True))
    d_out_low = d_attended.reshape(length, HK, groups, HA).astype(jnp.bfloat16)
    delta = jnp.transpose(jnp.sum(d_out_low.astype(jnp.float32) * attended, axis=-1), (1, 2, 0))
    score = (
        jnp.einsum("qkgd,rkd->kgqr", query_groups, keys_all, preferred_element_type=jnp.float32)
        * scale
    )
    prob = jnp.where(
        allowed[None, None],
        jnp.exp(jnp.where(allowed[None, None], score, 0.0) - log_total[..., None]),
        0.0,
    )
    d_prob = jnp.einsum(
        "qkgd,rkd->kgqr", d_out_low, values_all, preferred_element_type=jnp.float32
    )
    score_grad = (prob * (d_prob - delta[..., None])).astype(jnp.bfloat16)
    d_query = (
        jnp.einsum("kgqr,rkd->qkgd", score_grad, keys_all, preferred_element_type=jnp.float32)
        * scale
    )
    d_keys = (
        jnp.einsum("kgqr,qkgd->rkd", score_grad, query_groups, preferred_element_type=jnp.float32)
        * scale
    )
    d_values = jnp.einsum(
        "kgqr,qkgd->rkd", prob.astype(jnp.bfloat16), d_out_low, preferred_element_type=jnp.float32
    )
    kv_terms = jnp.concatenate(
        [d_keys.reshape(seq_len, HK * HA), d_values.reshape(seq_len, HK * HA)], 1
    ).astype(jnp.bfloat16)
    kv_terms, d_query = rounds.turn((kv_terms, d_query))
    kv_task = rounds.start(sum_rows_steps(kv_terms, my_index))
    y_grads = rounds.turn(y_pull(d_core))
    rounds.until(later_task)
    later_grad = later_task.result
    state_grads = rounds.turn(state_pull(later_grad))
    d_decay = jnp.sum(later_grad * state_in, axis=(1, 2))
    d_log_decay = decay_pull(d_decay)[0]
    d_states, d_step, d_log, d_b, d_c = jax.tree.map(jnp.add, y_grads, state_grads)
    d_conv_in, d_tail, d_conv_weight, d_conv_bias = conv_pull(
        (d_states + d_states_tail, d_b, d_c + d_c_carry)
    )
    d_step_raw, d_dt_bias, d_a_log = step_pull((d_step, d_log + d_log_carry + d_log_decay))
    d_conv_in, d_tail, d_step_raw = rounds.turn((d_conv_in, d_tail, d_step_raw))
    rounds.until(kv_task)
    d_kv = kv_task.result.astype(jnp.float32)
    qkv_low = jnp.concatenate(
        [
            rotate(d_query.reshape(length, HQ, HA), places, -1.0).reshape(length, HQ * HA),
            rotate(d_kv[:, : HK * HA].reshape(length, HK, HA), places, -1.0).reshape(
                length, HK * HA
            ),
            d_kv[:, HK * HA :],
        ],
        1,
    ).astype(jnp.bfloat16)
    from_next = from_behind(d_tail.astype(jnp.bfloat16), "ctx", -1).astype(d_tail.dtype)
    d_conv_in = jnp.concatenate(
        [d_conv_in[: length - (KC - 1)], d_conv_in[length - (KC - 1) :] + from_next], 0
    )
    conv_grad_low = d_conv_in.astype(jnp.bfloat16)
    step_low = d_step_raw.astype(jnp.bfloat16)
    blank = jnp.zeros((length, 512 - NH), jnp.bfloat16)
    tail_low = jnp.concatenate([conv_grad_low, step_low, blank[:, : 256 - NH], qkv_low], 1)
    conv_grad_low, step_low, qkv_low, tail_low = rounds.turn(
        (conv_grad_low, step_low, qkv_low, tail_low)
    )
    tail_grad = weight_grad(
        [(early_deal, 1, every(tail_low, 4))], lambda pair: pair
    )
    d_normed_in = (
        back(idx, conv_grad_low[:, :part], x_w.ready)
        + back(
            idx,
            jnp.concatenate([conv_grad_low[:, part:DS], z_low[:, : DS - part]], 1),
            xz_w.ready,
        )
    )
    d_normed_in = rounds.turn(d_normed_in)
    d_normed_in = (
        d_normed_in
        + back(idx, z_low[:, DS - part :], z_w.ready)
        + back(idx, jnp.concatenate([qkv_low, conv_grad_low[:, DS:]], 1), qb_w.ready)
        + project_back(step_low, dt_task.result)
    )
    d_hidden_part, d_first_gain = norm_pull(d_normed_in)
    d_tokens = d_middle + d_hidden_part
    d_tokens, d_first_gain = rounds.turn((d_tokens, d_first_gain))
    smalls_task = rounds.start(
        sum_steps(
            (
                d_conv_weight,
                d_conv_bias,
                d_dt_bias,
                d_a_log,
                d_d_skip,
                d_mixer_gain,
                d_first_gain,
                d_second_gain,
            )
        )
    )
    rounds.until(smalls_task, gate_up_grad, down_grad, oo_z_grad, tail_grad)
    smalls = smalls_task.result
    tail_pair, (oo_z_pair, out_grad, o_grad) = tail_grad.result, oo_z_grad.result
    z_first = branches_low.shape[1] // layers // shard_rows * D
    tail_half = tail_pair[0].shape[1]
    step_grad = jnp.where(core == 1, tail_pair[0], tail_pair[1])
    return (
        mixed[None].astype(jnp.bfloat16),
        d_tokens[None],
        finished(idx, [oo_z_pair, tail_pair], [(0, z_first, z_first + DS), (1, 0, conv_cols)]),
        step_grad[:, conv_cols - tail_half : conv_cols - tail_half + NH].astype(jnp.float32),
        smalls[0],
        smalls[1],
        smalls[2],
        smalls[3],
        smalls[4],
        smalls[5],
        out_grad,
        finished(idx, [tail_pair], [(0, conv_cols + 256, conv_cols + 256 + qkv_cols)]),
        o_grad,
        smalls[6],
        smalls[7],
        gate_up_grad.result,
        down_grad.result,
    )


def solution(mesh):
    return jax.shard_map(
        body,
        mesh=mesh,
        in_specs=(
            P("fsdp", "ctx", None),
            P("fsdp", "ctx", None),
            P("fsdp", "ctx"),
            P("fsdp", None),
            P("fsdp", None),
            P(),
            P(),
            P(),
            P(),
            P(),
            P(),
            P("fsdp", None),
            P("fsdp", None),
            P("fsdp", None),
            P(),
            P(),
            P("fsdp", None),
            P("fsdp", None),
        ),
        out_specs=(
            P("fsdp", "ctx", None),
            P("fsdp", "ctx", None),
            P("fsdp", None),
            P("fsdp", None),
            P(),
            P(),
            P(),
            P(),
            P(),
            P(),
            P("fsdp", None),
            P("fsdp", None),
            P("fsdp", None),
            P(),
            P(),
            P("fsdp", None),
            P("fsdp", None),
        ),
        check_vma=False,
    )
```

```python
import jax
import jax.numpy as jnp
from jax import lax
from jax.experimental import pallas as pl
from jax.experimental.pallas import tpu as pltpu
from jax.sharding import PartitionSpec as P

D = 2048
FF = 4096
NH = 48
HP = 64
NS = 256
KC = 4
HQ = 8
HK = 2
HA = 128
DS = 3072


HIGH = lax.Precision.HIGHEST
epsilon = 1e-05
rope_base = 100000000000.0


def from_behind(block, axis, distance):
    devices = range(lax.axis_size(axis))
    route = [(i - distance, i) for i in devices if i - distance in devices]
    return lax.ppermute(block, axis, route)


def normed(operand, gain_vec):
    return (
        operand
        * lax.rsqrt(jnp.mean(operand * operand, axis=-1, keepdims=True) + epsilon)
        * gain_vec
    )


def rotate(operand, places, direction):
    half_width = operand.shape[-1] // 2
    frequency = rope_base ** (
        -jnp.arange(half_width, dtype=jnp.float32) * (2.0 / operand.shape[-1])
    )
    angles = places.astype(jnp.float32)[:, None] * frequency[None, :]
    cosine = jnp.cos(angles)[:, None, :]
    sine_part = direction * jnp.sin(angles)[:, None, :]
    first_half = operand[..., :half_width]
    second_half = operand[..., half_width:]
    return jnp.concatenate(
        [
            first_half * cosine - second_half * sine_part,
            second_half * cosine + first_half * sine_part,
        ],
        -1,
    )


def project(left_side, right_side):
    return jnp.dot(left_side, right_side, preferred_element_type=jnp.float32)


def project_back(grad_in, weight):
    return lax.dot_general(
        grad_in, weight, (((1,), (1,)), ((), ())), preferred_element_type=jnp.float32
    )


def convolve(padded, pad_ids, row_ids, kernel_in, bias_in):
    length = row_ids.shape[0]
    total = jnp.zeros((length, padded.shape[1]), jnp.float32) + bias_in[None, :]
    for offset in range(KC):
        same_doc = (pad_ids[offset : offset + length] == row_ids).astype(jnp.float32)
        total = (
            total
            + kernel_in[offset][None, :] * padded[offset : offset + length] * same_doc[:, None]
        )
    return total


def ssm_local(states_x, step_size, log_decay, b_matrix, c_matrix, row_ids):
    length = states_x.shape[0]
    running = jnp.cumsum(log_decay, axis=0)
    places = jnp.arange(length, dtype=jnp.int32)
    allowed = (places[:, None] >= places[None, :]) & (row_ids[:, None] == row_ids[None, :])
    spread = running.T[:, :, None] - running.T[:, None, :]
    decay_matrix = jnp.where(allowed[None], jnp.exp(jnp.where(allowed[None], spread, 0.0)), 0.0)
    intersection = jnp.dot(c_matrix, b_matrix.T, precision=HIGH, preferred_element_type=jnp.float32)
    driven = step_size[:, :, None] * states_x
    y_part = jnp.einsum("hts,shp->thp", decay_matrix * intersection[None], driven, precision=HIGH)
    to_end = jnp.where(
        (row_ids == row_ids[-1])[:, None], jnp.exp(running[-1][None, :] - running), 0.0
    )
    local_state = jnp.einsum("sh,shp,sn->hpn", to_end, driven, b_matrix, precision=HIGH)
    return (y_part, local_state)


def ssm_carry(c_matrix, log_decay, row_ids, prev_id, state_in):
    kept_mask = (row_ids == prev_id).astype(jnp.float32)
    weight = jnp.exp(jnp.cumsum(log_decay, axis=0)) * kept_mask[:, None]
    return weight[:, :, None] * jnp.einsum("hpn,tn->thp", state_in, c_matrix, precision=HIGH)


def block_decay(log_decay, row_ids, prev_id):
    return jnp.exp(jnp.sum(log_decay, axis=0)) * (row_ids[-1] == prev_id).astype(jnp.float32)


def mixer_tail(core_in, states_x, gate_z, skip_in, gain_in):
    length = core_in.shape[0]
    core = core_in + skip_in[None, :, None] * states_x
    gated = core.reshape(length, DS) * jax.nn.silu(gate_z)
    return normed(gated, gain_in)


def swiglu(gate_up_out):
    return jax.nn.silu(gate_up_out[:, :FF]) * gate_up_out[:, FF:]


def swap(block, distance):
    peers = lax.axis_size("ctx")
    return lax.ppermute(block, "ctx", [(i, i ^ distance) for i in range(peers)])


def shifted(block, hops):
    peers = lax.axis_size("fsdp")
    return lax.ppermute(block, "fsdp", [(i, (i + hops) % peers) for i in range(peers)])


def powers(first, limit):
    found = []
    while first < limit:
        found.append(first)
        first *= 2
    return found


def chip_steps():
    return powers(2, lax.axis_size("ctx"))


def ordered(flag, first, second, axis):
    return jnp.where(
        flag,
        jnp.concatenate([second, first], axis),
        jnp.concatenate([first, second], axis),
    )


def halves(flag, array, axis):
    size = array.shape[axis] // 2
    low = lax.slice_in_dim(array, 0, size, axis=axis)
    high = lax.slice_in_dim(array, size, 2 * size, axis=axis)
    return (jnp.where(flag, high, low), jnp.where(flag, low, high))


def join(earlier, later):
    return (earlier[0] * later[0], later[0][:, None, None] * earlier[1] + later[1])


def either(flag, when, otherwise):
    return jax.tree.map(lambda a, b: jnp.where(flag, a, b), when, otherwise)


class Last:
    def __init__(self, value):
        self.value = value


class Task:
    def __init__(self, steps):
        self.steps, self.ready, self.result = steps, None, None


class Rounds:
    def __init__(self):
        self.tasks = []

    def start(self, steps):
        self.tasks.append(Task(steps))
        return self.tasks[-1]

    def turn(self, values=()):
        found = []
        for task in self.tasks:
            try:
                found.append(task.steps.send(task.ready))
            except StopIteration:
                found.append(Last(()))
        held = [step.value if isinstance(step, Last) else step for step in found]
        values, held = lax.optimization_barrier((values, held))
        going = []
        for task, step, ready in zip(self.tasks, found, held, strict=True):
            task.ready = ready
            if isinstance(step, Last):
                task.result = ready
            else:
                going.append(task)
        self.tasks = going
        return values

    def until(self, *tasks):
        while any(task.result is None for task in tasks):
            self.turn()

    def until_ready(self, *weights):
        while any(weight.ready is None for weight in weights):
            self.turn()


def entering_steps(decay, state, place, backwards):
    def sent(pair, step):
        return (swap(pair[0], step), swap(pair[1].astype(jnp.bfloat16), step))

    def read(pair):
        return (pair[0], pair[1].astype(jnp.float32))

    def is_later(step):
        return (jnp.bitwise_and(place, step) != 0) != backwards

    core = jnp.bitwise_and(place, 1) == 1
    near = read(sent((decay, state), 1))
    total = either(is_later(1), join(near, (decay, state)), join((decay, state), near))
    total = tuple(halves(core, part, 0)[0] for part in total)
    before = (jnp.ones_like(total[0]), jnp.zeros_like(total[1]))
    steps = chip_steps()
    for step in steps:
        there = read(sent(total, step))
        before = either(is_later(step), join(there, before), before)
        if step != steps[-1]:
            total = either(is_later(step), join(there, total), join(total, there))
            total, before, near = yield total, before, near
    across = swap(before[1].astype(jnp.bfloat16), 1).astype(jnp.float32)
    whole = ordered(core, before[1], across, 0)
    yield Last(jnp.where(is_later(1), near[0][:, None, None] * whole + near[1], whole))


class Weight:
    def __init__(self, shard, width):
        self.shard, self.width, self.chunks, self.ready = shard, width, [], None

    def cuts(self, idx, rows, columns):
        chip, core = idx[0], idx[1]
        per = rows * (lax.axis_size("ctx") // 2)
        for first_row in range(0, self.shard.shape[0], per):
            for first_col in range(0, self.width // 2, columns):
                piece = lax.dynamic_slice(
                    self.shard,
                    (first_row + chip * rows, first_col + core * (self.width // 2)),
                    (rows, columns),
                )
                self.chunks.append((first_row, first_col, []))
                yield piece, self.chunks[-1][2]


class Box:
    def __init__(self, value):
        self.value = value


def copy_all(copies):
    for copy in copies:
        copy.start()
    for copy in copies:
        copy.wait()


def place_kernel(chunks, idx_ref, shard_ref, *refs):
    whole_ref, sems = refs[-2], refs[-1]
    chip, core, layer = idx_ref[0], idx_ref[1], idx_ref[2]
    depth, width = shard_ref.shape[0], whole_ref.shape[1]
    layers = whole_ref.shape[0] // depth
    copies = [
        pltpu.make_async_copy(
            shard_ref.at[:, pl.ds(pl.multiple_of(core * width, 128), width)],
            whole_ref.at[pl.ds(pl.multiple_of(layer * depth, depth), depth), :],
            sems.at[0],
        )
    ]
    for first_row, first_col, found in chunks:
        for side, others, source, first in found:
            rows, columns = refs[source].shape[1:]
            for number, other in enumerate(others):
                for hop in range(layers - 1):
                    owner = lax.rem(layer + 1 + hop, layers)
                    begin = owner * depth + first_row + jnp.bitwise_xor(chip, other) * rows
                    copies.append(
                        pltpu.make_async_copy(
                            refs[source].at[first + number * (layers - 1) + hop],
                            whole_ref.at[
                                pl.ds(pl.multiple_of(begin, rows), rows),
                                pl.ds(first_col + side * columns, columns),
                            ],
                            sems.at[len(copies)],
                        )
                    )
    copy_all(copies)


def placed(idx, weight):
    layers = lax.axis_size("fsdp")
    depth, width = weight.shard.shape[0], weight.width // 2
    boxes = list({id(box): box for _, _, found in weight.chunks for _, _, box, _ in found}.values())
    chunks = [
        (
            first_row,
            first_col,
            [(side, others, boxes.index(box), first) for side, others, box, first in found],
        )
        for first_row, first_col, found in weight.chunks
    ]
    count = 1 + sum(
        (layers - 1) * len(others) for _, _, found in chunks for _, others, _, _ in found
    )
    return pl.pallas_call(
        lambda *refs: place_kernel(chunks, *refs),
        out_shape=jax.ShapeDtypeStruct((layers * depth, width), weight.shard.dtype),
        in_specs=[pl.BlockSpec(memory_space=pltpu.SMEM)]
        + [pl.BlockSpec(memory_space=pl.ANY)] * (1 + len(boxes)),
        out_specs=pl.BlockSpec(memory_space=pltpu.VMEM),
        scratch_shapes=[pltpu.SemaphoreType.DMA((count,))],
        compiler_params=pltpu.CompilerParams(vmem_limit_bytes=56 * 1024 * 1024),
        cost_estimate=pl.CostEstimate(flops=1024, bytes_accessed=1024, transcendentals=0),
        name="place",
    )(idx, weight.shard, *[box.value for box in boxes])


def pack_kernel(fresh, plan, inputs, idx_ref, *refs):
    layer = idx_ref[2]
    outs, sems = refs[inputs:-1], refs[-1]
    copies = []
    for out, first, side in fresh:
        layers, columns = refs[0].shape[0], outs[out].shape[2]
        for hop in range(layers - 1):
            owner = lax.rem(layer + 1 + hop, layers)
            copies.append(
                pltpu.make_async_copy(
                    refs[0].at[owner, :, pl.ds(side * columns, columns)],
                    outs[out].at[first + hop],
                    sems.at[len(copies)],
                )
            )
    for out, first, source, begin, size in plan:
        copies.append(
            pltpu.make_async_copy(
                refs[source].at[pl.ds(begin, size)],
                outs[out].at[pl.ds(first, size)],
                sems.at[len(copies)],
            )
        )
    copy_all(copies)


def packed(idx, along, fresh, plan, sizes, rows, columns):
    boxes = list({id(entry[2]): entry[2] for entry in plan}.values())
    arrays = ([] if along is None else [along]) + [box.value for box in boxes]
    skip = len(arrays) - len(boxes)
    plan = [(out, row, skip + boxes.index(box), begin, size) for out, row, box, begin, size in plan]
    count = len(fresh) * (lax.axis_size("fsdp") - 1) + len(plan)
    return pl.pallas_call(
        lambda *refs: pack_kernel(fresh, plan, len(arrays), *refs),
        out_shape=[jax.ShapeDtypeStruct((size, rows, columns), jnp.bfloat16) for size in sizes],
        in_specs=[pl.BlockSpec(memory_space=pltpu.SMEM)]
        + [pl.BlockSpec(memory_space=pl.ANY)] * len(arrays),
        out_specs=[pl.BlockSpec(memory_space=pltpu.VMEM)] * len(sizes),
        scratch_shapes=[pltpu.SemaphoreType.DMA((count,))],
        compiler_params=pltpu.CompilerParams(vmem_limit_bytes=56 * 1024 * 1024),
        cost_estimate=pl.CostEstimate(flops=1024, bytes_accessed=1024, transcendentals=0),
        name="pack",
    )(idx, *arrays)


def whole_steps(piece, turns, wait):
    for _ in range(turns):
        piece = yield piece
    whole = lax.all_gather(piece, ("fsdp", "ctx"), axis=0, tiled=True)
    for _ in range(wait):
        yield ()
    yield Last(whole)


def gather_steps(idx, weights, rows, columns):
    steps, layers = chip_steps(), lax.axis_size("fsdp")
    half, near = columns // 2, layers - 1
    pieces, sinks, owners = [], [], []
    for weight in weights:
        for piece, sink in weight.cuts(idx, rows, columns):
            pieces.append(piece)
            sinks.append(sink)
            owners.append(weight)
    along, halved = {}, []
    for turn in range(len(pieces) + len(steps) + 3):
        if turn < len(pieces):
            along[turn] = lax.all_gather(pieces[turn], "fsdp")
        fresh, plan, sizes, comes = [], [], {step: 0 for step in steps}, []
        used = []
        for stage in range(len(steps)):
            at = turn - 1 - stage
            if not 0 <= at < len(pieces):
                continue
            for side in range(2):
                step = (steps[side:] + steps[:side])[stage]
                out = steps.index(step)
                first = sizes[step]
                reached = []
                if stage == 0:
                    fresh.append((out, first, side))
                    used.append((at, side, [0], step, first))
                    reached, sizes[step] = [0], first + near
                for _, others, box, begin in [e for e in sinks[at] if e[0] == side]:
                    plan.append((out, sizes[step], box, begin, near * len(others)))
                    sizes[step] += near * len(others)
                    reached = reached + others
                comes.append((at, side, [other ^ (step // 2) for other in reached], step, first))
        active = [step for step in steps if sizes[step]]
        blocks = {}
        if active:
            rank = {steps.index(step): number for number, step in enumerate(active)}
            made = packed(
                idx,
                along.pop(turn - 1, None) if fresh else None,
                [(rank[out], first, side) for out, first, side in fresh],
                [(rank[out], *rest) for out, *rest in plan],
                [sizes[step] for step in active],
                rows,
                half,
            )
            blocks = dict(zip(active, made, strict=True))
        blocks, pieces = lax.optimization_barrier((blocks, pieces))
        got = {step: swap(block, step) for step, block in blocks.items()}
        whole = [
            weight
            for at, weight in enumerate(owners)
            if at == turn - 1 - len(steps) and weight not in owners[at + 1 :]
        ]
        ready = [(weight, mine, swap(mine, 1)) for weight, mine in halved]
        halved = [(weight, placed(idx, weight)) for weight in whole]
        for weight in whole:
            for sink, owner in zip(sinks, owners, strict=True):
                if owner is weight:
                    sink.clear()
        kept = {step: Box(block) for step, block in blocks.items()}
        sent = {step: Box(block) for step, block in got.items()}
        flying = list(sent.values())
        for at, side, others, step, first in used:
            sinks[at].append((side, others, kept[step], first))
        for at, side, others, step, first in comes:
            sinks[at].append((side, others, sent[step], first))
        now_ready = [weight for weight, _, _ in ready]
        for weight, mine, other in ready:
            weight.ready = (mine, other)
        late, pieces, now, ready, mines = yield (
            [box.value for box in flying],
            pieces,
            {turn: along[turn]} if turn in along else {},
            [(mine, other) for _, mine, other in ready],
            [mine for _, mine in halved],
        )
        for box, value in zip(flying, late, strict=True):
            box.value = value
        along.update(now)
        for weight, pair in zip(now_ready, ready, strict=True):
            weight.ready = pair
        halved = [(weight, mine) for (weight, _), mine in zip(halved, mines, strict=True)]


def ring_steps(block, layer):
    peers, length = lax.axis_size("fsdp"), block.shape[0]
    found = [block]
    for _ in range(peers - 1):
        found.append((yield shifted(found[-1], 1)))
    ahead = found[:1] + found[:0:-1]
    twice = jnp.concatenate(ahead + ahead, 0)
    whole = lax.dynamic_slice_in_dim(
        twice, lax.rem(peers - layer, peers) * length, peers * length, 0
    )
    yield Last(whole)


def deal_steps(arrays, layer):
    peers = lax.axis_size("fsdp")
    widths = [array.shape[1] // peers for array in arrays]

    def cut(hops):
        to = lax.rem(layer + hops, peers)
        return jnp.concatenate(
            [
                lax.dynamic_slice_in_dim(array, to * width, width, 1)
                for array, width in zip(arrays, widths, strict=True)
            ],
            1,
        )

    ahead = [cut(0)]
    for hops in range(1, peers):
        ahead.append((yield shifted(cut(peers - hops), peers - hops)))
    whole = jnp.concatenate(
        [lax.select_n(lax.rem(at + peers - layer, peers), *ahead) for at in range(peers)], 0
    )
    found, at = [], 0
    for width in widths:
        found.append(whole[:, at : at + width])
        at += width
    yield Last(found)


def every_steps(block, wait):
    found = lax.all_gather(block, "fsdp", axis=0, tiled=True)
    for _ in range(wait):
        yield ()
    yield Last(found)


def added(left_side, right_side):
    return (left_side.astype(jnp.float32) + right_side.astype(jnp.float32)).astype(jnp.bfloat16)


def weight_steps(products, place, finish, after):
    steps, core = chip_steps(), jnp.bitwise_and(place, 1) == 1
    while any(task.result is None for act, _, grad in products for task in (act, grad)) or any(
        task.result is None for task in after
    ):
        yield ()
    rows = min(act.result[which].shape[1] for act, which, _ in products)
    parts = []
    for act, which, grad in products:
        array = act.result[which]
        for first in range(0, array.shape[1], rows):
            parts.append(
                lax.dot_general(
                    array[:, first : first + rows],
                    grad.result,
                    (((0,), (0,)), ((), ())),
                    preferred_element_type=jnp.float32,
                ).astype(jnp.bfloat16)
            )
    part = jnp.concatenate(parts, 1) if len(parts) > 1 else parts[0]
    own, other = halves(core, part, 1)
    own = added(own, swap(other, 1))
    size = own.shape[0] // 2
    blocks = [own[:size], own[size:]]
    orders = [steps[side:] + steps[:side] for side in range(2)]
    moves = [(stage, True) for stage in range(len(steps))]
    moves += [(stage, False) for stage in range(len(steps))[::-1]]
    for number, (stage, adds) in enumerate(moves):
        for side in range(2):
            step = orders[side][stage]
            flag = jnp.bitwise_and(place, step) != 0
            if adds:
                keep, send = halves(flag, blocks[side], 0)
                blocks[side] = added(keep, swap(send, step))
            else:
                blocks[side] = ordered(flag, blocks[side], swap(blocks[side], step), 0)
        if number % 2 == 0:
            blocks = list((yield blocks))
    own = jnp.concatenate(blocks, 0)
    pair = yield own, swap(own, 1)
    yield Last(finish(pair))


def finish_kernel(segments, idx_ref, *refs):
    out_ref = refs[-1]
    for flag in (0, 1):

        @pl.when(idx_ref[1] == flag)
        def _():
            at = 0
            for number, first, last in segments:
                pair = refs[2 * number : 2 * number + 2]
                half = pair[0].shape[1]
                for part, begin, end in (
                    (pair[flag], first, min(last, half)),
                    (pair[1 - flag], max(first, half) - half, last - half),
                ):
                    if begin < end:
                        out_ref[:, at : at + end - begin] = part[:, begin:end].astype(jnp.float32)
                        at += end - begin


def finished(idx, pairs, segments, first_row=0, rows=None):
    rows = rows or pairs[0][0].shape[0]
    width = sum(last - first for _, first, last in segments)
    block = 32
    while block < 256 and rows % (2 * block) == 0 and first_row % (2 * block) == 0:
        block *= 2
    while block > 32 and block * width > 1024 * 1024:
        block //= 2
    skip = first_row // block
    flat = [part for pair in pairs for part in pair]
    return pl.pallas_call(
        lambda *refs: finish_kernel(segments, *refs),
        grid=(rows // block,),
        out_shape=jax.ShapeDtypeStruct((rows, width), jnp.float32),
        in_specs=[pl.BlockSpec(memory_space=pltpu.SMEM)]
        + [pl.BlockSpec((block, part.shape[1]), lambda i: (i + skip, 0)) for part in flat],
        out_specs=pl.BlockSpec((block, width), lambda i: (i, 0)),
        compiler_params=pltpu.CompilerParams(vmem_limit_bytes=56 * 1024 * 1024),
        cost_estimate=pl.CostEstimate(flops=1024, bytes_accessed=1024, transcendentals=0),
        name="finish",
    )(idx, *flat)


def finish_steps(task, wait, finish, after):
    while task.result is None or after.result is None:
        yield ()
    for _ in range(wait):
        yield ()
    yield Last(finish(task.result))


def rows_kernel(cases, idx_ref, low_ref, high_ref, out_ref):
    half = low_ref.shape[1]
    for number, (_, first, last) in enumerate(cases):
        for flag in (0, 1):
            low, high = (low_ref, high_ref) if flag == 0 else (high_ref, low_ref)

            @pl.when((pl.program_id(0) == number) & (idx_ref[1] == flag))
            def _():
                at = 0
                for part, begin, end in (
                    (low, first, min(last, half)),
                    (high, max(first, half) - half, last - half),
                ):
                    if begin < end:
                        out_ref[:, at : at + end - begin] = part[:, begin:end].astype(jnp.float32)
                        at += end - begin


def finished_rows(idx, pair, cases, rows):
    width, numbers = cases[0][2] - cases[0][1], [number for number, _, _ in cases]

    def place(i, idx):
        return (sum((i == at) * number for at, number in enumerate(numbers)), 0)

    return pl.pallas_call(
        lambda *refs: rows_kernel(cases, *refs),
        grid_spec=pltpu.PrefetchScalarGridSpec(
            num_scalar_prefetch=1,
            grid=(len(cases),),
            in_specs=[pl.BlockSpec((rows, part.shape[1]), place) for part in pair],
            out_specs=pl.BlockSpec((rows, width), lambda i, idx: (i, 0)),
        ),
        out_shape=jax.ShapeDtypeStruct((len(cases) * rows, width), jnp.float32),
        compiler_params=pltpu.CompilerParams(vmem_limit_bytes=56 * 1024 * 1024),
        cost_estimate=pl.CostEstimate(flops=1024, bytes_accessed=1024, transcendentals=0),
        name="finish_rows",
    )(idx, *pair)


def along_ctx(block, place):
    for step in powers(1, lax.axis_size("ctx")):
        block = ordered(jnp.bitwise_and(place, step) != 0, block, swap(block, step), 0)
    return block


def along_ctx_steps(block, place):
    for step in powers(1, lax.axis_size("ctx")):
        got = yield swap(block, step)
        block = ordered(jnp.bitwise_and(place, step) != 0, block, got, 0)
    yield Last(block)


def sum_rows_steps(block, place):
    for step in powers(1, lax.axis_size("ctx"))[::-1]:
        keep, send = halves(jnp.bitwise_and(place, step) != 0, block, 0)
        got, keep = yield swap(send, step), keep
        block = added(keep, got)
    yield Last(block)


def summed_rows(block, place):
    for step in powers(1, lax.axis_size("ctx"))[::-1]:
        keep, send = halves(jnp.bitwise_and(place, step) != 0, block, 0)
        block = added(keep, swap(send, step))
    return block


def forth_kernel(idx_ref, left_ref, own_ref, other_ref, out_ref):
    width = own_ref.shape[1]
    for part_ref, half in ((own_ref, idx_ref[1]), (other_ref, 1 - idx_ref[1])):
        columns = pl.ds(pl.multiple_of(half * width, 128), width)
        term = jnp.dot(left_ref[...], part_ref[...], preferred_element_type=jnp.float32)

        @pl.when(pl.program_id(0) == 0)
        def _():
            out_ref[:, columns] = term

        @pl.when(pl.program_id(0) != 0)
        def _():
            out_ref[:, columns] += term


def back_kernel(idx_ref, grad_ref, own_ref, other_ref, out_ref):
    width, total = own_ref.shape[1], None
    for part_ref, half in ((own_ref, idx_ref[1]), (other_ref, 1 - idx_ref[1])):
        term = lax.dot_general(
            grad_ref[:, pl.ds(pl.multiple_of(half * width, 128), width)],
            part_ref[...],
            (((1,), (1,)), ((), ())),
            preferred_element_type=jnp.float32,
        )
        total = term if total is None else total + term
    out_ref[...] = total


def product(kernel, name, idx, operand, chunk, in_spec, out_spec, columns):
    rows, (depth, width) = operand.shape[0], chunk[0].shape
    part = pl.BlockSpec((depth // 4, width), lambda t, idx: (t, 0))
    return pl.pallas_call(
        kernel,
        grid_spec=pltpu.PrefetchScalarGridSpec(
            num_scalar_prefetch=1, grid=(4,), in_specs=[in_spec, part, part], out_specs=out_spec
        ),
        out_shape=jax.ShapeDtypeStruct((rows, columns), jnp.float32),
        compiler_params=pltpu.CompilerParams(vmem_limit_bytes=56 * 1024 * 1024),
        cost_estimate=pl.CostEstimate(flops=1024, bytes_accessed=1024, transcendentals=0),
        name=name,
    )(idx, operand, *chunk)


def forth(idx, left_side, chunk):
    rows, (depth, width) = left_side.shape[0], chunk[0].shape
    in_spec = pl.BlockSpec((rows, depth // 4), lambda t, idx: (0, t))
    out_spec = pl.BlockSpec((rows, 2 * width), lambda t, idx: (0, 0))
    return product(forth_kernel, "forth", idx, left_side, chunk, in_spec, out_spec, 2 * width)


def back(idx, grad_in, chunk):
    rows, (depth, width) = grad_in.shape[0], chunk[0].shape
    in_spec = pl.BlockSpec((rows, 2 * width), lambda t, idx: (0, 0))
    out_spec = pl.BlockSpec((rows, depth // 4), lambda t, idx: (0, t))
    return product(back_kernel, "back", idx, grad_in, chunk, in_spec, out_spec, depth)


def sum_steps(arrays):
    flat = jnp.concatenate([array.reshape(-1) for array in arrays])
    size = flat.shape[0]
    flat = jnp.pad(flat, (0, -size % 1024)).reshape(-1, 128)
    for axis in ("ctx", "fsdp"):
        peers = lax.axis_size(axis)
        for step in powers(1, peers):
            flat = yield flat + lax.ppermute(flat, axis, [(i, i ^ step) for i in range(peers)])
    flat, found, at = flat.reshape(-1), [], 0
    for array in arrays:
        found.append(flat[at : at + array.size].reshape(array.shape))
        at += array.size
    yield Last(found)


def body(
    tokens,
    cotangent,
    doc_ids,
    in_proj,
    dt_proj,
    conv_weight,
    conv_bias,
    dt_bias,
    a_log,
    d_skip,
    mixer_gain,
    out_proj,
    qkv_proj,
    o_proj,
    first_gain,
    second_gain,
    gate_up,
    down_proj,
):
    my_index, layer = lax.axis_index("ctx"), lax.axis_index("fsdp")
    layers = lax.axis_size("fsdp")
    core, chip = jnp.bitwise_and(my_index, 1), my_index // 2
    idx = jnp.stack([chip, core, layer]).astype(jnp.int32)
    conv_cols, qkv_cols = DS + 2 * NS, (HQ + 2 * HK) * HA
    kv_bc = jnp.concatenate([qkv_proj, in_proj[:, 2 * DS :]], 1)
    z_x = in_proj[:, : 2 * DS]
    out_o = jnp.concatenate([out_proj, o_proj], 0)
    rounds = Rounds()

    def dealt(*arrays):
        return rounds.start(deal_steps(arrays, layer))

    def every(block, wait):
        return rounds.start(every_steps(block, wait))

    def weight_grad(products, finish, *after):
        return rounds.start(weight_steps(products, my_index, finish, list(after)))

    part = 2048
    qb_w = Weight(kv_bc, part)
    x_w = Weight(in_proj[:, DS : DS + part], part)
    xz_w = Weight(
        jnp.concatenate([in_proj[:, DS + part : 2 * DS], in_proj[:, : DS - part]], 1), part
    )
    z_w = Weight(in_proj[:, DS - part : DS], part)
    oo_w, down_w = Weight(out_o, D), Weight(down_proj, D)
    gate_w, up_w = Weight(gate_up[:, :FF], FF), Weight(gate_up[:, FF:], FF)
    rows = gate_up.shape[0] // (lax.axis_size("ctx") // 2)
    rounds.start(
        gather_steps(idx, [qb_w, x_w, xz_w, z_w, oo_w, gate_w, up_w, down_w], rows, part // 2)
    )
    dt_task = rounds.start(ring_steps(dt_proj, layer))

    hidden = tokens[0].astype(jnp.float32)
    grad_out = cotangent[0].astype(jnp.float32)
    own_ids = doc_ids[0]
    length = hidden.shape[0]
    all_ids = along_ctx(own_ids.reshape(1, length), my_index).reshape(-1)
    first_row = my_index * length
    places = first_row + jnp.arange(length, dtype=jnp.int32)
    before = first_row - (KC - 1) + jnp.arange(KC - 1, dtype=jnp.int32)
    earlier_ids = lax.dynamic_slice_in_dim(all_ids, jnp.maximum(first_row - (KC - 1), 0), KC - 1, 0)
    earlier_ids = jnp.where(before >= 0, earlier_ids, -1)
    pad_ids = jnp.concatenate([earlier_ids, own_ids], 0)
    prev_id = jnp.where(my_index > 0, all_ids[jnp.maximum(first_row - 1, 0)], -1)
    normed_in, norm_pull = jax.vjp(normed, hidden, first_gain)
    input_low = normed_in.astype(jnp.bfloat16)
    input_low, all_ids, pad_ids, prev_id = rounds.turn((input_low, all_ids, pad_ids, prev_id))
    rounds.until_ready(qb_w)
    rounds.until(dt_task)

    qb_out = forth(idx, input_low, qb_w.ready)
    attn_in, bc_out = qb_out[:, :qkv_cols], qb_out[:, qkv_cols:]
    step_raw = project(input_low, dt_task.result)
    groups = HQ // HK
    scale = HA ** (-0.5)
    query_low = rotate(attn_in[:, : HQ * HA].reshape(length, HQ, HA), places, 1.0).astype(
        jnp.bfloat16
    )
    key_low = rotate(
        attn_in[:, HQ * HA : (HQ + HK) * HA].reshape(length, HK, HA), places, 1.0
    ).astype(jnp.bfloat16)
    value_low = attn_in[:, (HQ + HK) * HA :].astype(jnp.bfloat16)
    both_low = jnp.concatenate([key_low.reshape(length, HK * HA), value_low], 1)
    query_low, both_low, step_raw, bc_out = rounds.turn((query_low, both_low, step_raw, bc_out))
    both_task = rounds.start(along_ctx_steps(both_low, my_index))
    rounds.until_ready(x_w)
    x_out = forth(idx, input_low, x_w.ready)
    x_out = rounds.turn(x_out)
    rounds.until_ready(xz_w)
    xz_out = forth(idx, input_low, xz_w.ready)
    conv_low = jnp.concatenate([x_out, xz_out[:, : DS - part], bc_out], 1).astype(jnp.bfloat16)
    tail_low = from_behind(conv_low[length - (KC - 1) :], "ctx", 1)
    conv_low, tail_low, xz_out = rounds.turn((conv_low, tail_low, xz_out))

    def conv_fn(conv_in, tail_in, kernel_in, bias_in):
        padded = jnp.concatenate([tail_in, conv_in], 0)
        activated = jax.nn.silu(convolve(padded, pad_ids, own_ids, kernel_in, bias_in))
        states_x = activated[:, :DS].reshape(length, NH, HP)
        return (states_x, activated[:, DS : DS + NS], activated[:, DS + NS :])

    def step_fn(shift_in, bias_step, log_rate):
        step_size = jax.nn.softplus(shift_in + bias_step)
        return (step_size, -step_size * jnp.exp(log_rate))

    (states_x, b_matrix, c_matrix), conv_pull = jax.vjp(
        conv_fn, conv_low.astype(jnp.float32), tail_low.astype(jnp.float32), conv_weight, conv_bias
    )
    (step_size, log_decay), step_pull = jax.vjp(step_fn, step_raw, dt_bias, a_log)
    own_parts = (states_x, step_size, log_decay, b_matrix, c_matrix)
    y_part, y_pull = jax.vjp(lambda *parts: ssm_local(*parts, own_ids)[0], *own_parts)
    local_state, state_pull = jax.vjp(lambda *parts: ssm_local(*parts, own_ids)[1], *own_parts)
    decay_now, decay_pull = jax.vjp(lambda log_in: block_decay(log_in, own_ids, prev_id), log_decay)
    y_part, local_state, decay_now = rounds.turn((y_part, local_state, decay_now))
    state_task = rounds.start(entering_steps(decay_now, local_state, my_index, False))
    rounds.until(both_task)
    both_all = both_task.result
    query_groups = query_low.reshape(length, HK, groups, HA)
    seq_len = both_all.shape[0]
    keys_all = both_all[:, : HK * HA].reshape(seq_len, HK, HA)
    values_all = both_all[:, HK * HA :].reshape(seq_len, HK, HA)
    key_places = jnp.arange(seq_len, dtype=jnp.int32)
    allowed = (places[:, None] >= key_places[None, :]) & (own_ids[:, None] == all_ids[None, :])

    score = (
        jnp.einsum("qkgd,rkd->kgqr", query_groups, keys_all, preferred_element_type=jnp.float32)
        * scale
    )
    score = jnp.where(allowed[None, None], score, -1e30)
    new_top = jnp.maximum(-1e30, jnp.max(score, axis=-1))
    soft = jnp.where(allowed[None, None], jnp.exp(score - new_top[..., None]), 0.0)
    total = jnp.sum(soft, axis=-1)
    accum = jnp.einsum(
        "kgqr,rkd->qkgd",
        soft.astype(jnp.bfloat16),
        values_all,
        preferred_element_type=jnp.float32,
    )
    attended = accum / jnp.transpose(total, (2, 0, 1))[..., None]
    log_total = new_top + jnp.log(total)
    attended_low = attended.reshape(length, HQ * HA).astype(jnp.bfloat16)
    attended, log_total, attended_low = rounds.turn((attended, log_total, attended_low))

    rounds.until_ready(z_w)
    gate_z = jnp.concatenate(
        [xz_out[:, DS - part :], forth(idx, input_low, z_w.ready)], 1
    )
    gate_z, grad_low = rounds.turn((gate_z, grad_out.astype(jnp.bfloat16)))
    cotangent_all = every(grad_low, 0)
    rounds.until(state_task)
    rounds.until_ready(oo_w)
    state_in = state_task.result
    y_carry, carry_pull = jax.vjp(
        lambda c_in, log_in, state_arg: ssm_carry(c_in, log_in, own_ids, prev_id, state_arg),
        c_matrix,
        log_decay,
        state_in,
    )
    mixer_normed, tail_pull = jax.vjp(
        mixer_tail, y_part + y_carry, states_x, gate_z, d_skip, mixer_gain
    )
    mixer_low = mixer_normed.astype(jnp.bfloat16)

    def interleaved(mixed_in, attended_in):
        return jnp.concatenate(
            [
                mixed_in.reshape(length, layers, DS // layers),
                attended_in.reshape(length, layers, HQ * HA // layers),
            ],
            2,
        ).reshape(length, DS + HQ * HA)

    def parted(both):
        both = both.reshape(length, layers, (DS + HQ * HA) // layers)
        return (
            both[:, :, : DS // layers].reshape(length, DS),
            both[:, :, DS // layers :].reshape(length, HQ * HA),
        )

    branches_low = interleaved(mixer_low, attended_low)
    middle = hidden + forth(idx, branches_low, oo_w.ready)
    normed_mid, mid_pull = jax.vjp(normed, middle, second_gain)
    mid_low = normed_mid.astype(jnp.bfloat16)
    middle, mid_low, branches_low = rounds.turn((middle, mid_low, branches_low))
    early_deal = dealt(branches_low, input_low)
    rounds.until_ready(gate_w)
    gate_out = forth(idx, mid_low, gate_w.ready)
    gate_out = rounds.turn(gate_out)
    rounds.until_ready(up_w)
    up_out = forth(idx, mid_low, up_w.ready)
    act_value, act_pull = jax.vjp(
        lambda gate_in, up_in: jax.nn.silu(gate_in) * up_in, gate_out, up_out
    )
    act_low = act_value.astype(jnp.bfloat16)
    act_low = rounds.turn(act_low)

    rounds.until_ready(down_w)
    late_deal = dealt(act_low, mid_low)
    d_act = rounds.turn(back(idx, grad_low, down_w.ready))
    d_gate, d_up = act_pull(d_act)
    gate_low, up_low = d_gate.astype(jnp.bfloat16), d_up.astype(jnp.bfloat16)
    gate_low, up_low = rounds.turn((gate_low, up_low))
    gate_all, up_all = every(gate_low, 3), every(up_low, 5)
    shard_rows = mid_low.shape[1] // layers

    down_grad = weight_grad(
        [(late_deal, 0, cotangent_all)], lambda pair: pair
    )
    gate_up_grad = weight_grad(
        [(late_deal, 1, gate_all), (late_deal, 1, up_all)],
        lambda pair: pair,
        down_grad,
    )
    d_mid_norm = back(idx, gate_low, gate_w.ready)
    d_mid_norm = rounds.turn(d_mid_norm)
    d_mid_norm = d_mid_norm + back(idx, up_low, up_w.ready)
    d_middle_part, d_second_gain = mid_pull(d_mid_norm)
    d_middle = grad_out + d_middle_part
    branch_low = d_middle.astype(jnp.bfloat16)
    branch_low, d_middle = rounds.turn((branch_low, d_middle))
    branch_all = every(branch_low, 5)
    d_mixer_norm, d_attended = parted(back(idx, branch_low, oo_w.ready))
    d_mixer_norm, d_attended = rounds.turn((d_mixer_norm, d_attended))
    d_core, d_states_tail, d_gate_z, d_d_skip, d_mixer_gain = tail_pull(d_mixer_norm)
    z_low = d_gate_z.astype(jnp.bfloat16)
    z_low, d_core, d_states_tail = rounds.turn((z_low, d_core, d_states_tail))
    z_all = every(z_low, 6)
    fine = HQ * HA // layers
    cases = [
        (at % (shard_rows // fine), at // (shard_rows // fine) * D, (at // (shard_rows // fine) + 1) * D)
        for at in range((DS + HQ * HA) // layers // fine)
    ]
    oo_z_grad = weight_grad(
        [(early_deal, 0, branch_all), (early_deal, 1, z_all)],
        lambda pair: pair,
        gate_up_grad,
    )
    d_c_carry, d_log_carry, d_state_in = carry_pull(d_core)
    mixed = middle + forth(idx, act_low, down_w.ready)
    d_c_carry, d_log_carry, d_state_in, mixed = rounds.turn(
        (d_c_carry, d_log_carry, d_state_in, mixed)
    )
    later_task = rounds.start(entering_steps(decay_now, d_state_in, my_index, True))
    d_out_low = d_attended.reshape(length, HK, groups, HA).astype(jnp.bfloat16)
    delta = jnp.transpose(jnp.sum(d_out_low.astype(jnp.float32) * attended, axis=-1), (1, 2, 0))
    score = (
        jnp.einsum("qkgd,rkd->kgqr", query_groups, keys_all, preferred_element_type=jnp.float32)
        * scale
    )
    prob = jnp.where(
        allowed[None, None],
        jnp.exp(jnp.where(allowed[None, None], score, 0.0) - log_total[..., None]),
        0.0,
    )
    d_prob = jnp.einsum(
        "qkgd,rkd->kgqr", d_out_low, values_all, preferred_element_type=jnp.float32
    )
    score_grad = (prob * (d_prob - delta[..., None])).astype(jnp.bfloat16)
    d_query = (
        jnp.einsum("kgqr,rkd->qkgd", score_grad, keys_all, preferred_element_type=jnp.float32)
        * scale
    )
    d_keys = (
        jnp.einsum("kgqr,qkgd->rkd", score_grad, query_groups, preferred_element_type=jnp.float32)
        * scale
    )
    d_values = jnp.einsum(
        "kgqr,qkgd->rkd", prob.astype(jnp.bfloat16), d_out_low, preferred_element_type=jnp.float32
    )
    kv_terms = jnp.concatenate(
        [d_keys.reshape(seq_len, HK * HA), d_values.reshape(seq_len, HK * HA)], 1
    ).astype(jnp.bfloat16)
    kv_terms, d_query = rounds.turn((kv_terms, d_query))
    kv_task = rounds.start(sum_rows_steps(kv_terms, my_index))
    y_grads = rounds.turn(y_pull(d_core))
    rounds.until(later_task)
    later_grad = later_task.result
    state_grads = rounds.turn(state_pull(later_grad))
    d_decay = jnp.sum(later_grad * state_in, axis=(1, 2))
    d_log_decay = decay_pull(d_decay)[0]
    d_states, d_step, d_log, d_b, d_c = jax.tree.map(jnp.add, y_grads, state_grads)
    d_conv_in, d_tail, d_conv_weight, d_conv_bias = conv_pull(
        (d_states + d_states_tail, d_b, d_c + d_c_carry)
    )
    d_step_raw, d_dt_bias, d_a_log = step_pull((d_step, d_log + d_log_carry + d_log_decay))
    d_conv_in, d_tail, d_step_raw = rounds.turn((d_conv_in, d_tail, d_step_raw))
    rounds.until(kv_task)
    d_kv = kv_task.result.astype(jnp.float32)
    qkv_low = jnp.concatenate(
        [
            rotate(d_query.reshape(length, HQ, HA), places, -1.0).reshape(length, HQ * HA),
            rotate(d_kv[:, : HK * HA].reshape(length, HK, HA), places, -1.0).reshape(
                length, HK * HA
            ),
            d_kv[:, HK * HA :],
        ],
        1,
    ).astype(jnp.bfloat16)
    from_next = from_behind(d_tail.astype(jnp.bfloat16), "ctx", -1).astype(d_tail.dtype)
    d_conv_in = jnp.concatenate(
        [d_conv_in[: length - (KC - 1)], d_conv_in[length - (KC - 1) :] + from_next], 0
    )
    conv_grad_low = d_conv_in.astype(jnp.bfloat16)
    step_low = d_step_raw.astype(jnp.bfloat16)
    blank = jnp.zeros((length, 512 - NH), jnp.bfloat16)
    tail_low = jnp.concatenate([conv_grad_low, step_low, blank[:, : 256 - NH], qkv_low], 1)
    conv_grad_low, step_low, qkv_low, tail_low = rounds.turn(
        (conv_grad_low, step_low, qkv_low, tail_low)
    )
    tail_grad = weight_grad(
        [(early_deal, 1, every(tail_low, 4))], lambda pair: pair
    )
    main_done = Task(None)
    main_done.result = ()
    down_out = rounds.start(
        finish_steps(
            down_grad, 1, lambda pair: finished(idx, [pair], [(0, 0, D)]), main_done
        )
    )
    gate_up_out_grad = rounds.start(
        finish_steps(
            gate_up_grad, 2, lambda pair: finished(idx, [pair], [(0, 0, 2 * FF)]), main_done
        )
    )
    oo_out = rounds.start(
        finish_steps(
            oo_z_grad,
            0,
            lambda pair: (
                finished_rows(idx, pair, cases[: DS // layers // fine], fine),
                finished_rows(idx, pair, cases[DS // layers // fine :], fine),
            ),
            main_done,
        )
    )
    d_normed_in = (
        back(idx, conv_grad_low[:, :part], x_w.ready)
        + back(
            idx,
            jnp.concatenate([conv_grad_low[:, part:DS], z_low[:, : DS - part]], 1),
            xz_w.ready,
        )
    )
    d_normed_in = rounds.turn(d_normed_in)
    d_normed_in = (
        d_normed_in
        + back(idx, z_low[:, DS - part :], z_w.ready)
        + back(idx, jnp.concatenate([qkv_low, conv_grad_low[:, DS:]], 1), qb_w.ready)
        + project_back(step_low, dt_task.result)
    )
    d_hidden_part, d_first_gain = norm_pull(d_normed_in)
    d_tokens = d_middle + d_hidden_part
    d_tokens, d_first_gain = rounds.turn((d_tokens, d_first_gain))
    smalls_task = rounds.start(
        sum_steps(
            (
                d_conv_weight,
                d_conv_bias,
                d_dt_bias,
                d_a_log,
                d_d_skip,
                d_mixer_gain,
                d_first_gain,
                d_second_gain,
            )
        )
    )
    rounds.until(smalls_task, gate_up_out_grad, down_out, oo_out, tail_grad)
    smalls = smalls_task.result
    tail_pair, oo_z_pair = tail_grad.result, oo_z_grad.result
    out_grad, o_grad = oo_out.result
    z_first = branches_low.shape[1] // layers // shard_rows * D
    tail_half = tail_pair[0].shape[1]
    step_grad = jnp.where(core == 1, tail_pair[0], tail_pair[1])
    return (
        mixed[None].astype(jnp.bfloat16),
        d_tokens[None],
        finished(idx, [oo_z_pair, tail_pair], [(0, z_first, z_first + DS), (1, 0, conv_cols)]),
        step_grad[:, conv_cols - tail_half : conv_cols - tail_half + NH].astype(jnp.float32),
        smalls[0],
        smalls[1],
        smalls[2],
        smalls[3],
        smalls[4],
        smalls[5],
        out_grad,
        finished(idx, [tail_pair], [(0, conv_cols + 256, conv_cols + 256 + qkv_cols)]),
        o_grad,
        smalls[6],
        smalls[7],
        gate_up_out_grad.result,
        down_out.result,
    )


def solution(mesh):
    return jax.shard_map(
        body,
        mesh=mesh,
        in_specs=(
            P("fsdp", "ctx", None),
            P("fsdp", "ctx", None),
            P("fsdp", "ctx"),
            P("fsdp", None),
            P("fsdp", None),
            P(),
            P(),
            P(),
            P(),
            P(),
            P(),
            P("fsdp", None),
            P("fsdp", None),
            P("fsdp", None),
            P(),
            P(),
            P("fsdp", None),
            P("fsdp", None),
        ),
        out_specs=(
            P("fsdp", "ctx", None),
            P("fsdp", "ctx", None),
            P("fsdp", None),
            P("fsdp", None),
            P(),
            P(),
            P(),
            P(),
            P(),
            P(),
            P("fsdp", None),
            P("fsdp", None),
            P("fsdp", None),
            P(),
            P(),
            P("fsdp", None),
            P("fsdp", None),
        ),
        check_vma=False,
    )
```
